256 devices in a mesh: dp: 4 (over z_hi), field: 64 (over z_lo, y, x, core).
Axes of the slice: x: 4, y: 4, z: 8 (z_hi: 4, z_lo: 2; z = z_hi * 2 + z_lo), core: 2. Of those that a mesh axis runs over, the one named last changes fastest.
Arguments:
- inputs: bfloat16 [12, 512, 64, 1024], P('dp', 'field'), may hold values from -6 to 6
- cotangent: bfloat16 [12, 512, 64, 1024], P('dp', 'field'), may hold values from -6 to 6
- spec_weight: float32 [1024, 2, 64, 64], P('field'), may hold values from -0.75 to 0.75
- point_weight: bfloat16 [64, 64], replicated, may hold values from -0.75 to 0.75
Outputs:
- input_grad: bfloat16 [12, 512, 64, 1024], P('dp', 'field')
- spec_grad: float32 [1024, 2, 64, 64], P('field')
- point_grad: float32 [64, 64], replicated
The draws below stay inside these ranges and needn't reach their ends.
All inputs are finite; a program needn't handle non-finite values.
Results may differ from the reference program's by a relative error of at most 0.018.
Values may be sent and summed in bfloat16 or wider, within the bound.
No kernel may reach another device: no remote copies, remote signals or barrier semaphores. Data moves between devices by JAX's collectives and lax.ppermute only.
A program may use at most 64 MiB of HBM per device.

```python
import math
import jax
import jax.numpy as jnp
from jax import lax

DEPTH = 512
DURATION = 1024
CHANNELS = 64
DMODES = 32
TMODES = 32
BATCH = 12


def steps_of(own_key, extent, cuts, least, high):
    factor_of, own = 1.0, jax.random.fold_in(own_key, 6)
    for position, shards_of in cuts:
        draws = jnp.exp(jax.random.uniform(jax.random.fold_in(own, position), (shards_of,), jnp.float32, least / len(cuts), high / len(cuts)))
        factor_of = factor_of * jnp.repeat(draws, extent[position] // shards_of).reshape([-1 if axis == position else 1 for axis in range(len(extent))])
    return factor_of


def scatter_about(rng, shape, width, most, cuts=(), kind=jnp.bfloat16):
    factor_of = steps_of(rng, shape, cuts, -0.22, 0.18) if cuts else 1.0
    result = jax.random.normal(rng, shape, jnp.float32) * width * factor_of
    return jnp.minimum(jnp.maximum(result, -most), most).astype(kind)


def setup_inputs(seed: int = 0) -> dict:
    key_of = jax.random.split(jax.random.key(seed), 5)
    inputs = scatter_about(key_of[0], (BATCH, DEPTH, CHANNELS, DURATION), 1.0, 6.0, ((0, 4), (1, 64)))
    cotangent = scatter_about(key_of[1], (BATCH, DEPTH, CHANNELS, DURATION), 1.0, 6.0, ((0, 4), (1, 64)))
    spec_weight = scatter_about(key_of[2], (DMODES * TMODES, 2, CHANNELS, CHANNELS), CHANNELS ** -0.5, 0.75, ((0, 64),), jnp.float32)
    point_weight = scatter_about(key_of[3], (CHANNELS, CHANNELS), CHANNELS ** -0.5, 0.75)
    return dict(inputs=inputs, cotangent=cotangent, spec_weight=spec_weight, point_weight=point_weight)


def time_table(count_t, modes):
    times = jnp.arange(count_t, dtype=jnp.int32)
    orders = jnp.arange(modes, dtype=jnp.int32)
    phase = jnp.mod(times[:, None] * orders[None, :], count_t).astype(jnp.float32) * (2.0 * math.pi / count_t)
    return jnp.concatenate([jnp.cos(phase), -jnp.sin(phase)], axis=1).astype(jnp.bfloat16)

def depth_table(positions, count_x, modes):
    orders = jnp.arange(modes, dtype=jnp.int32)
    freqs = jnp.where(orders < modes // 2, orders, orders - modes)
    phase = jnp.mod(freqs[:, None] * positions[None, :], count_x).astype(jnp.float32) * (2.0 * math.pi / count_x)
    return (jnp.cos(phase), jnp.sin(phase))

def precise(form, left, right):
    return jnp.einsum(form, left, right, precision=lax.Precision.HIGHEST)

def forward_depth(rows, cosines, sine_vals, modes):
    real_part = rows[..., :modes]
    imag_part = rows[..., modes:]
    spec_real = precise('kx,bxcm->kmbc', cosines, real_part) + precise('kx,bxcm->kmbc', sine_vals, imag_part)
    spec_imag = precise('kx,bxcm->kmbc', cosines, imag_part) - precise('kx,bxcm->kmbc', sine_vals, real_part)
    stacked = jnp.stack([spec_real, spec_imag], axis=2)
    return stacked.reshape(cosines.shape[0] * modes, 2, rows.shape[0], rows.shape[2])

def inverse_depth(spectrum, cosines, sine_vals, modes):
    shaped = spectrum.reshape(cosines.shape[0], modes, 2, spectrum.shape[2], spectrum.shape[3])
    spec_real = shaped[:, :, 0]
    spec_imag = shaped[:, :, 1]
    row_real = precise('kx,kmbc->bxcm', cosines, spec_real) - precise('kx,kmbc->bxcm', sine_vals, spec_imag)
    row_imag = precise('kx,kmbc->bxcm', sine_vals, spec_real) + precise('kx,kmbc->bxcm', cosines, spec_imag)
    return jnp.concatenate([row_real, row_imag], axis=3)

def mix(spectrum, weights):
    s_real, s_imag = (spectrum[:, 0], spectrum[:, 1])
    w_real, w_imag = (weights[:, 0], weights[:, 1])
    out_real = precise('pbc,pco->pbo', s_real, w_real) - precise('pbc,pco->pbo', s_imag, w_imag)
    out_imag = precise('pbc,pco->pbo', s_real, w_imag) + precise('pbc,pco->pbo', s_imag, w_real)
    return jnp.stack([out_real, out_imag], axis=1)

def mix_adjoint(dspec, weights):
    d_real, d_imag = (dspec[:, 0], dspec[:, 1])
    w_real, w_imag = (weights[:, 0], weights[:, 1])
    out_real = precise('pbo,pco->pbc', d_real, w_real) + precise('pbo,pco->pbc', d_imag, w_imag)
    out_imag = precise('pbo,pco->pbc', d_imag, w_real) - precise('pbo,pco->pbc', d_real, w_imag)
    return jnp.stack([out_real, out_imag], axis=1)

def weight_term(spectrum, dspec):
    s_real, s_imag = (spectrum[:, 0], spectrum[:, 1])
    d_real, d_imag = (dspec[:, 0], dspec[:, 1])
    g_real = precise('pbc,pbo->pco', s_real, d_real) + precise('pbc,pbo->pco', s_imag, d_imag)
    g_imag = precise('pbc,pbo->pco', s_real, d_imag) - precise('pbc,pbo->pco', s_imag, d_real)
    return jnp.stack([g_real, g_imag], axis=1)

def reference(inputs, cotangent, spec_weight, point_weight):
    table = time_table(DURATION, TMODES).astype(jnp.float32)
    scale = 1.0 / math.sqrt(DEPTH * DURATION)
    inv_scale = 1.0 / math.sqrt(DMODES * TMODES)
    cosines, sine_vals = depth_table(jnp.arange(DEPTH, dtype=jnp.int32), DEPTH, DMODES)
    mixing = point_weight.astype(jnp.float32)

    def one_sample(carry, pair):
        spec_sum, point_sum = carry
        field_in = pair[0][None].astype(jnp.float32)
        upstream = pair[1][None].astype(jnp.float32)
        coeffs = precise('bxct,tj->bxcj', field_in, table) * scale
        spectrum = forward_depth(coeffs, cosines, sine_vals, TMODES)
        mixed = mix(spectrum, spec_weight)
        spec_rows = inverse_depth(mixed, cosines, sine_vals, TMODES).astype(jnp.bfloat16).astype(jnp.float32)
        spatial = precise('bxcj,tj->bxct', spec_rows, table) * inv_scale
        pre = spatial + precise('bxct,co->bxot', field_in, mixing)
        slope = jax.vjp(jax.nn.gelu, pre)[1](upstream)[0]
        dpre = slope.astype(jnp.bfloat16).astype(jnp.float32)
        point_sum = point_sum + precise('bxct,bxot->co', field_in, dpre)
        drows = precise('bxot,tj->bxoj', dpre, table) * inv_scale
        dmixed = forward_depth(drows, cosines, sine_vals, TMODES)
        spec_sum = spec_sum + weight_term(spectrum, dmixed)
        dspec = mix_adjoint(dmixed, spec_weight)
        dcoeffs = inverse_depth(dspec, cosines, sine_vals, TMODES).astype(jnp.bfloat16).astype(jnp.float32)
        grad_in = precise('bxcj,tj->bxct', dcoeffs, table) * scale + precise('bxot,co->bxct', dpre, mixing)
        return ((spec_sum, point_sum), grad_in[0].astype(jnp.bfloat16))
    start = (jnp.zeros(spec_weight.shape, jnp.float32), jnp.zeros((CHANNELS, CHANNELS), jnp.float32))
    (spec_sum, point_sum), input_grad = lax.scan(one_sample, start, (inputs, cotangent))
    spec_grad = spec_sum / math.sqrt(BATCH * DEPTH)
    point_grad = point_sum / math.sqrt(BATCH * DEPTH * DURATION)
    return (input_grad, spec_grad, point_grad)
```

```python
import math

import jax
import jax.numpy as jnp
import ml_dtypes
import numpy as np
from jax import lax
from jax.experimental import pallas as pl
from jax.experimental.pallas import tpu as pltpu
from jax.sharding import Mesh
from jax.sharding import PartitionSpec as P

DEPTH = 512
DURATION = 1024
CHANNELS = 64
DMODES = 32
TMODES = 32
BATCH = 12

FIELD = ("z", "y", "x", "core")
BF16 = jnp.bfloat16
F32 = jnp.float32
SCALE = 1.0 / math.sqrt(DEPTH * DURATION)
INV_SCALE = 1.0 / math.sqrt(DMODES * TMODES)
NT = (((1,), (1,)), ((), ()))
TN = (((0,), (0,)), ((), ()))
VMEM_LIMIT = 48 * 1024 * 1024


def time_rows():
    q = np.arange(TMODES)
    m = (q % 2) * 16 + q // 2
    phase = ((m[:, None] * np.arange(DURATION)[None, :]) % DURATION) * (2.0 * np.pi / DURATION)
    return np.concatenate([np.cos(phase), -np.sin(phase)], axis=0).astype(ml_dtypes.bfloat16)


def depth_rows():
    orders = np.arange(DMODES)
    freqs = np.where(orders < DMODES // 2, orders, orders - DMODES)
    phase = ((freqs[:, None] * np.arange(DEPTH)[None, :]) % DEPTH) * (2.0 * np.pi / DEPTH)
    halves = []
    for half in range(2):
        part = phase[half * 16 : half * 16 + 16]
        both = np.concatenate([np.cos(part), np.sin(part)], axis=0)
        high = both.astype(ml_dtypes.bfloat16)
        low = (both - high.astype(np.float64)).astype(ml_dtypes.bfloat16)
        halves.append(np.concatenate([high, low], axis=0))
    return np.stack(halves)


def lanes(shape):
    return lax.broadcasted_iota(jnp.int32, shape, len(shape) - 1)


def swap(v):
    return pltpu.roll(v, 64, 1)


def turn(v, first):
    return swap(v) * jnp.where(lanes(v.shape) < 64, first, -first).astype(F32)


def dot(a, b, dims=(((1,), (0,)), ((), ()))):
    return lax.dot_general(a, b, dims, preferred_element_type=F32)


def emit_rows(r, scratch, store):
    for xl in range(8):
        cols = slice(xl * 64, xl * 64 + 64)
        block = jnp.concatenate([r[:32, cols], r[32:, cols]], axis=1)
        scratch[pl.ds(xl, 32, stride=8), :] = block
    store(scratch[...].reshape(32, 8, 128).astype(BF16))


def load_rows(recv, scratch):
    both = recv[:32, 0].astype(F32) + recv[32:, 0].astype(F32)
    scratch[...] = both.reshape(256, 128)


def mode_block(scratch, xl):
    g = scratch[pl.ds(xl, 32, stride=8), :]
    return jnp.concatenate([g[:, :64], g[:, 64:]], axis=0)


def weight_kernel(w_ref, o_ref):
    o_ref[...] = jnp.concatenate([w_ref[:, 0], w_ref[:, 1]], axis=2).astype(BF16)


def coeff_kernel(in_ref, tab_ref, o_ref, scratch):
    r = dot(tab_ref[...], in_ref[0].reshape(512, DURATION), NT) * SCALE

    def store(v):
        o_ref[:32, 0] = v
        o_ref[32:, 0] = v

    emit_rows(r, scratch, store)


def to_modes(recv, table):
    out = []
    for b in range(3):
        rows = recv[:, b].astype(F32).reshape(DEPTH, 128).astype(BF16)
        both = dot(table, rows)
        both = both[:32] + both[32:]
        out.append(both[:16] + turn(both[16:], 1.0))
    return jnp.concatenate(out, axis=0)


def from_modes(modes, table, factor, o_ref):
    turned = turn(modes, -1.0)
    for b in range(3):
        rows = slice(b * 16, b * 16 + 16)
        pair = jnp.concatenate([modes[rows], turned[rows]], axis=0)
        pair = jnp.concatenate([pair, pair], axis=0).astype(BF16)
        back = dot(table, pair, TN)
        if factor != 1.0:
            back = back * factor
        o_ref[:, b] = back.reshape(64, 8, 128).astype(BF16)


def own_pair(kp):
    row = lax.broadcasted_iota(jnp.int32, (48, 128), 0) % 16
    return row == 2 * kp + lanes((48, 128)) // 64


def mix_kernel(recv_ref, tab_ref, w_ref, o_ref, spec_ref):
    table = tab_ref[lax.axis_index("z")]
    spec = to_modes(recv_ref, table)
    spec_ref[...] = spec
    low = lanes((48, 128)) < 64
    other = swap(spec)
    real = jnp.where(low, spec, other)
    imag = jnp.where(low, other, spec)
    cols = []
    for kp in range(8):
        own = own_pair(kp)
        cols.append(
            jnp.concatenate([jnp.where(own, real, 0.0), jnp.where(own, imag, 0.0)], axis=0).astype(BF16)
        )
    prod = dot(jnp.concatenate(cols, axis=1), w_ref[...].reshape(1024, 128))
    mixed = prod[:48] + turn(prod[48:], -1.0)
    from_modes(mixed, table, 1.0, o_ref)


def adjoint_kernel(recv_ref, tab_ref, w_ref, spec_ref, o_ref, fact_ref, scratch):
    table = tab_ref[lax.axis_index("z")]
    dmix = to_modes(recv_ref, table)
    both = jnp.concatenate([dmix, turn(dmix, 1.0)], axis=0).astype(BF16)
    prod = dot(both, w_ref[...].reshape(1024, 128), NT)
    real = jnp.zeros((48, 128), F32)
    imag = jnp.zeros((48, 128), F32)
    for kp in range(8):
        own = own_pair(kp)
        cols = slice(kp * 128, kp * 128 + 128)
        real = real + jnp.where(own, prod[:48, cols], 0.0)
        imag = imag + jnp.where(own, prod[48:, cols], 0.0)
    real = real + swap(real)
    imag = imag + swap(imag)
    dspec = jnp.where(lanes((48, 128)) < 64, real, imag)
    from_modes(dspec, table, SCALE, o_ref)
    scratch[...] = jnp.zeros_like(scratch)
    for b in range(3):
        scratch[pl.ds(b, 16, stride=16), :] = spec_ref[b * 16 : b * 16 + 16, :]
        scratch[pl.ds(8 + b, 16, stride=16), :] = dmix[b * 16 : b * 16 + 16]
    point = jnp.sum(recv_ref[:, 3].astype(F32), axis=0)
    point = split_pair(point + swap(point))[:4]
    for k in range(16):
        scratch[k * 16 + 12 : k * 16 + 16, :] = point
    fact = scratch[...].reshape(16, 16, 128).astype(BF16)
    for dp in range(4):
        fact_ref[dp * 16 : dp * 16 + 16] = fact


def split_pair(v):
    high = v.astype(BF16).astype(F32)
    return jnp.where(lanes(v.shape) < 64, high, v - high)


def field_kernel(in_ref, cot_ref, recv_ref, tab_ref, w_ref, dpre_ref, o_ref, rows, scratch, point):
    b = pl.program_id(0)

    @pl.when(b == 0)
    def _():
        point[...] = jnp.zeros_like(point)

    load_rows(recv_ref, rows)
    mix_t = w_ref[...].astype(F32).T.astype(BF16)
    root = math.sqrt(2.0 / math.pi)
    for xl in range(8):
        g = (mode_block(rows, xl).T * INV_SCALE).astype(BF16)
        for chunk in range(4):
            ts = slice(chunk * 256, chunk * 256 + 256)
            pre = dot(g, tab_ref[:, ts]) + dot(mix_t, in_ref[0, xl, :, ts])
            sq = pre * pre
            th = jnp.tanh(pre * (root + (root * 0.044715) * sq))
            slope = 0.5 + 0.5 * th + (0.5 * pre) * (1.0 - th * th) * (
                root + (3.0 * root * 0.044715) * sq
            )
            dpre_ref[0, xl, :, ts] = (slope * cot_ref[0, xl, :, ts].astype(F32)).astype(BF16)
        point[...] += dot(in_ref[0, xl], dpre_ref[0, xl], NT)
    r = dot(tab_ref[...], dpre_ref[0].reshape(512, DURATION), NT) * INV_SCALE

    def store(v):
        o_ref[:32, b] = v
        o_ref[32:, b] = v

    emit_rows(r, scratch, store)

    @pl.when(b == 2)
    def _():
        total = point[...]
        pair = split_pair(jnp.concatenate([total, total], axis=1))
        for q in range(32):
            piece = pair[(q // 2) * 4 : (q // 2) * 4 + 4]
            piece = jnp.concatenate([piece, jnp.zeros_like(piece)], axis=0).astype(BF16)
            o_ref[q, 3] = piece
            o_ref[32 + q, 3] = piece


def grad_kernel(dpre_ref, recv_ref, tab_ref, w_ref, o_ref, rows):
    load_rows(recv_ref, rows)
    mixing = w_ref[...]
    for xl in range(8):
        g = mode_block(rows, xl).T.astype(BF16)
        for chunk in range(4):
            ts = slice(chunk * 256, chunk * 256 + 256)
            total = dot(g, tab_ref[:, ts]) + dot(mixing, dpre_ref[0, xl, :, ts])
            o_ref[0, xl, :, ts] = total.astype(BF16)


def weight_grad_kernel(fact_ref, spec_ref, point_ref, scratch):
    for m in range(16):
        parts = [fact_ref[dp * 16 + m].astype(F32) for dp in range(4)]
        s = jnp.concatenate([p[:8] for p in parts], axis=0)
        d = jnp.concatenate([p[8:] for p in parts], axis=0)
        left = jnp.concatenate([s[:, :64], s[:, 64:]], axis=0).astype(BF16)
        right = jnp.concatenate([d, turn(d, 1.0)], axis=0).astype(BF16)
        g = dot(left, right, TN) * (1.0 / math.sqrt(BATCH * DEPTH))
        spec_ref[m, 0] = g[:, :64]
        spec_ref[m, 1] = g[:, 64:]
        total = d[4:8] + d[12:16] + d[20:24] + d[28:32]
        scratch[m * 4 : m * 4 + 4, :] = total
    point = scratch[...]
    point = (point + swap(point)) * (1.0 / math.sqrt(BATCH * DEPTH * DURATION))
    point_ref[...] = point[:, :64]


def whole(shape):
    return pl.BlockSpec(shape, lambda *_: (0,) * len(shape))


def call(kernel, out_shape, grid, in_specs, out_specs, scratch=()):
    return pl.pallas_call(
        kernel,
        out_shape=out_shape,
        grid=grid,
        in_specs=in_specs,
        out_specs=out_specs,
        scratch_shapes=list(scratch),
        compiler_params=pltpu.CompilerParams(vmem_limit_bytes=VMEM_LIMIT),
    )


def shape(*dims, dtype=BF16):
    return jax.ShapeDtypeStruct(dims, dtype)


def exchange(v, axes):
    return lax.all_to_all(v, axes, 0, 0, tiled=True)


def local(inputs, cotangent, spec_weight, point_weight):
    tab = jnp.asarray(time_rows())
    depth = jnp.asarray(depth_rows())
    field_block = pl.BlockSpec((1, 8, 64, DURATION), lambda b: (b, 0, 0, 0))
    recv_block = pl.BlockSpec((64, 1, 8, 128), lambda b: (0, b, 0, 0))
    tab_block = whole((64, DURATION))
    mix_block = whole((64, 64))
    message = (64, 3, 8, 128)

    w_send = call(
        weight_kernel, shape(16, 64, 128), (1,), [whole((16, 2, 64, 64))], whole((16, 64, 128))
    )(spec_weight)
    weights = exchange(w_send, ("y", "x"))
    coeffs = call(
        coeff_kernel,
        shape(*message),
        (3,),
        [field_block, tab_block],
        recv_block,
        [pltpu.VMEM((256, 128), F32)],
    )(inputs, tab)
    got = exchange(coeffs, FIELD)
    rows, spectrum = call(
        mix_kernel,
        (shape(*message), shape(48, 128, dtype=F32)),
        (1,),
        [whole(message), whole((2, 64, DEPTH)), whole((16, 64, 128))],
        (whole(message), whole((48, 128))),
    )(got, depth, weights)
    got = exchange(rows, FIELD)
    dpre, drows = call(
        field_kernel,
        (shape(3, 8, 64, DURATION), shape(64, 4, 8, 128)),
        (3,),
        [field_block, field_block, recv_block, tab_block, mix_block],
        (field_block, whole((64, 4, 8, 128))),
        [pltpu.VMEM((256, 128), F32), pltpu.VMEM((256, 128), F32), pltpu.VMEM((64, 64), F32)],
    )(inputs, cotangent, got, tab, point_weight)
    got = exchange(drows, FIELD)
    drows, factors = call(
        adjoint_kernel,
        (shape(*message), shape(64, 16, 128)),
        (1,),
        [whole((64, 4, 8, 128)), whole((2, 64, DEPTH)), whole((16, 64, 128)), whole((48, 128))],
        (whole(message), whole((64, 16, 128))),
        [pltpu.VMEM((256, 128), F32)],
    )(got, depth, weights, spectrum)
    got = exchange(drows, FIELD)
    factors = exchange(factors, ("dp", "y", "x"))
    input_grad = call(
        grad_kernel,
        shape(3, 8, 64, DURATION),
        (3,),
        [field_block, recv_block, tab_block, mix_block],
        field_block,
        [pltpu.VMEM((256, 128), F32)],
    )(dpre, got, tab, point_weight)
    spec_grad, point_grad = call(
        weight_grad_kernel,
        (shape(16, 2, 64, 64, dtype=F32), shape(64, 64, dtype=F32)),
        (1,),
        [whole((64, 16, 128))],
        (whole((16, 2, 64, 64)), whole((64, 64))),
        [pltpu.VMEM((64, 128), F32)],
    )(factors)
    return (input_grad, spec_grad, point_grad)


def solution(mesh):
    fine = Mesh(mesh.devices.reshape(4, 2, 4, 4, 2), ("dp",) + FIELD)
    fields = P("dp", FIELD, None, None)
    weights = P(FIELD, None, None, None)
    return jax.shard_map(
        local,
        mesh=fine,
        in_specs=(fields, fields, weights, P()),
        out_specs=(fields, weights, P()),
        check_vma=False,
    )
```

```python
import math

import jax
import jax.numpy as jnp
import ml_dtypes
import numpy as np
from jax import lax
from jax.experimental import pallas as pl
from jax.experimental.pallas import tpu as pltpu
from jax.sharding import Mesh
from jax.sharding import PartitionSpec as P

DEPTH = 512
DURATION = 1024
CHANNELS = 64
DMODES = 32
TMODES = 32
BATCH = 12

CHIP = ("z", "y", "x")
FIELD = CHIP + ("core",)
BF16 = jnp.bfloat16
F32 = jnp.float32
SCALE = 1.0 / math.sqrt(DEPTH * DURATION)
INV_SCALE = 1.0 / math.sqrt(DMODES * TMODES)
NN = (((1,), (0,)), ((), ()))
NT = (((1,), (1,)), ((), ()))
VMEM_LIMIT = 48 * 1024 * 1024
PAIRS = 48
ROWS = 56


def time_rows():
    out = []
    for core in range(2):
        m = np.concatenate([core * 16 + np.arange(16), (1 - core) * 16 + np.arange(16)])
        phase = ((m[:, None] * np.arange(DURATION)[None, :]) % DURATION) * (2.0 * np.pi / DURATION)
        out.append(np.concatenate([np.cos(phase), -np.sin(phase)], axis=0))
    return np.stack(out).astype(ml_dtypes.bfloat16)


def depth_rows():
    orders = np.arange(DMODES)
    freqs = np.where(orders < DMODES // 2, orders, orders - DMODES)
    forward, inverse = [], []
    for f in range(64):
        x = np.concatenate([f * 8 + np.arange(8), (f ^ 1) * 8 + np.arange(8)])
        phase = ((freqs[:, None] * x[None, :]) % DEPTH) * (2.0 * np.pi / DEPTH)
        both = np.concatenate([np.cos(phase), np.sin(phase)], axis=0)
        high = both.astype(ml_dtypes.bfloat16)
        low = (both - high.astype(np.float64)).astype(ml_dtypes.bfloat16)
        forward.append(np.concatenate([high, low], axis=1))
        inverse.append(np.concatenate([high, low], axis=0).T)
    return np.stack(forward), np.stack(inverse)


def lanes(shape):
    return lax.broadcasted_iota(jnp.int32, shape, len(shape) - 1)


def swap(v):
    return pltpu.roll(v, 64, 1)


def turn(v, first):
    return swap(v) * jnp.where(lanes(v.shape) < 64, first, -first).astype(F32)


def split_pair(v):
    high = v.astype(BF16).astype(F32)
    return jnp.where(lanes(v.shape) < 64, high, v - high)


def dot(a, b, dims=NN):
    return lax.dot_general(a, b, dims, preferred_element_type=F32)


def emit_rows(r, scratch):
    for xl in range(8):
        cols = slice(xl * 64, xl * 64 + 64)
        block = jnp.concatenate([r[:32, cols], r[32:, cols]], axis=1)
        scratch[pl.ds(xl, 32, stride=8), :] = block
    return scratch[...].reshape(32, 8, 128).astype(BF16)


def load_rows(own_ref, other_ref, scratch):
    scratch[:128] = own_ref[:, 0].astype(F32).reshape(128, 128)
    scratch[128:] = other_ref[:, 0].astype(F32).reshape(128, 128)


def mode_block(scratch, xl):
    g = scratch[pl.ds(xl, 32, stride=8), :]
    return jnp.concatenate([g[:, :64], g[:, 64:]], axis=0)


def own_pair(kp, rows):
    row = lax.broadcasted_iota(jnp.int32, (rows, 128), 0)
    first = row - lanes((rows, 128)) // 64 * 3 - 6 * kp
    return (first >= 0) & (first < 3)


def weight_kernel(w_ref, o_ref):
    o_ref[...] = jnp.concatenate([w_ref[:, 0], w_ref[:, 1]], axis=2).astype(BF16)


def coeff_kernel(in_ref, tab_ref, own_ref, send_ref, scratch):
    table = tab_ref[lax.axis_index("core")]
    rows = emit_rows(dot(table, in_ref[0].reshape(512, DURATION), NT) * SCALE, scratch)
    own_ref[:, 0] = rows[:16]
    send_ref[:, 0] = rows[16:]


def spread_kernel(f_ref, own_ref, other_ref, tab_ref, o_ref, scratch, *point, rows):
    del f_ref
    table = tab_ref[0]
    both = jnp.concatenate([own_ref[:, :3].astype(F32), other_ref[:, :3].astype(F32)], axis=2).astype(BF16)
    both = both.reshape(PAIRS, 16, 128)
    for group in range(4):
        data = jnp.concatenate([both[group * 12 + i] for i in range(12)], axis=1)
        modes = dot(table, jnp.concatenate([data, data], axis=0))
        for i in range(12):
            cols = slice(i * 128, i * 128 + 128)
            part = modes[:32, cols] + turn(modes[32:, cols], 1.0)
            scratch[pl.ds(group * 12 + i, 32, stride=rows), :] = part
    if point:
        (pairs,) = point
        total = own_ref[:8, 3].astype(F32).reshape(64, 128) + other_ref[:8, 3].astype(F32).reshape(64, 128)
        pairs[...] = split_pair(total + swap(total))
        for i in range(2):
            scratch[pl.ds(PAIRS + i, 32, stride=rows), :] = pairs[pl.ds(i, 32, stride=2), :]
        for i in range(2, 8):
            scratch[pl.ds(PAIRS + i, 32, stride=rows), :] = jnp.zeros((32, 128), F32)
    o_ref[...] = scratch[...].reshape(32, rows, 128).astype(BF16)


def mix_kernel(recv_ref, w_ref, o_ref, spec_ref):
    spec = jnp.sum(recv_ref[...].astype(F32), axis=0)
    spec_ref[...] = spec
    low = lanes(spec.shape) < 64
    other = swap(spec)
    real = jnp.where(low, spec, other)
    imag = jnp.where(low, other, spec)
    cols = []
    for kp in range(8):
        own = own_pair(kp, PAIRS)
        cols.append(
            jnp.concatenate([jnp.where(own, real, 0.0), jnp.where(own, imag, 0.0)], axis=0).astype(BF16)
        )
    prod = dot(jnp.concatenate(cols, axis=1), w_ref[...].reshape(1024, 128))
    mixed = (prod[:PAIRS] + turn(prod[PAIRS:], -1.0)).astype(BF16)
    o_ref[...] = jnp.broadcast_to(mixed[None], (32, PAIRS, 128))


def adjoint_kernel(recv_ref, w_ref, o_ref, dmix_ref):
    total = jnp.sum(recv_ref[...].astype(F32), axis=0)
    dmix = total[:PAIRS]
    dmix_ref[...] = dmix
    both = jnp.concatenate([dmix, turn(dmix, 1.0)], axis=0).astype(BF16)
    prod = dot(both, w_ref[...].reshape(1024, 128), NT)
    real = jnp.zeros((PAIRS, 128), F32)
    imag = jnp.zeros((PAIRS, 128), F32)
    for kp in range(8):
        own = own_pair(kp, PAIRS)
        cols = slice(kp * 128, kp * 128 + 128)
        real = real + jnp.where(own, prod[:PAIRS, cols], 0.0)
        imag = imag + jnp.where(own, prod[PAIRS:, cols], 0.0)
    real = real + swap(real)
    imag = imag + swap(imag)
    dspec = jnp.where(lanes(real.shape) < 64, real, imag) * SCALE
    point = total[PAIRS:]
    point = split_pair(point + swap(point))
    message = jnp.concatenate([dspec, point], axis=0).astype(BF16)
    o_ref[...] = jnp.broadcast_to(message[None], (32, ROWS, 128))


def gather_kernel(f_ref, recv_ref, tab_ref, *rest, rows):
    del f_ref
    if rows == ROWS:
        spec_ref, dmix_ref, own_ref, send_ref, fact_ref, scratch, fact = rest
    else:
        own_ref, send_ref, scratch = rest
    table = tab_ref[0]
    scratch[...] = recv_ref[...].astype(F32).reshape(32 * rows, 128)
    for group in range(4):
        cols = []
        for i in range(12):
            modes = scratch[pl.ds(group * 12 + i, 32, stride=rows), :]
            pair = jnp.concatenate([modes, turn(modes, -1.0)], axis=0)
            cols.append(jnp.concatenate([pair, pair], axis=0).astype(BF16))
        back = dot(table, jnp.concatenate(cols, axis=1))
        for i in range(12):
            m, b = divmod(group * 12 + i, 3)
            part = back[:, i * 128 : i * 128 + 128].astype(BF16)
            own_ref[m, b] = part[:8]
            send_ref[m, b] = part[8:]
    if rows == ROWS:
        fact[...] = jnp.zeros_like(fact)
        fact[:PAIRS] = spec_ref[...]
        fact[64 : 64 + PAIRS] = dmix_ref[...]
        for i in range(2):
            fact[pl.ds(128 + i, 32, stride=2), :] = scratch[pl.ds(PAIRS + i, 32, stride=rows), :]
        whole_fact = fact[...].astype(BF16)
        fact_ref[...] = jnp.broadcast_to(whole_fact[None], (4, 192, 128))


def field_kernel(
    in_ref, cot_ref, got_ref, other_ref, tab_ref, w_ref, dpre_ref, own_ref, send_ref, rows, scratch, point
):
    b = pl.program_id(0)

    @pl.when(b == 0)
    def _():
        point[...] = jnp.zeros_like(point)

    load_rows(got_ref, other_ref, rows)
    table = tab_ref.at[lax.axis_index("core")]
    mix_t = w_ref[...].astype(F32).T.astype(BF16)
    root = math.sqrt(2.0 / math.pi)
    for xl in range(8):
        g = (mode_block(rows, xl).T * INV_SCALE).astype(BF16)
        for chunk in range(4):
            ts = slice(chunk * 256, chunk * 256 + 256)
            pre = dot(g, table[:, ts]) + dot(mix_t, in_ref[0, xl, :, ts])
            sq = pre * pre
            th = jnp.tanh(pre * (root + (root * 0.044715) * sq))
            slope = 0.5 + 0.5 * th + (0.5 * pre) * (1.0 - th * th) * (
                root + (3.0 * root * 0.044715) * sq
            )
            dpre_ref[0, xl, :, ts] = (slope * cot_ref[0, xl, :, ts].astype(F32)).astype(BF16)
        point[...] += dot(in_ref[0, xl], dpre_ref[0, xl], NT)
    r = dot(table[...], dpre_ref[0].reshape(512, DURATION), NT) * INV_SCALE
    out = emit_rows(r, scratch)
    own_ref[:, b] = out[:16]
    send_ref[:, b] = out[16:]

    @pl.when(b == 2)
    def _():
        total = point[...]
        pair = split_pair(jnp.concatenate([total, total], axis=1))
        pair = jnp.concatenate([pair, jnp.zeros_like(pair)], axis=0).reshape(16, 8, 128).astype(BF16)
        own_ref[:, 3] = pair
        send_ref[:, 3] = pair


def grad_kernel(dpre_ref, got_ref, other_ref, tab_ref, w_ref, o_ref, rows):
    load_rows(got_ref, other_ref, rows)
    table = tab_ref.at[lax.axis_index("core")]
    mixing = w_ref[...]
    for xl in range(8):
        g = mode_block(rows, xl).T.astype(BF16)
        for chunk in range(4):
            ts = slice(chunk * 256, chunk * 256 + 256)
            total = dot(g, table[:, ts]) + dot(mixing, dpre_ref[0, xl, :, ts])
            o_ref[0, xl, :, ts] = total.astype(BF16)


def weight_grad_kernel(fact_ref, spec_ref, point_ref):
    fact = fact_ref[...].astype(F32)
    turned = fact[:, :64].reshape(256, 128).T
    real = turned[:64]
    imag = turned[64:]
    left = jnp.concatenate([real, imag], axis=1)
    row = lanes((64, 512)) % 64
    d = fact[:, 64:128].reshape(256, 128)
    right = jnp.concatenate([d, turn(d, 1.0)], axis=0).astype(BF16)
    parts = [
        jnp.where((row >= 3 * m) & (row < 3 * m + 3), left, 0.0).astype(BF16) for m in range(16)
    ]
    g = dot(jnp.concatenate(parts, axis=0), right) * (1.0 / math.sqrt(BATCH * DEPTH))
    g = g.reshape(16, 64, 128)
    spec_ref[:, 0] = g[:, :, :64]
    spec_ref[:, 1] = g[:, :, 64:]
    point = fact[0, 128:] + fact[1, 128:] + fact[2, 128:] + fact[3, 128:]
    point = (point + swap(point)) * (1.0 / math.sqrt(BATCH * DEPTH * DURATION))
    point_ref[...] = point[:, :64]


def whole(shape):
    return pl.BlockSpec(shape, lambda *_: (0,) * len(shape))


def call(kernel, out_shape, grid, in_specs, out_specs, scratch=(), prefetch=0):
    return pl.pallas_call(
        kernel,
        out_shape=out_shape,
        grid_spec=pltpu.PrefetchScalarGridSpec(
            num_scalar_prefetch=prefetch,
            grid=grid,
            in_specs=in_specs,
            out_specs=out_specs,
            scratch_shapes=list(scratch),
        ),
        compiler_params=pltpu.CompilerParams(vmem_limit_bytes=VMEM_LIMIT),
    )


def shape(*dims, dtype=BF16):
    return jax.ShapeDtypeStruct(dims, dtype)


def exchange(v, axes):
    return lax.all_to_all(v, axes, 0, 0, tiled=True)


def to_other_core(v):
    return lax.ppermute(v, "core", [(0, 1), (1, 0)])


def local(inputs, cotangent, spec_weight, point_weight):
    tab = jnp.asarray(time_rows())
    forward, inverse = (jnp.asarray(v) for v in depth_rows())
    place = lax.axis_index(FIELD).reshape(1)
    field_block = pl.BlockSpec((1, 8, 64, DURATION), lambda b: (b, 0, 0, 0))
    part_block = pl.BlockSpec((16, 1, 8, 128), lambda b: (0, b, 0, 0))
    tab_block = whole((2, 64, DURATION))
    mix_block = whole((64, 64))
    forward_block = pl.BlockSpec((1, 64, 32), lambda i, f: (f[0], 0, 0))
    inverse_block = pl.BlockSpec((1, 16, 128), lambda i, f: (f[0], 0, 0))
    part = shape(16, 3, 8, 128)
    part4 = shape(16, 4, 8, 128)

    def spread(own, other, rows):
        scratch = [pltpu.VMEM((32 * rows, 128), F32)]
        if rows == ROWS:
            scratch.append(pltpu.VMEM((64, 128), F32))
        return call(
            lambda *refs: spread_kernel(*refs, rows=rows),
            shape(32, rows, 128),
            (1,),
            [whole(own.shape), whole(own.shape), forward_block],
            whole((32, rows, 128)),
            scratch,
            prefetch=1,
        )(place, own, other, forward)

    weights = call(
        weight_kernel, shape(16, 64, 128), (1,), [whole((16, 2, 64, 64))], whole((16, 64, 128))
    )(spec_weight)
    own, send = call(
        coeff_kernel,
        (part, part),
        (3,),
        [field_block, tab_block],
        (part_block, part_block),
        [pltpu.VMEM((256, 128), F32)],
    )(inputs, tab)
    got = exchange(spread(own, to_other_core(send), PAIRS), CHIP)
    mixed, spectrum = call(
        mix_kernel,
        (shape(32, PAIRS, 128), shape(PAIRS, 128, dtype=F32)),
        (1,),
        [whole((32, PAIRS, 128)), whole((16, 64, 128))],
        (whole((32, PAIRS, 128)), whole((PAIRS, 128))),
    )(got, weights)
    got = exchange(mixed, CHIP)
    own, send = call(
        lambda *refs: gather_kernel(*refs, rows=PAIRS),
        (part, part),
        (1,),
        [whole((32, PAIRS, 128)), inverse_block],
        (whole(part.shape), whole(part.shape)),
        [pltpu.VMEM((32 * PAIRS, 128), F32)],
        prefetch=1,
    )(place, got, inverse)
    dpre, own, send = call(
        field_kernel,
        (shape(3, 8, 64, DURATION), part4, part4),
        (3,),
        [field_block, field_block, part_block, part_block, tab_block, mix_block],
        (field_block, whole(part4.shape), whole(part4.shape)),
        [pltpu.VMEM((256, 128), F32), pltpu.VMEM((256, 128), F32), pltpu.VMEM((64, 64), F32)],
    )(inputs, cotangent, own, to_other_core(send), tab, point_weight)
    got = exchange(spread(own, to_other_core(send), ROWS), CHIP)
    dmodes, dmixed = call(
        adjoint_kernel,
        (shape(32, ROWS, 128), shape(PAIRS, 128, dtype=F32)),
        (1,),
        [whole((32, ROWS, 128)), whole((16, 64, 128))],
        (whole((32, ROWS, 128)), whole((PAIRS, 128))),
    )(got, weights)
    got = exchange(dmodes, CHIP)
    own, send, factors = call(
        lambda *refs: gather_kernel(*refs, rows=ROWS),
        (part, part, shape(4, 192, 128)),
        (1,),
        [whole((32, ROWS, 128)), inverse_block, whole((PAIRS, 128)), whole((PAIRS, 128))],
        (whole(part.shape), whole(part.shape), whole((4, 192, 128))),
        [pltpu.VMEM((32 * ROWS, 128), F32), pltpu.VMEM((192, 128), F32)],
        prefetch=1,
    )(place, got, inverse, spectrum, dmixed)
    factors = exchange(factors, "dp")
    input_grad = call(
        grad_kernel,
        shape(3, 8, 64, DURATION),
        (3,),
        [field_block, part_block, part_block, tab_block, mix_block],
        field_block,
        [pltpu.VMEM((256, 128), F32)],
    )(dpre, own, to_other_core(send), tab, point_weight)
    spec_grad, point_grad = call(
        weight_grad_kernel,
        (shape(16, 2, 64, 64, dtype=F32), shape(64, 64, dtype=F32)),
        (1,),
        [whole((4, 192, 128))],
        (whole((16, 2, 64, 64)), whole((64, 64))),
    )(factors)
    return (input_grad, spec_grad, point_grad)


def solution(mesh):
    fine = Mesh(mesh.devices.reshape(4, 2, 4, 4, 2), ("dp",) + FIELD)
    fields = P("dp", FIELD, None, None)
    weights = P(FIELD, None, None, None)
    return jax.shard_map(
        local,
        mesh=fine,
        in_specs=(fields, fields, weights, P()),
        out_specs=(fields, weights, P()),
        check_vma=False,
    )
```

```python
import math

import jax
import jax.numpy as jnp
import ml_dtypes
import numpy as np
from jax import lax
from jax.experimental import pallas as pl
from jax.experimental.pallas import tpu as pltpu
from jax.sharding import Mesh
from jax.sharding import PartitionSpec as P

DEPTH = 512
DURATION = 1024
CHANNELS = 64
DMODES = 32
TMODES = 32
BATCH = 12

CHIP = ("z", "y", "x")
FIELD = CHIP + ("core",)
BF16 = jnp.bfloat16
F32 = jnp.float32
SCALE = 1.0 / math.sqrt(DEPTH * DURATION)
INV_SCALE = 1.0 / math.sqrt(DMODES * TMODES)
NN = (((1,), (0,)), ((), ()))
NT = (((1,), (1,)), ((), ()))
MIB = 1024 * 1024
GROUPS = ((0, 3), (3, 3), (6, 2))
PAIRS = 48
ROWS = 56


def time_rows():
    m = np.arange(TMODES)
    phase = ((m[:, None] * np.arange(DURATION)[None, :]) % DURATION) * (2.0 * np.pi / DURATION)
    return np.concatenate([np.cos(phase), -np.sin(phase)], axis=0).astype(ml_dtypes.bfloat16)


def depth_rows():
    orders = np.arange(DMODES)
    freqs = np.where(orders < DMODES // 2, orders, orders - DMODES)
    forward, inverse = [], []
    for f in range(64):
        x = np.concatenate([f * 8 + np.arange(8), (f ^ 1) * 8 + np.arange(8)])
        phase = ((freqs[:, None] * x[None, :]) % DEPTH) * (2.0 * np.pi / DEPTH)
        both = np.concatenate([np.cos(phase), np.sin(phase)], axis=0)
        high = both.astype(ml_dtypes.bfloat16)
        low = (both - high.astype(np.float64)).astype(ml_dtypes.bfloat16)
        forward.append(np.concatenate([high, low], axis=1))
        inverse.append(np.concatenate([high, low], axis=0).T)
    return np.stack(forward), np.stack(inverse)


def lanes(shape):
    return lax.broadcasted_iota(jnp.int32, shape, len(shape) - 1)


def swap(v):
    return pltpu.roll(v, 64, 1)


def turn(v, first):
    return swap(v) * jnp.where(lanes(v.shape) < 64, first, -first).astype(F32)


def split_pair(v):
    high = v.astype(BF16).astype(F32)
    return jnp.where(lanes(v.shape) < 64, high, v - high)


def dot(a, b, dims=NN):
    return lax.dot_general(a, b, dims, preferred_element_type=F32)


def emit_rows(r, scratch):
    for xl in range(8):
        cols = slice(xl * 64, xl * 64 + 64)
        block = jnp.concatenate([r[:32, cols], r[32:, cols]], axis=1)
        scratch[pl.ds(xl, 32, stride=8), :] = block
    core = lax.axis_index("core")
    return [
        scratch[pl.ds(pl.multiple_of(c * 128, 128), 128), :].reshape(16, 8, 128).astype(BF16)
        for c in (core, 1 - core)
    ]


def load_rows(own_ref, other_ref, scratch):
    core = lax.axis_index("core")
    for c, ref in ((core, own_ref), (1 - core, other_ref)):
        scratch[pl.ds(pl.multiple_of(c * 128, 128), 128), :] = ref[:, 0].astype(F32).reshape(128, 128)


def mode_block(scratch, xl):
    g = scratch[pl.ds(xl, 32, stride=8), :]
    return jnp.concatenate([g[:, :64], g[:, 64:]], axis=0)


def left_of(blocks, mixing):
    zero = jnp.zeros((64, 64), BF16)
    rows = []
    for i, g in enumerate(blocks):
        rows.append(jnp.concatenate([g] + [mixing if k == i else zero for k in range(len(blocks))], axis=1))
    return jnp.concatenate(rows, axis=0)


def gelu_slope(pre, cot):
    root = math.sqrt(2.0 / math.pi)
    p = (root * 0.044715) * (pre * pre) + root
    th = jnp.tanh(pre * p)
    q = 3.0 * p - 2.0 * root
    return ((1.0 + th) * (1.0 + (pre * q) * (1.0 - th))) * (0.5 * cot)


def own_pair(kp, rows):
    row = lax.broadcasted_iota(jnp.int32, (rows, 128), 0)
    first = row - lanes((rows, 128)) // 64 * 3 - 6 * kp
    return (first >= 0) & (first < 3)


def weight_kernel(w_ref, o_ref):
    o_ref[...] = jnp.concatenate([w_ref[:, 0], w_ref[:, 1]], axis=2).astype(BF16)


def coeff_kernel(in_ref, tab_ref, own_ref, send_ref, scratch):
    r = dot(tab_ref[...], in_ref[0].reshape(512, DURATION), NT) * SCALE
    own_ref[:, 0], send_ref[:, 0] = emit_rows(r, scratch)


def spread_kernel(f_ref, own_ref, other_ref, tab_ref, o_ref, scratch, *point, rows):
    del f_ref
    table = tab_ref[0]
    both = jnp.concatenate([own_ref[:, :3].astype(F32), other_ref[:, :3].astype(F32)], axis=2).astype(BF16)
    both = both.reshape(PAIRS, 16, 128)
    for group in range(4):
        data = jnp.concatenate([both[group * 12 + i] for i in range(12)], axis=1)
        modes = dot(table, jnp.concatenate([data, data], axis=0))
        for i in range(12):
            cols = slice(i * 128, i * 128 + 128)
            part = modes[:32, cols] + turn(modes[32:, cols], 1.0)
            scratch[pl.ds(group * 12 + i, 32, stride=rows), :] = part
    if point:
        (pairs,) = point
        total = own_ref[:8, 3].astype(F32).reshape(64, 128) + other_ref[:8, 3].astype(F32).reshape(64, 128)
        pairs[...] = split_pair(total + swap(total))
        for i in range(2):
            scratch[pl.ds(PAIRS + i, 32, stride=rows), :] = pairs[pl.ds(i, 32, stride=2), :]
        for i in range(2, 8):
            scratch[pl.ds(PAIRS + i, 32, stride=rows), :] = jnp.zeros((32, 128), F32)
    o_ref[...] = scratch[...].reshape(32, rows, 128).astype(BF16)


def mix_kernel(recv_ref, w_ref, o_ref, spec_ref):
    spec = jnp.sum(recv_ref[...].astype(F32), axis=0)
    spec_ref[...] = spec
    low = lanes(spec.shape) < 64
    other = swap(spec)
    real = jnp.where(low, spec, other)
    imag = jnp.where(low, other, spec)
    cols = []
    for kp in range(8):
        own = own_pair(kp, PAIRS)
        cols.append(
            jnp.concatenate([jnp.where(own, real, 0.0), jnp.where(own, imag, 0.0)], axis=0).astype(BF16)
        )
    prod = dot(jnp.concatenate(cols, axis=1), w_ref[...].reshape(1024, 128))
    mixed = (prod[:PAIRS] + turn(prod[PAIRS:], -1.0)).astype(BF16)
    o_ref[...] = jnp.broadcast_to(mixed[None], (32, PAIRS, 128))


def adjoint_kernel(recv_ref, w_ref, o_ref, dmix_ref):
    total = jnp.sum(recv_ref[...].astype(F32), axis=0)
    dmix = total[:PAIRS]
    dmix_ref[...] = dmix
    both = jnp.concatenate([dmix, turn(dmix, 1.0)], axis=0).astype(BF16)
    prod = dot(both, w_ref[...].reshape(1024, 128), NT)
    real = jnp.zeros((PAIRS, 128), F32)
    imag = jnp.zeros((PAIRS, 128), F32)
    for kp in range(8):
        own = own_pair(kp, PAIRS)
        cols = slice(kp * 128, kp * 128 + 128)
        real = real + jnp.where(own, prod[:PAIRS, cols], 0.0)
        imag = imag + jnp.where(own, prod[PAIRS:, cols], 0.0)
    real = real + swap(real)
    imag = imag + swap(imag)
    dspec = jnp.where(lanes(real.shape) < 64, real, imag) * SCALE
    point = total[PAIRS:]
    point = split_pair(point + swap(point))
    message = jnp.concatenate([dspec, point], axis=0).astype(BF16)
    o_ref[...] = jnp.broadcast_to(message[None], (32, ROWS, 128))


def gather_kernel(f_ref, recv_ref, tab_ref, *rest, rows):
    del f_ref
    if rows == ROWS:
        spec_ref, dmix_ref, own_ref, send_ref, fact_ref, scratch, fact = rest
    else:
        own_ref, send_ref, scratch = rest
    table = tab_ref[0]
    scratch[...] = recv_ref[...].astype(F32).reshape(32 * rows, 128)
    for group in range(4):
        cols = []
        for i in range(12):
            modes = scratch[pl.ds(group * 12 + i, 32, stride=rows), :]
            pair = jnp.concatenate([modes, turn(modes, -1.0)], axis=0)
            cols.append(jnp.concatenate([pair, pair], axis=0).astype(BF16))
        back = dot(table, jnp.concatenate(cols, axis=1))
        for i in range(12):
            m, b = divmod(group * 12 + i, 3)
            part = back[:, i * 128 : i * 128 + 128].astype(BF16)
            own_ref[m, b] = part[:8]
            send_ref[m, b] = part[8:]
    if rows == ROWS:
        fact[...] = jnp.zeros_like(fact)
        fact[:PAIRS] = spec_ref[...]
        fact[64 : 64 + PAIRS] = dmix_ref[...]
        for i in range(2):
            fact[pl.ds(128 + i, 32, stride=2), :] = scratch[pl.ds(PAIRS + i, 32, stride=rows), :]
        whole_fact = fact[...].astype(BF16)
        fact_ref[...] = jnp.broadcast_to(whole_fact[None], (4, 192, 128))


def field_kernel(
    in_ref, cot_ref, got_ref, other_ref, tab_ref, w_ref, dpre_ref, own_ref, send_ref, rows, scratch, point
):
    b = pl.program_id(0)

    @pl.when(b == 0)
    def _():
        point[...] = jnp.zeros_like(point)

    load_rows(got_ref, other_ref, rows)
    mix_t = w_ref[...].astype(F32).T.astype(BF16)
    total = point[...]
    drows = []
    for first, n in GROUPS:
        blocks = [(mode_block(rows, first + i).T * INV_SCALE).astype(BF16) for i in range(n)]
        left = left_of(blocks, mix_t)
        for chunk in range(4):
            ts = slice(chunk * 256, chunk * 256 + 256)
            right = jnp.concatenate(
                [tab_ref[:, ts]] + [in_ref[0, first + i, :, ts] for i in range(n)], axis=0
            )
            pre = dot(left, right)
            for i in range(n):
                slope = gelu_slope(pre[i * 64 : i * 64 + 64], cot_ref[0, first + i, :, ts].astype(F32))
                dpre_ref[0, first + i, :, ts] = slope.astype(BF16)
        left = jnp.concatenate([tab_ref[...]] + [in_ref[0, first + i] for i in range(n)], axis=0)
        r = dot(left, dpre_ref[0, first : first + n].reshape(n * 64, DURATION), NT)
        drows.append(r[:64])
        for i in range(n):
            total = total + r[64 + i * 64 : 128 + i * 64, i * 64 : i * 64 + 64]
    point[...] = total
    out = emit_rows(jnp.concatenate(drows, axis=1) * INV_SCALE, scratch)
    own_ref[:, b], send_ref[:, b] = out

    @pl.when(b == 2)
    def _():
        pair = split_pair(jnp.concatenate([total, total], axis=1))
        pair = jnp.concatenate([pair, jnp.zeros_like(pair)], axis=0).reshape(16, 8, 128).astype(BF16)
        own_ref[:, 3] = pair
        send_ref[:, 3] = pair


def grad_kernel(dpre_ref, got_ref, other_ref, tab_ref, w_ref, o_ref, rows):
    load_rows(got_ref, other_ref, rows)
    mixing = w_ref[...]
    for first, n in GROUPS:
        left = left_of([mode_block(rows, first + i).T.astype(BF16) for i in range(n)], mixing)
        for chunk in range(4):
            ts = slice(chunk * 256, chunk * 256 + 256)
            right = jnp.concatenate(
                [tab_ref[:, ts]] + [dpre_ref[0, first + i, :, ts] for i in range(n)], axis=0
            )
            grad = dot(left, right).astype(BF16)
            for i in range(n):
                o_ref[0, first + i, :, ts] = grad[i * 64 : i * 64 + 64]


def weight_grad_kernel(fact_ref, spec_ref, point_ref):
    fact = fact_ref[...].astype(F32)
    turned = fact[:, :64].reshape(256, 128).T
    real = turned[:64]
    imag = turned[64:]
    left = jnp.concatenate([real, imag], axis=1)
    row = lanes((64, 512)) % 64
    d = fact[:, 64:128].reshape(256, 128)
    right = jnp.concatenate([d, turn(d, 1.0)], axis=0).astype(BF16)
    parts = [
        jnp.where((row >= 3 * m) & (row < 3 * m + 3), left, 0.0).astype(BF16) for m in range(16)
    ]
    g = dot(jnp.concatenate(parts, axis=0), right) * (1.0 / math.sqrt(BATCH * DEPTH))
    g = g.reshape(16, 64, 128)
    spec_ref[:, 0] = g[:, :, :64]
    spec_ref[:, 1] = g[:, :, 64:]
    point = fact[0, 128:] + fact[1, 128:] + fact[2, 128:] + fact[3, 128:]
    point = (point + swap(point)) * (1.0 / math.sqrt(BATCH * DEPTH * DURATION))
    point_ref[...] = point[:, :64]


def whole(shape):
    return pl.BlockSpec(shape, lambda *_: (0,) * len(shape))


def call(kernel, out_shape, grid, in_specs, out_specs, scratch=(), prefetch=0, limit=8):
    return pl.pallas_call(
        kernel,
        out_shape=out_shape,
        grid_spec=pltpu.PrefetchScalarGridSpec(
            num_scalar_prefetch=prefetch,
            grid=grid,
            in_specs=in_specs,
            out_specs=out_specs,
            scratch_shapes=list(scratch),
        ),
        compiler_params=pltpu.CompilerParams(vmem_limit_bytes=limit * MIB),
    )


def shape(*dims, dtype=BF16):
    return jax.ShapeDtypeStruct(dims, dtype)


def exchange(v, axes):
    return lax.all_to_all(v, axes, 0, 0, tiled=True)


def to_other_core(v):
    return lax.ppermute(v, "core", [(0, 1), (1, 0)])


def local(inputs, cotangent, spec_weight, point_weight):
    tab = jnp.asarray(time_rows())
    forward, inverse = (jnp.asarray(v) for v in depth_rows())
    place = lax.axis_index(FIELD).reshape(1)
    field_block = pl.BlockSpec((1, 8, 64, DURATION), lambda b: (b, 0, 0, 0))
    part_block = pl.BlockSpec((16, 1, 8, 128), lambda b: (0, b, 0, 0))
    tab_block = whole((64, DURATION))
    mix_block = whole((64, 64))
    forward_block = pl.BlockSpec((1, 64, 32), lambda i, f: (f[0], 0, 0))
    inverse_block = pl.BlockSpec((1, 16, 128), lambda i, f: (f[0], 0, 0))
    part = shape(16, 3, 8, 128)
    part4 = shape(16, 4, 8, 128)

    def spread(own, other, rows):
        scratch = [pltpu.VMEM((32 * rows, 128), F32)]
        if rows == ROWS:
            scratch.append(pltpu.VMEM((64, 128), F32))
        return call(
            lambda *refs: spread_kernel(*refs, rows=rows),
            shape(32, rows, 128),
            (1,),
            [whole(own.shape), whole(own.shape), forward_block],
            whole((32, rows, 128)),
            scratch,
            prefetch=1,
        )(place, own, other, forward)

    weights = call(
        weight_kernel, shape(16, 64, 128), (1,), [whole((16, 2, 64, 64))], whole((16, 64, 128))
    )(spec_weight)
    own, send = call(
        coeff_kernel,
        (part, part),
        (3,),
        [field_block, tab_block],
        (part_block, part_block),
        [pltpu.VMEM((256, 128), F32)],
        limit=14,
    )(inputs, tab)
    got = exchange(spread(own, to_other_core(send), PAIRS), CHIP)
    mixed, spectrum = call(
        mix_kernel,
        (shape(32, PAIRS, 128), shape(PAIRS, 128, dtype=F32)),
        (1,),
        [whole((32, PAIRS, 128)), whole((16, 64, 128))],
        (whole((32, PAIRS, 128)), whole((PAIRS, 128))),
    )(got, weights)
    got = exchange(mixed, CHIP)
    own, send = call(
        lambda *refs: gather_kernel(*refs, rows=PAIRS),
        (part, part),
        (1,),
        [whole((32, PAIRS, 128)), inverse_block],
        (whole(part.shape), whole(part.shape)),
        [pltpu.VMEM((32 * PAIRS, 128), F32)],
        prefetch=1,
    )(place, got, inverse)
    dpre, own, send = call(
        field_kernel,
        (shape(3, 8, 64, DURATION), part4, part4),
        (3,),
        [field_block, field_block, part_block, part_block, tab_block, mix_block],
        (field_block, whole(part4.shape), whole(part4.shape)),
        [pltpu.VMEM((256, 128), F32), pltpu.VMEM((256, 128), F32), pltpu.VMEM((64, 64), F32)],
        limit=14,
    )(inputs, cotangent, own, to_other_core(send), tab, point_weight)
    got = exchange(spread(own, to_other_core(send), ROWS), CHIP)
    dmodes, dmixed = call(
        adjoint_kernel,
        (shape(32, ROWS, 128), shape(PAIRS, 128, dtype=F32)),
        (1,),
        [whole((32, ROWS, 128)), whole((16, 64, 128))],
        (whole((32, ROWS, 128)), whole((PAIRS, 128))),
    )(got, weights)
    got = exchange(dmodes, CHIP)
    own, send, factors = call(
        lambda *refs: gather_kernel(*refs, rows=ROWS),
        (part, part, shape(4, 192, 128)),
        (1,),
        [whole((32, ROWS, 128)), inverse_block, whole((PAIRS, 128)), whole((PAIRS, 128))],
        (whole(part.shape), whole(part.shape), whole((4, 192, 128))),
        [pltpu.VMEM((32 * ROWS, 128), F32), pltpu.VMEM((192, 128), F32)],
        prefetch=1,
    )(place, got, inverse, spectrum, dmixed)
    factors = exchange(factors, "dp")
    input_grad = call(
        grad_kernel,
        shape(3, 8, 64, DURATION),
        (3,),
        [field_block, part_block, part_block, tab_block, mix_block],
        field_block,
        [pltpu.VMEM((256, 128), F32)],
        limit=14,
    )(dpre, own, to_other_core(send), tab, point_weight)
    spec_grad, point_grad = call(
        weight_grad_kernel,
        (shape(16, 2, 64, 64, dtype=F32), shape(64, 64, dtype=F32)),
        (1,),
        [whole((4, 192, 128))],
        (whole((16, 2, 64, 64)), whole((64, 64))),
    )(factors)
    return (input_grad, spec_grad, point_grad)


def solution(mesh):
    fine = Mesh(mesh.devices.reshape(4, 2, 4, 4, 2), ("dp",) + FIELD)
    fields = P("dp", FIELD, None, None)
    weights = P(FIELD, None, None, None)
    return jax.shard_map(
        local,
        mesh=fine,
        in_specs=(fields, fields, weights, P()),
        out_specs=(fields, weights, P()),
        check_vma=False,
    )
```

```python
import functools
import math

import jax
import jax.numpy as jnp
import ml_dtypes
import numpy as np
from jax import lax
from jax.experimental import pallas as pl
from jax.experimental.pallas import tpu as pltpu
from jax.sharding import Mesh
from jax.sharding import PartitionSpec as P

DEPTH = 512
DURATION = 1024
CHANNELS = 64
DMODES = 32
TMODES = 32
BATCH = 12

CHIP = ("z", "y", "x")
FIELD = CHIP + ("core",)
BF16 = jnp.bfloat16
F32 = jnp.float32
SCALE = 1.0 / math.sqrt(DEPTH * DURATION)
INV_SCALE = 1.0 / math.sqrt(DMODES * TMODES)
NN = (((1,), (0,)), ((), ()))
NT = (((1,), (1,)), ((), ()))
MIB = 1024 * 1024
FIELDS = 24
GROUPS = 8
PAIRS = 48
ROWS = 56


def time_rows():
    m = np.arange(TMODES)
    phase = ((m[:, None] * np.arange(DURATION)[None, :]) % DURATION) * (2.0 * np.pi / DURATION)
    return np.concatenate([np.cos(phase), -np.sin(phase)], axis=0).astype(ml_dtypes.bfloat16)


def depth_table(k, x, sine):
    freq = jnp.where(k < DMODES // 2, k, k - DMODES)
    phase = ((freq * x - jnp.where(sine, DEPTH // 4, 0) + DEPTH // 2) & (DEPTH - 1)) - DEPTH // 2
    return jnp.cos(phase.astype(F32) * (2.0 * math.pi / DEPTH))


def high_or_low(v, low):
    high = v.astype(BF16).astype(F32)
    return jnp.where(low, v - high, high).astype(BF16)


def position(i):
    return 8 * (lax.axis_index(FIELD) ^ (i >> 3)) + (i & 7)


def forward_table():
    row = lax.broadcasted_iota(jnp.int32, (64, 32), 0)
    col = lax.broadcasted_iota(jnp.int32, (64, 32), 1)
    return high_or_low(depth_table(row & 31, position(col & 15), row >= 32), col >= 16)


def inverse_table():
    row = lax.broadcasted_iota(jnp.int32, (16, 128), 0)
    col = lax.broadcasted_iota(jnp.int32, (16, 128), 1)
    return high_or_low(depth_table(col & 31, position(row), (col & 32) != 0), col >= 64)


def lanes(shape):
    return lax.broadcasted_iota(jnp.int32, shape, len(shape) - 1)


def swap(v):
    return pltpu.roll(v, 64, 1)


def turn(v, first):
    return swap(v) * jnp.where(lanes(v.shape) < 64, first, -first).astype(F32)


def split_pair(v):
    high = v.astype(BF16).astype(F32)
    return jnp.where(lanes(v.shape) < 64, high, v - high)


def dot(a, b, dims=NN):
    return lax.dot_general(a, b, dims, preferred_element_type=F32)


def store_rows(scratch, own_ref, send_ref):
    core = lax.axis_index("core")
    for b in range(3):
        for c, ref in ((core, own_ref), (1 - core, send_ref)):
            rows = scratch[pl.ds(pl.multiple_of(b * 256 + c * 128, 128), 128), :]
            ref[:, b] = rows.reshape(16, 8, 128).astype(BF16)


def load_rows(own_ref, other_ref, scratch):
    core = lax.axis_index("core")
    for b in range(3):
        for c, ref in ((core, own_ref), (1 - core, other_ref)):
            rows = ref[:, b].astype(F32).reshape(128, 128)
            scratch[pl.ds(pl.multiple_of(b * 256 + c * 128, 128), 128), :] = rows


def field_rows(field):
    b, xl = divmod(field, 8)
    return pl.ds(b * 256 + xl, 32, stride=8)


def mode_block(scratch, field):
    g = scratch[field_rows(field), :]
    return jnp.concatenate([g[:, :64], g[:, 64:]], axis=0).T


def left_of(blocks, mixing):
    zero = jnp.zeros((64, 64), BF16)
    rows = []
    for i, g in enumerate(blocks):
        rows.append(jnp.concatenate([g] + [mixing if k == i else zero for k in range(len(blocks))], axis=1))
    return jnp.concatenate(rows, axis=0)


def gelu_slope(pre, cot):
    root = math.sqrt(2.0 / math.pi)
    p = (root * 0.044715) * (pre * pre) + root
    th = jnp.tanh(pre * p)
    q = 3.0 * p - 2.0 * root
    return ((1.0 + th) * (1.0 + (pre * q) * (1.0 - th))) * (0.5 * cot)


def own_pair(kp, rows):
    row = lax.broadcasted_iota(jnp.int32, (rows, 128), 0)
    first = row - lanes((rows, 128)) // 64 * 3 - 6 * kp
    return (first >= 0) & (first < 3)


def coeff_kernel(
    in_ref, tab_ref, mix_ref, own_ref, send_ref, table, mixing, fields, scratch, sems
):
    copies = [
        pltpu.make_async_copy(tab_ref, table, sems.at[3]),
        pltpu.make_async_copy(mix_ref, mixing, sems.at[4]),
    ]
    for b in range(3):
        part = pl.ds(8 * b, 8)
        copies.append(pltpu.make_async_copy(in_ref.at[part], fields.at[part], sems.at[b]))
    for copy in copies:
        copy.start()
    copies[0].wait()
    for b in range(3):
        copies[2 + b].wait()
        coeffs = dot(table[...], fields[8 * b : 8 * b + 8].reshape(512, DURATION), NT) * SCALE
        for i in range(8):
            cols = slice(i * 64, i * 64 + 64)
            scratch[field_rows(8 * b + i), :] = jnp.concatenate([coeffs[:32, cols], coeffs[32:, cols]], axis=1)
    store_rows(scratch, own_ref, send_ref)
    copies[1].wait()


def weight_kernel(w_ref, o_ref, scratch, sem):
    copy = pltpu.make_async_copy(w_ref, scratch, sem)
    copy.start()
    copy.wait()
    o_ref[...] = jnp.concatenate([scratch[:, 0], scratch[:, 1]], axis=2).astype(BF16)


def spread_kernel(own_ref, other_ref, o_ref, scratch, *point, rows):
    table = forward_table()
    both = jnp.concatenate([own_ref[:, :3].astype(F32), other_ref[:, :3].astype(F32)], axis=2).astype(BF16)
    both = both.reshape(PAIRS, 16, 128)
    for group in range(4):
        data = jnp.concatenate([both[group * 12 + i] for i in range(12)], axis=1)
        modes = dot(table, jnp.concatenate([data, data], axis=0))
        for i in range(12):
            cols = slice(i * 128, i * 128 + 128)
            part = modes[:32, cols] + turn(modes[32:, cols], 1.0)
            scratch[pl.ds(group * 12 + i, 32, stride=rows), :] = part
    if point:
        (pairs,) = point
        total = own_ref[:8, 3].astype(F32).reshape(64, 128) + other_ref[:8, 3].astype(F32).reshape(64, 128)
        pairs[...] = split_pair(total + swap(total))
        for i in range(2):
            scratch[pl.ds(PAIRS + i, 32, stride=rows), :] = pairs[pl.ds(i, 32, stride=2), :]
        for i in range(2, 8):
            scratch[pl.ds(PAIRS + i, 32, stride=rows), :] = jnp.zeros((32, 128), F32)
    o_ref[...] = scratch[...].reshape(32, rows, 128).astype(BF16)


def mix_kernel(recv_ref, w_ref, o_ref, spec_ref):
    spec = jnp.sum(recv_ref[...].astype(F32), axis=0)
    spec_ref[...] = spec
    low = lanes(spec.shape) < 64
    other = swap(spec)
    real = jnp.where(low, spec, other)
    imag = jnp.where(low, other, spec)
    cols = []
    for kp in range(8):
        own = own_pair(kp, PAIRS)
        cols.append(
            jnp.concatenate([jnp.where(own, real, 0.0), jnp.where(own, imag, 0.0)], axis=0).astype(BF16)
        )
    prod = dot(jnp.concatenate(cols, axis=1), w_ref[...].reshape(1024, 128))
    mixed = (prod[:PAIRS] + turn(prod[PAIRS:], -1.0)).astype(BF16)
    o_ref[...] = jnp.broadcast_to(mixed[None], (32, PAIRS, 128))


def adjoint_kernel(recv_ref, w_ref, o_ref, dmix_ref):
    total = jnp.sum(recv_ref[...].astype(F32), axis=0)
    dmix = total[:PAIRS]
    dmix_ref[...] = dmix
    both = jnp.concatenate([dmix, turn(dmix, 1.0)], axis=0).astype(BF16)
    prod = dot(both, w_ref[...].reshape(1024, 128), NT)
    real = jnp.zeros((PAIRS, 128), F32)
    imag = jnp.zeros((PAIRS, 128), F32)
    for kp in range(8):
        own = own_pair(kp, PAIRS)
        cols = slice(kp * 128, kp * 128 + 128)
        real = real + jnp.where(own, prod[:PAIRS, cols], 0.0)
        imag = imag + jnp.where(own, prod[PAIRS:, cols], 0.0)
    real = real + swap(real)
    imag = imag + swap(imag)
    dspec = jnp.where(lanes(real.shape) < 64, real, imag) * SCALE
    point = total[PAIRS:]
    point = split_pair(point + swap(point))
    message = jnp.concatenate([dspec, point], axis=0).astype(BF16)
    o_ref[...] = jnp.broadcast_to(message[None], (32, ROWS, 128))


def gather_kernel(recv_ref, *rest, rows):
    if rows == ROWS:
        spec_ref, dmix_ref, own_ref, send_ref, fact_ref, scratch, fact = rest
    else:
        own_ref, send_ref, scratch = rest
    table = inverse_table()
    scratch[...] = recv_ref[...].astype(F32).reshape(32 * rows, 128)
    for group in range(4):
        cols = []
        for i in range(12):
            modes = scratch[pl.ds(group * 12 + i, 32, stride=rows), :]
            pair = jnp.concatenate([modes, turn(modes, -1.0)], axis=0)
            cols.append(jnp.concatenate([pair, pair], axis=0).astype(BF16))
        back = dot(table, jnp.concatenate(cols, axis=1))
        for i in range(12):
            m, b = divmod(group * 12 + i, 3)
            part = back[:, i * 128 : i * 128 + 128].astype(BF16)
            own_ref[m, b] = part[:8]
            send_ref[m, b] = part[8:]
    if rows == ROWS:
        fact[:PAIRS] = spec_ref[...]
        fact[PAIRS : 2 * PAIRS] = dmix_ref[...]
        for i in range(2):
            fact[pl.ds(2 * PAIRS + i, 32, stride=2), :] = scratch[pl.ds(PAIRS + i, 32, stride=rows), :]
        whole_fact = fact[...].astype(BF16)
        fact_ref[...] = jnp.broadcast_to(whole_fact[None], (4, 160, 128))


def field_kernel(
    in_ref, cot_ref, got_ref, other_ref, tab_ref, w_ref, dpre_ref, own_ref, send_ref, rows, scratch, dpre, sems
):
    load_rows(got_ref, other_ref, rows)
    mix_t = w_ref[...].astype(F32).T.astype(BF16)
    point = jnp.zeros((64, 64), F32)
    copies = []
    for g in range(GROUPS):
        fields = [3 * g + i for i in range(3)]
        left = left_of([(mode_block(rows, f) * INV_SCALE).astype(BF16) for f in fields], mix_t)
        for chunk in range(4):
            ts = slice(chunk * 256, chunk * 256 + 256)
            right = jnp.concatenate([tab_ref[:, ts]] + [in_ref[f, :, ts] for f in fields], axis=0)
            pre = dot(left, right)
            for i, f in enumerate(fields):
                slope = gelu_slope(pre[i * 64 : i * 64 + 64], cot_ref[f, :, ts].astype(F32))
                dpre[f, :, ts] = slope.astype(BF16)
        part = pl.ds(3 * g, 3)
        copies.append(pltpu.make_async_copy(dpre.at[part], dpre_ref.at[part], sems.at[g]))
        copies[g].start()
        left = jnp.concatenate([tab_ref[...]] + [in_ref[f] for f in fields], axis=0)
        r = dot(left, dpre[3 * g : 3 * g + 3].reshape(192, DURATION), NT)
        for i, f in enumerate(fields):
            cols = slice(i * 64, i * 64 + 64)
            point = point + r[64 + i * 64 : 128 + i * 64, cols]
            drows = jnp.concatenate([r[:32, cols], r[32:64, cols]], axis=1)
            scratch[field_rows(f), :] = drows * INV_SCALE
    store_rows(scratch, own_ref, send_ref)
    pair = split_pair(jnp.concatenate([point, point], axis=1))
    pair = jnp.concatenate([pair, jnp.zeros_like(pair)], axis=0).reshape(16, 8, 128).astype(BF16)
    own_ref[:, 3] = pair
    send_ref[:, 3] = pair
    for copy in copies:
        copy.wait()


def grad_kernel(
    dpre_ref, got_ref, other_ref, tab_ref, w_ref, o_ref, rows, dpre, grad, in_sems, out_sems
):
    ins, outs = [], []
    for g in range(GROUPS):
        part = pl.ds(3 * g, 3)
        ins.append(pltpu.make_async_copy(dpre_ref.at[part], dpre.at[part], in_sems.at[g]))
        outs.append(pltpu.make_async_copy(grad.at[part], o_ref.at[part], out_sems.at[g]))
        ins[g].start()
    load_rows(got_ref, other_ref, rows)
    mixing = w_ref[...]
    for g in range(GROUPS):
        fields = [3 * g + i for i in range(3)]
        left = left_of([mode_block(rows, f).astype(BF16) for f in fields], mixing)
        ins[g].wait()
        for chunk in range(4):
            ts = slice(chunk * 256, chunk * 256 + 256)
            right = jnp.concatenate([tab_ref[:, ts]] + [dpre[f, :, ts] for f in fields], axis=0)
            total = dot(left, right).astype(BF16)
            for i, f in enumerate(fields):
                grad[f, :, ts] = total[i * 64 : i * 64 + 64]
        outs[g].start()
    for copy in outs:
        copy.wait()


def weight_grad_kernel(fact_ref, spec_ref, point_ref):
    fact = fact_ref[...].astype(F32)
    place = lanes((1, 256)) & 127
    place = place - 24 * ((place * 171) >> 12)
    mode = (place * 43) >> 7
    empty = jnp.zeros((32, 128), F32)
    for half in range(2):
        rows = slice(half * 24, half * 24 + 24)
        s = jnp.concatenate([fact[:, rows].reshape(96, 128), empty], axis=0).T
        d = jnp.concatenate([fact[:, 48:96][:, rows].reshape(96, 128), empty], axis=0)
        left = jnp.concatenate([s[:64], s[64:]], axis=1)
        right = jnp.concatenate([d, turn(d, 1.0)], axis=0).astype(BF16)
        parts = [jnp.where(mode == m, left, 0.0).astype(BF16) for m in range(8)]
        g = dot(jnp.concatenate(parts, axis=0), right) * (1.0 / math.sqrt(BATCH * DEPTH))
        g = g.reshape(8, 64, 128)
        modes = slice(half * 8, half * 8 + 8)
        spec_ref[modes, 0] = g[:, :, :64]
        spec_ref[modes, 1] = g[:, :, 64:]
    point = fact[0, 96:] + fact[1, 96:] + fact[2, 96:] + fact[3, 96:]
    point = (point + swap(point)) * (1.0 / math.sqrt(BATCH * DEPTH * DURATION))
    point_ref[...] = point[:, :64]


FAST = pl.BlockSpec(memory_space=pltpu.VMEM)
SLOW = pl.BlockSpec(memory_space=pl.ANY)


def call(kernel, out_shape, in_specs, out_specs, scratch=(), limit=8):
    return pl.pallas_call(
        kernel,
        out_shape=out_shape,
        in_specs=in_specs,
        out_specs=out_specs,
        scratch_shapes=list(scratch),
        compiler_params=pltpu.CompilerParams(vmem_limit_bytes=limit * MIB),
    )


def shape(*dims, dtype=BF16):
    return jax.ShapeDtypeStruct(dims, dtype)


def exchange(v, axes):
    return lax.all_to_all(v, axes, 0, 0, tiled=True)


def to_other_core(v):
    return lax.ppermute(v, "core", [(0, 1), (1, 0)])


def spread(own, other, rows):
    scratch = [pltpu.VMEM((32 * rows, 128), F32)]
    if rows == ROWS:
        scratch.append(pltpu.VMEM((64, 128), F32))
    kernel = functools.partial(spread_kernel, rows=rows)
    return call(kernel, shape(32, rows, 128), [FAST] * 2, FAST, scratch)(own, other)


def local(inputs, cotangent, spec_weight, point_weight):
    tab = jnp.asarray(time_rows())
    fields = inputs.reshape(FIELDS, CHANNELS, DURATION)
    cots = cotangent.reshape(FIELDS, CHANNELS, DURATION)
    part = shape(16, 3, 8, 128)
    part4 = shape(16, 4, 8, 128)
    rows = pltpu.VMEM((FIELDS * 32, 128), F32)
    whole_field = pltpu.VMEM((FIELDS, CHANNELS, DURATION), BF16)
    sems = pltpu.SemaphoreType.DMA((GROUPS,))

    own, send, table, mixing, fields = call(
        coeff_kernel,
        (
            pltpu.VMEM((16, 3, 8, 128), BF16),
            pltpu.VMEM((16, 3, 8, 128), BF16),
            pltpu.VMEM((64, DURATION), BF16),
            pltpu.VMEM((CHANNELS, CHANNELS), BF16),
            pltpu.VMEM((FIELDS, CHANNELS, DURATION), BF16),
        ),
        [SLOW] * 3,
        (FAST,) * 5,
        [rows, pltpu.SemaphoreType.DMA((5,))],
        limit=56,
    )(*(pltpu.with_memory_space_constraint(v, pltpu.HBM) for v in (fields, tab, point_weight)))
    weights = call(
        weight_kernel,
        shape(16, 64, 128),
        [SLOW],
        FAST,
        [pltpu.VMEM((16, 2, CHANNELS, CHANNELS), F32), pltpu.SemaphoreType.DMA],
    )(pltpu.with_memory_space_constraint(spec_weight, pltpu.HBM))
    other, weights = lax.optimization_barrier((to_other_core(send), weights))
    got = exchange(spread(own, other, PAIRS), CHIP)
    mixed, spectrum = call(
        mix_kernel,
        (shape(32, PAIRS, 128), shape(PAIRS, 128, dtype=F32)),
        [FAST] * 2,
        (FAST,) * 2,
    )(got, weights)
    got = exchange(mixed, CHIP)
    own, send = call(
        functools.partial(gather_kernel, rows=PAIRS),
        (part, part),
        [FAST],
        (FAST, FAST),
        [pltpu.VMEM((32 * PAIRS, 128), F32)],
    )(got)
    dpre, own, send = call(
        field_kernel,
        (pltpu.HBM((FIELDS, CHANNELS, DURATION), BF16), part4, part4),
        [FAST] * 6,
        (SLOW, FAST, FAST),
        [rows, rows, whole_field, sems],
        limit=16,
    )(pltpu.with_memory_space_constraint(fields, pltpu.VMEM), cots, own, to_other_core(send), table, mixing)
    got = exchange(spread(own, to_other_core(send), ROWS), CHIP)
    dmodes, dmixed = call(
        adjoint_kernel,
        (shape(32, ROWS, 128), shape(PAIRS, 128, dtype=F32)),
        [FAST] * 2,
        (FAST, FAST),
    )(got, weights)
    got = exchange(dmodes, CHIP)
    own, send, factors = call(
        functools.partial(gather_kernel, rows=ROWS),
        (part, part, shape(4, 160, 128)),
        [FAST] * 3,
        (FAST,) * 3,
        [pltpu.VMEM((32 * ROWS, 128), F32), pltpu.VMEM((160, 128), F32)],
    )(got, spectrum, dmixed)
    factors = exchange(factors, "dp")
    input_grad = call(
        grad_kernel,
        pltpu.HBM((FIELDS, CHANNELS, DURATION), BF16),
        [SLOW] + [FAST] * 4,
        SLOW,
        [rows, whole_field, whole_field, sems, sems],
        limit=16,
    )(pltpu.with_memory_space_constraint(dpre, pltpu.HBM), own, to_other_core(send), table, mixing)
    spec_grad, point_grad = call(
        weight_grad_kernel,
        (shape(16, 2, 64, 64, dtype=F32), shape(64, 64, dtype=F32)),
        [FAST],
        (FAST, FAST),
    )(factors)
    return (input_grad.reshape(inputs.shape), spec_grad, point_grad)


def solution(mesh):
    fine = Mesh(mesh.devices.reshape(4, 2, 4, 4, 2), ("dp",) + FIELD)
    fields = P("dp", FIELD, None, None)
    weights = P(FIELD, None, None, None)
    return jax.shard_map(
        local,
        mesh=fine,
        in_specs=(fields, fields, weights, P()),
        out_specs=(fields, weights, P()),
        check_vma=False,
    )
```

```python
import functools
import math

import jax
import jax.numpy as jnp
import ml_dtypes
import numpy as np
from jax import lax
from jax.experimental import pallas as pl
from jax.experimental.pallas import tpu as pltpu
from jax.sharding import Mesh
from jax.sharding import PartitionSpec as P

DEPTH = 512
DURATION = 1024
CHANNELS = 64
DMODES = 32
TMODES = 32
BATCH = 12

CHIP = ("z", "y", "x")
FIELD = CHIP + ("core",)
BF16 = jnp.bfloat16
F32 = jnp.float32
SCALE = 1.0 / math.sqrt(DEPTH * DURATION)
INV_SCALE = 1.0 / math.sqrt(DMODES * TMODES)
NN = (((1,), (0,)), ((), ()))
NT = (((1,), (1,)), ((), ()))
MIB = 1024 * 1024
FIELDS = 24
GROUPS = 8
PAIRS = 48
ROWS = 56


def time_rows():
    m = np.arange(TMODES)
    phase = ((m[:, None] * np.arange(DURATION)[None, :]) % DURATION) * (2.0 * np.pi / DURATION)
    return np.concatenate([np.cos(phase), -np.sin(phase)], axis=0).astype(ml_dtypes.bfloat16)


def depth_table(k, x, sine):
    freq = jnp.where(k < DMODES // 2, k, k - DMODES)
    phase = ((freq * x - jnp.where(sine, DEPTH // 4, 0) + DEPTH // 2) & (DEPTH - 1)) - DEPTH // 2
    return jnp.cos(phase.astype(F32) * (2.0 * math.pi / DEPTH))


def high_or_low(v, low):
    high = v.astype(BF16).astype(F32)
    return jnp.where(low, v - high, high).astype(BF16)


def position(i):
    return 8 * (lax.axis_index(FIELD) ^ (i >> 3)) + (i & 7)


def forward_table():
    row = lax.broadcasted_iota(jnp.int32, (64, 32), 0)
    col = lax.broadcasted_iota(jnp.int32, (64, 32), 1)
    return high_or_low(depth_table(row & 31, position(col & 15), row >= 32), col >= 16)


def inverse_table():
    row = lax.broadcasted_iota(jnp.int32, (16, 128), 0)
    col = lax.broadcasted_iota(jnp.int32, (16, 128), 1)
    return high_or_low(depth_table(col & 31, position(row), (col & 32) != 0), col >= 64)


def lanes(shape):
    return lax.broadcasted_iota(jnp.int32, shape, len(shape) - 1)


def swap(v):
    return pltpu.roll(v, 64, 1)


def turn(v, first):
    return swap(v) * jnp.where(lanes(v.shape) < 64, first, -first).astype(F32)


def split_pair(v):
    high = v.astype(BF16).astype(F32)
    return jnp.where(lanes(v.shape) < 64, high, v - high)


def dot(a, b, dims=NN):
    return lax.dot_general(a, b, dims, preferred_element_type=F32)


def store_rows(scratch, own_ref, send_ref):
    core = lax.axis_index("core")
    for b in range(3):
        for c, ref in ((core, own_ref), (1 - core, send_ref)):
            rows = scratch[pl.ds(pl.multiple_of(b * 256 + c * 128, 128), 128), :]
            ref[:, b] = rows.reshape(16, 8, 128).astype(BF16)


def load_rows(own_ref, other_ref, scratch):
    core = lax.axis_index("core")
    for b in range(3):
        for c, ref in ((core, own_ref), (1 - core, other_ref)):
            rows = ref[:, b].astype(F32).reshape(128, 128)
            scratch[pl.ds(pl.multiple_of(b * 256 + c * 128, 128), 128), :] = rows


def field_rows(field):
    b, xl = divmod(field, 8)
    return pl.ds(b * 256 + xl, 32, stride=8)


def mode_block(scratch, field):
    g = scratch[field_rows(field), :]
    return jnp.concatenate([g[:, :64], g[:, 64:]], axis=0).T


def left_of(blocks, mixing):
    zero = jnp.zeros((64, 64), BF16)
    rows = []
    for i, g in enumerate(blocks):
        rows.append(jnp.concatenate([g] + [mixing if k == i else zero for k in range(len(blocks))], axis=1))
    return jnp.concatenate(rows, axis=0)


def gelu_slope(pre, cot):
    root = math.sqrt(2.0 / math.pi)
    p = (root * 0.044715) * (pre * pre) + root
    th = jnp.tanh(pre * p)
    q = 3.0 * p - 2.0 * root
    return ((1.0 + th) * (1.0 + (pre * q) * (1.0 - th))) * (0.5 * cot)


def own_pair(kp, rows):
    row = lax.broadcasted_iota(jnp.int32, (rows, 128), 0)
    first = row - lanes((rows, 128)) // 64 * 3 - 6 * kp
    return (first >= 0) & (first < 3)


def coeff_kernel(
    in_ref, tab_ref, mix_ref, own_ref, send_ref, table, mixing, fields, scratch, sems
):
    copies = [
        pltpu.make_async_copy(tab_ref, table, sems.at[3]),
        pltpu.make_async_copy(mix_ref, mixing, sems.at[4]),
    ]
    for b in range(3):
        part = pl.ds(8 * b, 8)
        copies.append(pltpu.make_async_copy(in_ref.at[part], fields.at[part], sems.at[b]))
    for copy in copies:
        copy.start()
    copies[0].wait()
    for b in range(3):
        copies[2 + b].wait()
        coeffs = dot(table[...], fields[8 * b : 8 * b + 8].reshape(512, DURATION), NT) * SCALE
        for i in range(8):
            cols = slice(i * 64, i * 64 + 64)
            scratch[field_rows(8 * b + i), :] = jnp.concatenate([coeffs[:32, cols], coeffs[32:, cols]], axis=1)
    store_rows(scratch, own_ref, send_ref)
    copies[1].wait()


def weight_kernel(w_ref, o_ref, scratch, sems):
    copies = []
    for part in range(4):
        modes = pl.ds(4 * part, 4)
        copies.append(pltpu.make_async_copy(w_ref.at[modes], scratch.at[modes], sems.at[part]))
        copies[part].start()
    for part in range(4):
        copies[part].wait()
        modes = slice(4 * part, 4 * part + 4)
        o_ref[modes] = jnp.concatenate([scratch[modes, 0], scratch[modes, 1]], axis=2).astype(BF16)


def spread_kernel(own_ref, other_ref, o_ref, scratch, *point, rows):
    table = forward_table()
    both = jnp.concatenate([own_ref[:, :3].astype(F32), other_ref[:, :3].astype(F32)], axis=2).astype(BF16)
    both = both.reshape(PAIRS, 16, 128)
    for group in range(4):
        data = jnp.concatenate([both[group * 12 + i] for i in range(12)], axis=1)
        modes = dot(table, jnp.concatenate([data, data], axis=0))
        for i in range(12):
            cols = slice(i * 128, i * 128 + 128)
            part = modes[:32, cols] + turn(modes[32:, cols], 1.0)
            scratch[pl.ds(group * 12 + i, 32, stride=rows), :] = part
    if point:
        (pairs,) = point
        total = own_ref[:8, 3].astype(F32).reshape(64, 128) + other_ref[:8, 3].astype(F32).reshape(64, 128)
        pairs[...] = split_pair(total + swap(total))
        for i in range(2):
            scratch[pl.ds(PAIRS + i, 32, stride=rows), :] = pairs[pl.ds(i, 32, stride=2), :]
        for i in range(2, 8):
            scratch[pl.ds(PAIRS + i, 32, stride=rows), :] = jnp.zeros((32, 128), F32)
    o_ref[...] = scratch[...].reshape(32, rows, 128).astype(BF16)


def mix_kernel(recv_ref, w_ref, o_ref, spec_ref):
    spec = jnp.sum(recv_ref[...].astype(F32), axis=0)
    spec_ref[...] = spec
    low = lanes(spec.shape) < 64
    other = swap(spec)
    real = jnp.where(low, spec, other)
    imag = jnp.where(low, other, spec)
    cols = []
    for kp in range(8):
        own = own_pair(kp, PAIRS)
        cols.append(
            jnp.concatenate([jnp.where(own, real, 0.0), jnp.where(own, imag, 0.0)], axis=0).astype(BF16)
        )
    prod = dot(jnp.concatenate(cols, axis=1), w_ref[...].reshape(1024, 128))
    mixed = (prod[:PAIRS] + turn(prod[PAIRS:], -1.0)).astype(BF16)
    o_ref[...] = jnp.broadcast_to(mixed[None], (32, PAIRS, 128))


def adjoint_kernel(recv_ref, w_ref, o_ref, dmix_ref):
    total = jnp.sum(recv_ref[...].astype(F32), axis=0)
    dmix = total[:PAIRS]
    dmix_ref[...] = dmix
    both = jnp.concatenate([dmix, turn(dmix, 1.0)], axis=0).astype(BF16)
    prod = dot(both, w_ref[...].reshape(1024, 128), NT)
    real = jnp.zeros((PAIRS, 128), F32)
    imag = jnp.zeros((PAIRS, 128), F32)
    for kp in range(8):
        own = own_pair(kp, PAIRS)
        cols = slice(kp * 128, kp * 128 + 128)
        real = real + jnp.where(own, prod[:PAIRS, cols], 0.0)
        imag = imag + jnp.where(own, prod[PAIRS:, cols], 0.0)
    real = real + swap(real)
    imag = imag + swap(imag)
    dspec = jnp.where(lanes(real.shape) < 64, real, imag) * SCALE
    point = total[PAIRS:]
    point = split_pair(point + swap(point))
    message = jnp.concatenate([dspec, point], axis=0).astype(BF16)
    o_ref[...] = jnp.broadcast_to(message[None], (32, ROWS, 128))


def factor_kernel(recv_ref, spec_ref, dmix_ref, fact_ref, fact):
    fact[:PAIRS] = spec_ref[...]
    fact[PAIRS : 2 * PAIRS] = dmix_ref[...]
    point = recv_ref[:, PAIRS:].astype(F32)
    for k in range(32):
        fact[2 * PAIRS + 2 * k : 2 * PAIRS + 2 * k + 2, :] = point[k, :2]
    fact_ref[...] = jnp.broadcast_to(fact[...].astype(BF16)[None], (4, 160, 128))


def gather_kernel(recv_ref, own_ref, send_ref, scratch, *, rows):
    table = inverse_table()
    scratch[...] = recv_ref[...].astype(F32).reshape(32 * rows, 128)
    for group in range(4):
        cols = []
        for i in range(12):
            modes = scratch[pl.ds(group * 12 + i, 32, stride=rows), :]
            pair = jnp.concatenate([modes, turn(modes, -1.0)], axis=0)
            cols.append(jnp.concatenate([pair, pair], axis=0).astype(BF16))
        back = dot(table, jnp.concatenate(cols, axis=1))
        for i in range(12):
            m, b = divmod(group * 12 + i, 3)
            part = back[:, i * 128 : i * 128 + 128].astype(BF16)
            own_ref[m, b] = part[:8]
            send_ref[m, b] = part[8:]


def field_kernel(
    in_ref, cot_ref, got_ref, other_ref, tab_ref, w_ref, dpre_ref, own_ref, send_ref, rows, scratch, dpre, sems
):
    load_rows(got_ref, other_ref, rows)
    mix_t = w_ref[...].astype(F32).T.astype(BF16)
    point = jnp.zeros((64, 64), F32)
    copies = []

    def fields_of(g):
        return [3 * g + i for i in range(3)]

    def pre_of(g):
        left = left_of([(mode_block(rows, f) * INV_SCALE).astype(BF16) for f in fields_of(g)], mix_t)
        out = []
        for chunk in range(4):
            ts = slice(chunk * 256, chunk * 256 + 256)
            right = jnp.concatenate([tab_ref[:, ts]] + [in_ref[f, :, ts] for f in fields_of(g)], axis=0)
            out.append(dot(left, right))
        return out

    pre = pre_of(0)
    for g in range(GROUPS):
        following = pre_of(g + 1) if g + 1 < GROUPS else None
        for chunk in range(4):
            ts = slice(chunk * 256, chunk * 256 + 256)
            for i, f in enumerate(fields_of(g)):
                slope = gelu_slope(pre[chunk][i * 64 : i * 64 + 64], cot_ref[f, :, ts].astype(F32))
                dpre[f, :, ts] = slope.astype(BF16)
        pre = following
        part = pl.ds(3 * g, 3)
        copies.append(pltpu.make_async_copy(dpre.at[part], dpre_ref.at[part], sems.at[g]))
        copies[g].start()
        left = jnp.concatenate([tab_ref[...]] + [in_ref[f] for f in fields_of(g)], axis=0)
        r = dot(left, dpre[3 * g : 3 * g + 3].reshape(192, DURATION), NT)
        for i, f in enumerate(fields_of(g)):
            cols = slice(i * 64, i * 64 + 64)
            point = point + r[64 + i * 64 : 128 + i * 64, cols]
            drows = jnp.concatenate([r[:32, cols], r[32:64, cols]], axis=1)
            scratch[field_rows(f), :] = drows * INV_SCALE
    store_rows(scratch, own_ref, send_ref)
    pair = split_pair(jnp.concatenate([point, point], axis=1))
    pair = jnp.concatenate([pair, jnp.zeros_like(pair)], axis=0).reshape(16, 8, 128).astype(BF16)
    own_ref[:, 3] = pair
    send_ref[:, 3] = pair
    for copy in copies:
        copy.wait()


def fetch_kernel(slow_ref, fast_ref, sem):
    copy = pltpu.make_async_copy(slow_ref, fast_ref, sem)
    copy.start()
    copy.wait()


def grad_kernel(dpre_ref, got_ref, other_ref, tab_ref, w_ref, o_ref, rows, grad, sems):
    load_rows(got_ref, other_ref, rows)
    mixing = w_ref[...]
    copies = []
    for g in range(GROUPS):
        fields = [3 * g + i for i in range(3)]
        left = left_of([mode_block(rows, f).astype(BF16) for f in fields], mixing)
        for chunk in range(4):
            ts = slice(chunk * 256, chunk * 256 + 256)
            right = jnp.concatenate([tab_ref[:, ts]] + [dpre_ref[f, :, ts] for f in fields], axis=0)
            total = dot(left, right).astype(BF16)
            for i, f in enumerate(fields):
                grad[f, :, ts] = total[i * 64 : i * 64 + 64]
        part = pl.ds(3 * g, 3)
        copies.append(pltpu.make_async_copy(grad.at[part], o_ref.at[part], sems.at[g]))
        copies[g].start()
    for copy in copies:
        copy.wait()


def weight_grad_kernel(fact_ref, spec_ref, point_ref):
    fact = fact_ref[...].astype(F32)
    place = lanes((1, 256)) & 127
    place = place - 24 * ((place * 171) >> 12)
    mode = (place * 43) >> 7
    empty = jnp.zeros((32, 128), F32)
    for half in range(2):
        rows = slice(half * 24, half * 24 + 24)
        s = jnp.concatenate([fact[:, rows].reshape(96, 128), empty], axis=0).T
        d = jnp.concatenate([fact[:, 48:96][:, rows].reshape(96, 128), empty], axis=0)
        left = jnp.concatenate([s[:64], s[64:]], axis=1)
        right = jnp.concatenate([d, turn(d, 1.0)], axis=0).astype(BF16)
        parts = [jnp.where(mode == m, left, 0.0).astype(BF16) for m in range(8)]
        g = dot(jnp.concatenate(parts, axis=0), right) * (1.0 / math.sqrt(BATCH * DEPTH))
        g = g.reshape(8, 64, 128)
        modes = slice(half * 8, half * 8 + 8)
        spec_ref[modes, 0] = g[:, :, :64]
        spec_ref[modes, 1] = g[:, :, 64:]
    point = fact[0, 96:] + fact[1, 96:] + fact[2, 96:] + fact[3, 96:]
    point = (point + swap(point)) * (1.0 / math.sqrt(BATCH * DEPTH * DURATION))
    point_ref[...] = point[:, :64]


FAST = pl.BlockSpec(memory_space=pltpu.VMEM)
SLOW = pl.BlockSpec(memory_space=pl.ANY)


def call(kernel, out_shape, in_specs, out_specs, scratch=(), limit=8):
    return pl.pallas_call(
        kernel,
        out_shape=out_shape,
        in_specs=in_specs,
        out_specs=out_specs,
        scratch_shapes=list(scratch),
        compiler_params=pltpu.CompilerParams(vmem_limit_bytes=limit * MIB),
    )


def shape(*dims, dtype=BF16):
    return jax.ShapeDtypeStruct(dims, dtype)


def exchange(v, axes):
    return lax.all_to_all(v, axes, 0, 0, tiled=True)


def to_other_core(v):
    return lax.ppermute(v, "core", [(0, 1), (1, 0)])


def spread(own, other, rows):
    scratch = [pltpu.VMEM((32 * rows, 128), F32)]
    if rows == ROWS:
        scratch.append(pltpu.VMEM((64, 128), F32))
    kernel = functools.partial(spread_kernel, rows=rows)
    return call(kernel, shape(32, rows, 128), [FAST] * 2, FAST, scratch)(own, other)


def gather(got, rows):
    return call(
        functools.partial(gather_kernel, rows=rows),
        (shape(16, 3, 8, 128),) * 2,
        [FAST],
        (FAST, FAST),
        [pltpu.VMEM((32 * rows, 128), F32)],
    )(got)


def local(inputs, cotangent, spec_weight, point_weight):
    tab = jnp.asarray(time_rows())
    fields = inputs.reshape(FIELDS, CHANNELS, DURATION)
    cots = cotangent.reshape(FIELDS, CHANNELS, DURATION)
    part4 = shape(16, 4, 8, 128)
    rows = pltpu.VMEM((FIELDS * 32, 128), F32)
    whole_field = pltpu.VMEM((FIELDS, CHANNELS, DURATION), BF16)
    sems = pltpu.SemaphoreType.DMA((GROUPS,))

    own, send, table, mixing, fields = call(
        coeff_kernel,
        (
            pltpu.VMEM((16, 3, 8, 128), BF16),
            pltpu.VMEM((16, 3, 8, 128), BF16),
            pltpu.VMEM((64, DURATION), BF16),
            pltpu.VMEM((CHANNELS, CHANNELS), BF16),
            pltpu.VMEM((FIELDS, CHANNELS, DURATION), BF16),
        ),
        [SLOW] * 3,
        (FAST,) * 5,
        [rows, pltpu.SemaphoreType.DMA((5,))],
        limit=56,
    )(*(pltpu.with_memory_space_constraint(v, pltpu.HBM) for v in (fields, tab, point_weight)))
    weights = call(
        weight_kernel,
        shape(16, 64, 128),
        [SLOW],
        FAST,
        [pltpu.VMEM((16, 2, CHANNELS, CHANNELS), F32), pltpu.SemaphoreType.DMA((4,))],
    )(pltpu.with_memory_space_constraint(spec_weight, pltpu.HBM))
    other, weights = lax.optimization_barrier((to_other_core(send), weights))
    got = exchange(spread(own, other, PAIRS), CHIP)
    mixed, spectrum = call(
        mix_kernel,
        (shape(32, PAIRS, 128), shape(PAIRS, 128, dtype=F32)),
        [FAST] * 2,
        (FAST,) * 2,
    )(got, weights)
    got = exchange(mixed, CHIP)
    own, send = gather(got, PAIRS)
    dpre, own, send = call(
        field_kernel,
        (pltpu.HBM((FIELDS, CHANNELS, DURATION), BF16), part4, part4),
        [FAST] * 6,
        (SLOW, FAST, FAST),
        [rows, rows, whole_field, sems],
        limit=16,
    )(pltpu.with_memory_space_constraint(fields, pltpu.VMEM), cots, own, to_other_core(send), table, mixing)
    got = exchange(spread(own, to_other_core(send), ROWS), CHIP)
    dmodes, dmixed = call(
        adjoint_kernel,
        (shape(32, ROWS, 128), shape(PAIRS, 128, dtype=F32)),
        [FAST] * 2,
        (FAST, FAST),
    )(got, weights)
    got = exchange(dmodes, CHIP)
    factors = call(
        factor_kernel,
        pltpu.HBM((4, 160, 128), BF16),
        [FAST] * 3,
        FAST,
        [pltpu.VMEM((160, 128), F32)],
    )(got, spectrum, dmixed)
    factors = exchange(factors, "dp")
    own, send = gather(got, ROWS)
    dpre = call(
        fetch_kernel,
        pltpu.VMEM((FIELDS, CHANNELS, DURATION), BF16),
        [SLOW],
        FAST,
        [pltpu.SemaphoreType.DMA],
        limit=1,
    )(pltpu.with_memory_space_constraint(dpre, pltpu.HBM))
    other, dpre = lax.optimization_barrier((to_other_core(send), dpre))
    input_grad = call(
        grad_kernel,
        pltpu.HBM((FIELDS, CHANNELS, DURATION), BF16),
        [FAST] * 5,
        SLOW,
        [rows, whole_field, sems],
        limit=12,
    )(pltpu.with_memory_space_constraint(dpre, pltpu.VMEM), own, other, table, mixing)
    spec_grad, point_grad = call(
        weight_grad_kernel,
        (shape(16, 2, 64, 64, dtype=F32), shape(64, 64, dtype=F32)),
        [FAST],
        (FAST, FAST),
    )(factors)
    return (input_grad.reshape(inputs.shape), spec_grad, point_grad)


def solution(mesh):
    fine = Mesh(mesh.devices.reshape(4, 2, 4, 4, 2), ("dp",) + FIELD)
    fields = P("dp", FIELD, None, None)
    weights = P(FIELD, None, None, None)
    return jax.shard_map(
        local,
        mesh=fine,
        in_specs=(fields, fields, weights, P()),
        out_specs=(fields, weights, P()),
        check_vma=False,
    )
```

```python
import functools
import math

import jax
import jax.numpy as jnp
import ml_dtypes
import numpy as np
from jax import lax
from jax.experimental import pallas as pl
from jax.experimental.pallas import tpu as pltpu
from jax.sharding import Mesh
from jax.sharding import PartitionSpec as P

DEPTH = 512
DURATION = 1024
CHANNELS = 64
DMODES = 32
TMODES = 32
BATCH = 12

CHIP = ("z", "y", "x")
FIELD = CHIP + ("core",)
BF16 = jnp.bfloat16
F32 = jnp.float32
SCALE = 1.0 / math.sqrt(DEPTH * DURATION)
INV_SCALE = 1.0 / math.sqrt(DMODES * TMODES)
NN = (((1,), (0,)), ((), ()))
NT = (((1,), (1,)), ((), ()))
MIB = 1024 * 1024
FIELDS = 24
GROUPS = 8
PARTS = ((0, 8), (8, 8), (16, 8))
PAIRS = 48
ROWS = 56


def time_rows():
    m = np.arange(TMODES)
    phase = ((m[:, None] * np.arange(DURATION)[None, :]) % DURATION) * (2.0 * np.pi / DURATION)
    return np.concatenate([np.cos(phase), -np.sin(phase)], axis=0).astype(ml_dtypes.bfloat16)


def depth_table(k, x, sine):
    freq = jnp.where(k < DMODES // 2, k, k - DMODES)
    phase = ((freq * x - jnp.where(sine, DEPTH // 4, 0) + DEPTH // 2) & (DEPTH - 1)) - DEPTH // 2
    return jnp.cos(phase.astype(F32) * (2.0 * math.pi / DEPTH))


def high_or_low(v, low):
    high = v.astype(BF16).astype(F32)
    return jnp.where(low, v - high, high).astype(BF16)


def position(i):
    return 8 * (lax.axis_index(FIELD) ^ (i >> 3)) + (i & 7)


def forward_table():
    row = lax.broadcasted_iota(jnp.int32, (64, 32), 0)
    col = lax.broadcasted_iota(jnp.int32, (64, 32), 1)
    return high_or_low(depth_table(row & 31, position(col & 15), row >= 32), col >= 16)


def inverse_table():
    row = lax.broadcasted_iota(jnp.int32, (16, 128), 0)
    col = lax.broadcasted_iota(jnp.int32, (16, 128), 1)
    return high_or_low(depth_table(col & 31, position(row), (col & 32) != 0), col >= 64)


def lanes(shape):
    return lax.broadcasted_iota(jnp.int32, shape, len(shape) - 1)


def swap(v):
    return pltpu.roll(v, 64, 1)


def turn(v, first):
    return swap(v) * jnp.where(lanes(v.shape) < 64, first, -first).astype(F32)


def split_pair(v):
    high = v.astype(BF16).astype(F32)
    return jnp.where(lanes(v.shape) < 64, high, v - high)


def dot(a, b, dims=NN):
    return lax.dot_general(a, b, dims, preferred_element_type=F32)


def store_rows(scratch, own_ref, send_ref):
    core = lax.axis_index("core")
    for b in range(3):
        for c, ref in ((core, own_ref), (1 - core, send_ref)):
            rows = scratch[pl.ds(pl.multiple_of(b * 256 + c * 128, 128), 128), :]
            ref[:, b] = rows.reshape(16, 8, 128).astype(BF16)


def load_rows(own_ref, other_ref, scratch):
    core = lax.axis_index("core")
    for b in range(3):
        for c, ref in ((core, own_ref), (1 - core, other_ref)):
            rows = ref[:, b].astype(F32).reshape(128, 128)
            scratch[pl.ds(pl.multiple_of(b * 256 + c * 128, 128), 128), :] = rows


def field_rows(field):
    b, xl = divmod(field, 8)
    return pl.ds(b * 256 + xl, 32, stride=8)


def mode_block(scratch, field):
    g = scratch[field_rows(field), :]
    return jnp.concatenate([g[:, :64], g[:, 64:]], axis=0).T


def left_of(blocks, mixing):
    zero = jnp.zeros((64, 64), BF16)
    rows = []
    for i, g in enumerate(blocks):
        rows.append(jnp.concatenate([g] + [mixing if k == i else zero for k in range(len(blocks))], axis=1))
    return jnp.concatenate(rows, axis=0)


def gelu_slope_twice(pre, cot):
    root = math.sqrt(2.0 / math.pi)
    p = (root * 0.044715) * (pre * pre) + root
    th = jnp.tanh(pre * p)
    q = 3.0 * p - 2.0 * root
    return ((1.0 + th) * (1.0 + (pre * q) * (1.0 - th))) * cot


def own_pair(kp, rows):
    row = lax.broadcasted_iota(jnp.int32, (rows, 128), 0)
    first = row - lanes((rows, 128)) // 64 * 3 - 6 * kp
    return (first >= 0) & (first < 3)


def coeff_kernel(
    in_ref, tab_ref, mix_ref, own_ref, send_ref, table, mixing, fields, forward, inverse, scratch, sems
):
    copies = [
        pltpu.make_async_copy(tab_ref, table, sems.at[len(PARTS)]),
        pltpu.make_async_copy(mix_ref, mixing, sems.at[len(PARTS) + 1]),
    ]
    for p, (first, n) in enumerate(PARTS):
        part = pl.ds(first, n)
        copies.append(pltpu.make_async_copy(in_ref.at[part], fields.at[part], sems.at[p]))
    for copy in copies:
        copy.start()
    forward[...] = forward_table()
    inverse[...] = inverse_table()
    copies[0].wait()
    for p, (first, n) in enumerate(PARTS):
        copies[2 + p].wait()
        coeffs = dot(table[...], fields[first : first + n].reshape(n * 64, DURATION), NT) * SCALE
        for i in range(n):
            cols = slice(i * 64, i * 64 + 64)
            scratch[field_rows(first + i), :] = jnp.concatenate([coeffs[:32, cols], coeffs[32:, cols]], axis=1)
    store_rows(scratch, own_ref, send_ref)
    copies[1].wait()


def weight_kernel(w_ref, o_ref, scratch, sems):
    copies = []
    for part in range(4):
        modes = pl.ds(4 * part, 4)
        copies.append(pltpu.make_async_copy(w_ref.at[modes], scratch.at[modes], sems.at[part]))
        copies[part].start()
    for part in range(4):
        copies[part].wait()
        modes = slice(4 * part, 4 * part + 4)
        o_ref[modes] = jnp.concatenate([scratch[modes, 0], scratch[modes, 1]], axis=2).astype(BF16)


def spread_kernel(own_ref, other_ref, tab_ref, o_ref, scratch, *point, rows):
    table = tab_ref[...]
    both = jnp.concatenate([own_ref[:, :3].astype(F32), other_ref[:, :3].astype(F32)], axis=2).astype(BF16)
    both = both.reshape(PAIRS, 16, 128)
    for group in range(4):
        data = jnp.concatenate([both[group * 12 + i] for i in range(12)], axis=1)
        modes = dot(table, jnp.concatenate([data, data], axis=0))
        for i in range(12):
            cols = slice(i * 128, i * 128 + 128)
            part = modes[:32, cols] + turn(modes[32:, cols], 1.0)
            scratch[pl.ds(group * 12 + i, 32, stride=rows), :] = part
    if point:
        (pairs,) = point
        total = own_ref[:8, 3].astype(F32).reshape(64, 128) + other_ref[:8, 3].astype(F32).reshape(64, 128)
        pairs[...] = split_pair(total + swap(total))
        for i in range(2):
            scratch[pl.ds(PAIRS + i, 32, stride=rows), :] = pairs[pl.ds(i, 32, stride=2), :]
        for i in range(2, 8):
            scratch[pl.ds(PAIRS + i, 32, stride=rows), :] = jnp.zeros((32, 128), F32)
    o_ref[...] = scratch[...].reshape(32, rows, 128).astype(BF16)


def mix_kernel(recv_ref, w_ref, o_ref, spec_ref):
    spec = jnp.sum(recv_ref[...].astype(F32), axis=0)
    spec_ref[...] = spec
    low = lanes(spec.shape) < 64
    other = swap(spec)
    real = jnp.where(low, spec, other)
    imag = jnp.where(low, other, spec)
    cols = []
    for kp in range(8):
        own = own_pair(kp, PAIRS)
        cols.append(
            jnp.concatenate([jnp.where(own, real, 0.0), jnp.where(own, imag, 0.0)], axis=0).astype(BF16)
        )
    prod = dot(jnp.concatenate(cols, axis=1), w_ref[...].reshape(1024, 128))
    mixed = (prod[:PAIRS] + turn(prod[PAIRS:], -1.0)).astype(BF16)
    o_ref[...] = jnp.broadcast_to(mixed[None], (32, PAIRS, 128))


def adjoint_kernel(recv_ref, w_ref, o_ref, dmix_ref):
    total = jnp.sum(recv_ref[...].astype(F32), axis=0)
    dmix = total[:PAIRS]
    dmix_ref[...] = dmix
    both = jnp.concatenate([dmix, turn(dmix, 1.0)], axis=0).astype(BF16)
    prod = dot(both, w_ref[...].reshape(1024, 128), NT)
    real = jnp.zeros((PAIRS, 128), F32)
    imag = jnp.zeros((PAIRS, 128), F32)
    for kp in range(8):
        own = own_pair(kp, PAIRS)
        cols = slice(kp * 128, kp * 128 + 128)
        real = real + jnp.where(own, prod[:PAIRS, cols], 0.0)
        imag = imag + jnp.where(own, prod[PAIRS:, cols], 0.0)
    real = real + swap(real)
    imag = imag + swap(imag)
    dspec = jnp.where(lanes(real.shape) < 64, real, imag) * SCALE
    point = total[PAIRS:]
    point = split_pair(point + swap(point))
    message = jnp.concatenate([dspec, point], axis=0).astype(BF16)
    o_ref[...] = jnp.broadcast_to(message[None], (32, ROWS, 128))


def factor_kernel(recv_ref, spec_ref, dmix_ref, fact_ref, fact):
    fact[:PAIRS] = spec_ref[...]
    fact[PAIRS : 2 * PAIRS] = dmix_ref[...]
    point = recv_ref[:, PAIRS:].astype(F32)
    for k in range(32):
        fact[2 * PAIRS + 2 * k : 2 * PAIRS + 2 * k + 2, :] = point[k, :2]
    fact_ref[...] = jnp.broadcast_to(fact[...].astype(BF16)[None], (4, 160, 128))


def gather_kernel(recv_ref, tab_ref, own_ref, send_ref, scratch, *, rows):
    table = tab_ref[...]
    scratch[...] = recv_ref[...].astype(F32).reshape(32 * rows, 128)
    for group in range(4):
        cols = []
        for i in range(12):
            modes = scratch[pl.ds(group * 12 + i, 32, stride=rows), :]
            pair = jnp.concatenate([modes, turn(modes, -1.0)], axis=0)
            cols.append(jnp.concatenate([pair, pair], axis=0).astype(BF16))
        back = dot(table, jnp.concatenate(cols, axis=1))
        for i in range(12):
            m, b = divmod(group * 12 + i, 3)
            part = back[:, i * 128 : i * 128 + 128].astype(BF16)
            own_ref[m, b] = part[:8]
            send_ref[m, b] = part[8:]


def field_kernel(
    in_ref, cot_ref, got_ref, other_ref, tab_ref, w_ref, dpre_ref, own_ref, send_ref, rows, scratch, dpre, sems
):
    load_rows(got_ref, other_ref, rows)
    mix_t = w_ref[...].astype(F32).T.astype(BF16)
    point = jnp.zeros((64, 64), F32)
    copies = []

    def fields_of(g):
        return [3 * g + i for i in range(3)]

    def pre_of(g):
        left = left_of([(mode_block(rows, f) * INV_SCALE).astype(BF16) for f in fields_of(g)], mix_t)
        out = []
        for chunk in range(4):
            ts = slice(chunk * 256, chunk * 256 + 256)
            right = jnp.concatenate([tab_ref[:, ts]] + [in_ref[f, :, ts] for f in fields_of(g)], axis=0)
            out.append(dot(left, right))
        return out

    pre = pre_of(0)
    for g in range(GROUPS):
        following = pre_of(g + 1) if g + 1 < GROUPS else None
        for chunk in range(4):
            ts = slice(chunk * 256, chunk * 256 + 256)
            for i, f in enumerate(fields_of(g)):
                slope = gelu_slope_twice(pre[chunk][i * 64 : i * 64 + 64], cot_ref[f, :, ts].astype(F32))
                dpre[f, :, ts] = slope.astype(BF16)
        pre = following
        part = pl.ds(3 * g, 3)
        copies.append(pltpu.make_async_copy(dpre.at[part], dpre_ref.at[part], sems.at[g]))
        copies[g].start()
        left = jnp.concatenate([tab_ref[...]] + [in_ref[f] for f in fields_of(g)], axis=0)
        r = dot(left, dpre[3 * g : 3 * g + 3].reshape(192, DURATION), NT)
        for i, f in enumerate(fields_of(g)):
            cols = slice(i * 64, i * 64 + 64)
            point = point + r[64 + i * 64 : 128 + i * 64, cols]
            drows = jnp.concatenate([r[:32, cols], r[32:64, cols]], axis=1)
            scratch[field_rows(f), :] = drows * (0.5 * INV_SCALE)
    store_rows(scratch, own_ref, send_ref)
    point = 0.5 * point
    pair = split_pair(jnp.concatenate([point, point], axis=1))
    pair = jnp.concatenate([pair, jnp.zeros_like(pair)], axis=0).reshape(16, 8, 128).astype(BF16)
    own_ref[:, 3] = pair
    send_ref[:, 3] = pair
    for copy in copies:
        copy.wait()


def fetch_kernel(slow_ref, fast_ref, sem):
    copy = pltpu.make_async_copy(slow_ref, fast_ref, sem)
    copy.start()
    copy.wait()


def grad_kernel(dpre_ref, got_ref, other_ref, tab_ref, w_ref, o_ref, rows, grad, sems):
    load_rows(got_ref, other_ref, rows)
    mixing = (w_ref[...].astype(F32) * 0.5).astype(BF16)
    copies = []
    for g in range(GROUPS):
        fields = [3 * g + i for i in range(3)]
        left = left_of([mode_block(rows, f).astype(BF16) for f in fields], mixing)
        for chunk in range(4):
            ts = slice(chunk * 256, chunk * 256 + 256)
            right = jnp.concatenate([tab_ref[:, ts]] + [dpre_ref[f, :, ts] for f in fields], axis=0)
            total = dot(left, right).astype(BF16)
            for i, f in enumerate(fields):
                grad[f, :, ts] = total[i * 64 : i * 64 + 64]
        part = pl.ds(3 * g, 3)
        copies.append(pltpu.make_async_copy(grad.at[part], o_ref.at[part], sems.at[g]))
        copies[g].start()
    for copy in copies:
        copy.wait()


def weight_grad_kernel(fact_ref, spec_ref, point_ref):
    fact = fact_ref[...].astype(F32)
    place = lanes((1, 256)) & 127
    place = place - 24 * ((place * 171) >> 12)
    mode = (place * 43) >> 7
    empty = jnp.zeros((32, 128), F32)
    for half in range(2):
        rows = slice(half * 24, half * 24 + 24)
        s = jnp.concatenate([fact[:, rows].reshape(96, 128), empty], axis=0).T
        d = jnp.concatenate([fact[:, 48:96][:, rows].reshape(96, 128), empty], axis=0)
        left = jnp.concatenate([s[:64], s[64:]], axis=1)
        right = jnp.concatenate([d, turn(d, 1.0)], axis=0).astype(BF16)
        parts = [jnp.where(mode == m, left, 0.0).astype(BF16) for m in range(8)]
        g = dot(jnp.concatenate(parts, axis=0), right) * (1.0 / math.sqrt(BATCH * DEPTH))
        g = g.reshape(8, 64, 128)
        modes = slice(half * 8, half * 8 + 8)
        spec_ref[modes, 0] = g[:, :, :64]
        spec_ref[modes, 1] = g[:, :, 64:]
    point = fact[0, 96:] + fact[1, 96:] + fact[2, 96:] + fact[3, 96:]
    point = (point + swap(point)) * (1.0 / math.sqrt(BATCH * DEPTH * DURATION))
    point_ref[...] = point[:, :64]


FAST = pl.BlockSpec(memory_space=pltpu.VMEM)
SLOW = pl.BlockSpec(memory_space=pl.ANY)


def call(kernel, out_shape, in_specs, out_specs, scratch=(), limit=8):
    return pl.pallas_call(
        kernel,
        out_shape=out_shape,
        in_specs=in_specs,
        out_specs=out_specs,
        scratch_shapes=list(scratch),
        compiler_params=pltpu.CompilerParams(vmem_limit_bytes=limit * MIB),
    )


def shape(*dims, dtype=BF16):
    return jax.ShapeDtypeStruct(dims, dtype)


def exchange(v, axes):
    return lax.all_to_all(v, axes, 0, 0, tiled=True)


def to_other_core(v):
    return lax.ppermute(v, "core", [(0, 1), (1, 0)])


def spread(own, other, table, rows):
    scratch = [pltpu.VMEM((32 * rows, 128), F32)]
    if rows == ROWS:
        scratch.append(pltpu.VMEM((64, 128), F32))
    kernel = functools.partial(spread_kernel, rows=rows)
    return call(kernel, shape(32, rows, 128), [FAST] * 3, FAST, scratch)(own, other, table)


def gather(got, table, rows):
    return call(
        functools.partial(gather_kernel, rows=rows),
        (shape(16, 3, 8, 128),) * 2,
        [FAST] * 2,
        (FAST, FAST),
        [pltpu.VMEM((32 * rows, 128), F32)],
    )(got, table)


def local(inputs, cotangent, spec_weight, point_weight):
    tab = jnp.asarray(time_rows())
    fields = inputs.reshape(FIELDS, CHANNELS, DURATION)
    cots = cotangent.reshape(FIELDS, CHANNELS, DURATION)
    part4 = shape(16, 4, 8, 128)
    rows = pltpu.VMEM((FIELDS * 32, 128), F32)
    whole_field = pltpu.VMEM((FIELDS, CHANNELS, DURATION), BF16)
    sems = pltpu.SemaphoreType.DMA((GROUPS,))

    own, send, table, mixing, fields, forward, inverse = call(
        coeff_kernel,
        (
            pltpu.VMEM((16, 3, 8, 128), BF16),
            pltpu.VMEM((16, 3, 8, 128), BF16),
            pltpu.VMEM((64, DURATION), BF16),
            pltpu.VMEM((CHANNELS, CHANNELS), BF16),
            pltpu.VMEM((FIELDS, CHANNELS, DURATION), BF16),
            pltpu.VMEM((64, 32), BF16),
            pltpu.VMEM((16, 128), BF16),
        ),
        [SLOW] * 3,
        (FAST,) * 7,
        [rows, pltpu.SemaphoreType.DMA((len(PARTS) + 2,))],
        limit=56,
    )(*(pltpu.with_memory_space_constraint(v, pltpu.HBM) for v in (fields, tab, point_weight)))
    weights = call(
        weight_kernel,
        shape(16, 64, 128),
        [SLOW],
        FAST,
        [pltpu.VMEM((16, 2, CHANNELS, CHANNELS), F32), pltpu.SemaphoreType.DMA((4,))],
    )(pltpu.with_memory_space_constraint(spec_weight, pltpu.HBM))
    other, weights = lax.optimization_barrier((to_other_core(send), weights))
    got = exchange(spread(own, other, forward, PAIRS), CHIP)
    mixed, spectrum = call(
        mix_kernel,
        (shape(32, PAIRS, 128), shape(PAIRS, 128, dtype=F32)),
        [FAST] * 2,
        (FAST,) * 2,
    )(got, weights)
    got = exchange(mixed, CHIP)
    own, send = gather(got, inverse, PAIRS)
    dpre, own, send = call(
        field_kernel,
        (pltpu.HBM((FIELDS, CHANNELS, DURATION), BF16), part4, part4),
        [FAST] * 6,
        (SLOW, FAST, FAST),
        [rows, rows, whole_field, sems],
        limit=16,
    )(pltpu.with_memory_space_constraint(fields, pltpu.VMEM), cots, own, to_other_core(send), table, mixing)
    got = exchange(spread(own, to_other_core(send), forward, ROWS), CHIP)
    dmodes, dmixed = call(
        adjoint_kernel,
        (shape(32, ROWS, 128), shape(PAIRS, 128, dtype=F32)),
        [FAST] * 2,
        (FAST, FAST),
    )(got, weights)
    got = exchange(dmodes, CHIP)
    factors = call(
        factor_kernel,
        pltpu.HBM((4, 160, 128), BF16),
        [FAST] * 3,
        FAST,
        [pltpu.VMEM((160, 128), F32)],
    )(got, spectrum, dmixed)
    factors = exchange(factors, "dp")
    own, send = gather(got, inverse, ROWS)
    dpre = call(
        fetch_kernel,
        pltpu.VMEM((FIELDS, CHANNELS, DURATION), BF16),
        [SLOW],
        FAST,
        [pltpu.SemaphoreType.DMA],
        limit=1,
    )(pltpu.with_memory_space_constraint(dpre, pltpu.HBM))
    other, dpre = lax.optimization_barrier((to_other_core(send), dpre))
    input_grad = call(
        grad_kernel,
        pltpu.HBM((FIELDS, CHANNELS, DURATION), BF16),
        [FAST] * 5,
        SLOW,
        [rows, whole_field, sems],
        limit=12,
    )(pltpu.with_memory_space_constraint(dpre, pltpu.VMEM), own, other, table, mixing)
    spec_grad, point_grad = call(
        weight_grad_kernel,
        (shape(16, 2, 64, 64, dtype=F32), shape(64, 64, dtype=F32)),
        [FAST],
        (FAST, FAST),
    )(factors)
    return (input_grad.reshape(inputs.shape), spec_grad, point_grad)


def solution(mesh):
    fine = Mesh(mesh.devices.reshape(4, 2, 4, 4, 2), ("dp",) + FIELD)
    fields = P("dp", FIELD, None, None)
    weights = P(FIELD, None, None, None)
    return jax.shard_map(
        local,
        mesh=fine,
        in_specs=(fields, fields, weights, P()),
        out_specs=(fields, weights, P()),
        check_vma=False,
    )
```

```python
import functools
import math

import jax
import jax.numpy as jnp
import ml_dtypes
import numpy as np
from jax import lax
from jax.experimental import pallas as pl
from jax.experimental.pallas import tpu as pltpu
from jax.sharding import Mesh
from jax.sharding import PartitionSpec as P

DEPTH = 512
DURATION = 1024
CHANNELS = 64
DMODES = 32
TMODES = 32
BATCH = 12

CHIP = ("z", "y", "x")
FIELD = CHIP + ("core",)
BF16 = jnp.bfloat16
F32 = jnp.float32
SCALE = 1.0 / math.sqrt(DEPTH * DURATION)
INV_SCALE = 1.0 / math.sqrt(DMODES * TMODES)
NN = (((1,), (0,)), ((), ()))
NT = (((1,), (1,)), ((), ()))
MIB = 1024 * 1024
FIELDS = 24
GROUPS = 8
PAIRS = 48
ROWS = 56


def time_rows():
    m = np.arange(TMODES)
    phase = ((m[:, None] * np.arange(DURATION)[None, :]) % DURATION) * (2.0 * np.pi / DURATION)
    return np.concatenate([np.cos(phase), -np.sin(phase)], axis=0).astype(ml_dtypes.bfloat16)


def depth_table(k, x, sine):
    freq = jnp.where(k < DMODES // 2, k, k - DMODES)
    phase = ((freq * x - jnp.where(sine, DEPTH // 4, 0) + DEPTH // 2) & (DEPTH - 1)) - DEPTH // 2
    return jnp.cos(phase.astype(F32) * (2.0 * math.pi / DEPTH))


def high_or_low(v, low):
    high = v.astype(BF16).astype(F32)
    return jnp.where(low, v - high, high).astype(BF16)


def position(i):
    return 8 * (lax.axis_index(FIELD) ^ (i >> 3)) + (i & 7)


def forward_table():
    row = lax.broadcasted_iota(jnp.int32, (64, 32), 0)
    col = lax.broadcasted_iota(jnp.int32, (64, 32), 1)
    return high_or_low(depth_table(row & 31, position(col & 15), row >= 32), col >= 16)


def inverse_table():
    row = lax.broadcasted_iota(jnp.int32, (16, 128), 0)
    col = lax.broadcasted_iota(jnp.int32, (16, 128), 1)
    return high_or_low(depth_table(col & 31, position(row), (col & 32) != 0), col >= 64)


def lanes(shape):
    return lax.broadcasted_iota(jnp.int32, shape, len(shape) - 1)


def swap(v):
    return pltpu.roll(v, 64, 1)


def turn(v, first):
    return swap(v) * jnp.where(lanes(v.shape) < 64, first, -first).astype(F32)


def split_pair(v):
    high = v.astype(BF16).astype(F32)
    return jnp.where(lanes(v.shape) < 64, high, v - high)


def dot(a, b, dims=NN):
    return lax.dot_general(a, b, dims, preferred_element_type=F32)


def store_rows(scratch, b, own_ref, send_ref):
    core = lax.axis_index("core")
    for c, ref in ((core, own_ref), (1 - core, send_ref)):
        rows = scratch[pl.ds(pl.multiple_of(b * 256 + c * 128, 128), 128), :]
        ref[:, b] = rows.reshape(16, 8, 128).astype(BF16)


def load_rows(own_ref, other_ref, scratch):
    core = lax.axis_index("core")
    for b in range(3):
        for c, ref in ((core, own_ref), (1 - core, other_ref)):
            rows = ref[:, b].astype(F32).reshape(128, 128)
            scratch[pl.ds(pl.multiple_of(b * 256 + c * 128, 128), 128), :] = rows


def field_rows(field):
    b, xl = divmod(field, 8)
    return pl.ds(b * 256 + xl, 32, stride=8)


def mode_block(scratch, field):
    g = scratch[field_rows(field), :]
    return jnp.concatenate([g[:, :64], g[:, 64:]], axis=0).T


def left_of(blocks, mixing):
    zero = jnp.zeros((64, 64), BF16)
    rows = []
    for i, g in enumerate(blocks):
        rows.append(jnp.concatenate([g] + [mixing if k == i else zero for k in range(len(blocks))], axis=1))
    return jnp.concatenate(rows, axis=0)


def gelu_slope_twice(pre, cot):
    root = math.sqrt(2.0 / math.pi)
    p = (root * 0.044715) * (pre * pre) + root
    th = jnp.tanh(pre * p)
    q = 3.0 * p - 2.0 * root
    return ((1.0 + th) * (1.0 + (pre * q) * (1.0 - th))) * cot


def own_pair(kp, rows):
    row = lax.broadcasted_iota(jnp.int32, (rows, 128), 0)
    first = row - lanes((rows, 128)) // 64 * 3 - 6 * kp
    return (first >= 0) & (first < 3)


def coeff_kernel(
    in_ref, tab_ref, mix_ref, own_ref, send_ref, table, mixing, fields, forward, inverse, scratch, sems
):
    copies = [
        pltpu.make_async_copy(tab_ref, table, sems.at[3]),
        pltpu.make_async_copy(mix_ref, mixing, sems.at[4]),
    ]
    for b in range(3):
        part = pl.ds(8 * b, 8)
        copies.append(pltpu.make_async_copy(in_ref.at[part], fields.at[part], sems.at[b]))
    for copy in copies:
        copy.start()
    forward[...] = forward_table()
    inverse[...] = inverse_table()
    copies[0].wait()
    for b in range(3):
        copies[2 + b].wait()
        coeffs = dot(table[...], fields[8 * b : 8 * b + 8].reshape(512, DURATION), NT) * SCALE
        for i in range(8):
            cols = slice(i * 64, i * 64 + 64)
            scratch[field_rows(8 * b + i), :] = jnp.concatenate([coeffs[:32, cols], coeffs[32:, cols]], axis=1)
        store_rows(scratch, b, own_ref, send_ref)
    copies[1].wait()


def weight_kernel(w_ref, o_ref, scratch, sems):
    copies = []
    for part in range(4):
        modes = pl.ds(4 * part, 4)
        copies.append(pltpu.make_async_copy(w_ref.at[modes], scratch.at[modes], sems.at[part]))
        copies[part].start()
    for part in range(4):
        copies[part].wait()
        modes = slice(4 * part, 4 * part + 4)
        o_ref[modes] = jnp.concatenate([scratch[modes, 0], scratch[modes, 1]], axis=2).astype(BF16)


def spread_kernel(own_ref, other_ref, tab_ref, o_ref, scratch, *point, rows):
    table = tab_ref[...]
    both = jnp.concatenate([own_ref[:, :3].astype(F32), other_ref[:, :3].astype(F32)], axis=2).astype(BF16)
    both = both.reshape(PAIRS, 16, 128)
    for group in range(4):
        data = jnp.concatenate([both[group * 12 + i] for i in range(12)], axis=1)
        modes = dot(table, jnp.concatenate([data, data], axis=0))
        for i in range(12):
            cols = slice(i * 128, i * 128 + 128)
            part = modes[:32, cols] + turn(modes[32:, cols], 1.0)
            scratch[pl.ds(group * 12 + i, 32, stride=rows), :] = part
    if point:
        (pairs,) = point
        total = own_ref[:8, 3].astype(F32).reshape(64, 128) + other_ref[:8, 3].astype(F32).reshape(64, 128)
        pairs[:64] = split_pair(total + swap(total))
        for i in range(2):
            scratch[pl.ds(PAIRS + i, 32, stride=rows), :] = pairs[pl.ds(i, 32, stride=2), :]
        for i in range(2, 8):
            scratch[pl.ds(PAIRS + i, 32, stride=rows), :] = jnp.zeros((32, 128), F32)
    o_ref[...] = scratch[: 32 * rows].reshape(32, rows, 128).astype(BF16)


def mix_kernel(recv_ref, w_ref, o_ref, spec_ref):
    spec = jnp.sum(recv_ref[...].astype(F32), axis=0)
    spec_ref[...] = spec
    low = lanes(spec.shape) < 64
    other = swap(spec)
    real = jnp.where(low, spec, other)
    imag = jnp.where(low, other, spec)
    cols = []
    for kp in range(8):
        own = own_pair(kp, PAIRS)
        cols.append(
            jnp.concatenate([jnp.where(own, real, 0.0), jnp.where(own, imag, 0.0)], axis=0).astype(BF16)
        )
    prod = dot(jnp.concatenate(cols, axis=1), w_ref[...].reshape(1024, 128))
    mixed = (prod[:PAIRS] + turn(prod[PAIRS:], -1.0)).astype(BF16)
    o_ref[...] = jnp.broadcast_to(mixed[None], (32, PAIRS, 128))


def adjoint_kernel(recv_ref, w_ref, o_ref, dmix_ref):
    total = jnp.sum(recv_ref[...].astype(F32), axis=0)
    dmix = total[:PAIRS]
    dmix_ref[...] = dmix
    both = jnp.concatenate([dmix, turn(dmix, 1.0)], axis=0).astype(BF16)
    prod = dot(both, w_ref[...].reshape(1024, 128), NT)
    real = jnp.zeros((PAIRS, 128), F32)
    imag = jnp.zeros((PAIRS, 128), F32)
    for kp in range(8):
        own = own_pair(kp, PAIRS)
        cols = slice(kp * 128, kp * 128 + 128)
        real = real + jnp.where(own, prod[:PAIRS, cols], 0.0)
        imag = imag + jnp.where(own, prod[PAIRS:, cols], 0.0)
    real = real + swap(real)
    imag = imag + swap(imag)
    dspec = jnp.where(lanes(real.shape) < 64, real, imag) * SCALE
    point = total[PAIRS:]
    point = split_pair(point + swap(point))
    message = jnp.concatenate([dspec, point], axis=0).astype(BF16)
    o_ref[...] = jnp.broadcast_to(message[None], (32, ROWS, 128))


def factor_kernel(recv_ref, spec_ref, dmix_ref, fact_ref, fact):
    fact[:PAIRS] = spec_ref[...]
    fact[PAIRS : 2 * PAIRS] = dmix_ref[...]
    point = recv_ref[:, PAIRS:].astype(F32)
    for k in range(32):
        fact[2 * PAIRS + 2 * k : 2 * PAIRS + 2 * k + 2, :] = point[k, :2]
    fact_ref[...] = jnp.broadcast_to(fact[...].astype(BF16)[None], (4, 160, 128))


def gather_kernel(recv_ref, tab_ref, own_ref, send_ref, scratch, *, rows):
    table = tab_ref[...]
    scratch[: 32 * rows] = recv_ref[...].astype(F32).reshape(32 * rows, 128)
    for group in range(4):
        cols = []
        for i in range(12):
            modes = scratch[pl.ds(group * 12 + i, 32, stride=rows), :]
            pair = jnp.concatenate([modes, turn(modes, -1.0)], axis=0)
            cols.append(jnp.concatenate([pair, pair], axis=0).astype(BF16))
        back = dot(table, jnp.concatenate(cols, axis=1))
        for i in range(12):
            m, b = divmod(group * 12 + i, 3)
            part = back[:, i * 128 : i * 128 + 128].astype(BF16)
            own_ref[m, b] = part[:8]
            send_ref[m, b] = part[8:]


def field_kernel(
    in_ref, cot_ref, got_ref, other_ref, tab_ref, w_ref, dpre_ref, own_ref, send_ref, rows, scratch, dpre, sems
):
    load_rows(got_ref, other_ref, rows)
    mix_t = w_ref[...].astype(F32).T.astype(BF16)
    point = jnp.zeros((64, 64), F32)
    copies = []

    def fields_of(g):
        return [3 * g + i for i in range(3)]

    def pre_of(g):
        left = left_of([(mode_block(rows, f) * INV_SCALE).astype(BF16) for f in fields_of(g)], mix_t)
        out = []
        for chunk in range(4):
            ts = slice(chunk * 256, chunk * 256 + 256)
            right = jnp.concatenate([tab_ref[:, ts]] + [in_ref[f, :, ts] for f in fields_of(g)], axis=0)
            out.append(dot(left, right))
        return out

    pre = pre_of(0)
    for g in range(GROUPS):
        following = pre_of(g + 1) if g + 1 < GROUPS else None
        for chunk in range(4):
            ts = slice(chunk * 256, chunk * 256 + 256)
            for i, f in enumerate(fields_of(g)):
                slope = gelu_slope_twice(pre[chunk][i * 64 : i * 64 + 64], cot_ref[f, :, ts].astype(F32))
                dpre[f, :, ts] = slope.astype(BF16)
        pre = following
        part = pl.ds(3 * g, 3)
        copies.append(pltpu.make_async_copy(dpre.at[part], dpre_ref.at[part], sems.at[g]))
        copies[g].start()
        left = jnp.concatenate([tab_ref[...]] + [in_ref[f] for f in fields_of(g)], axis=0)
        r = dot(left, dpre[3 * g : 3 * g + 3].reshape(192, DURATION), NT)
        for i, f in enumerate(fields_of(g)):
            cols = slice(i * 64, i * 64 + 64)
            point = point + r[64 + i * 64 : 128 + i * 64, cols]
            drows = jnp.concatenate([r[:32, cols], r[32:64, cols]], axis=1)
            scratch[field_rows(f), :] = drows * (0.5 * INV_SCALE)
            if f % 8 == 7:
                store_rows(scratch, f // 8, own_ref, send_ref)
    point = 0.5 * point
    pair = split_pair(jnp.concatenate([point, point], axis=1))
    pair = jnp.concatenate([pair, jnp.zeros_like(pair)], axis=0).reshape(16, 8, 128).astype(BF16)
    own_ref[:, 3] = pair
    send_ref[:, 3] = pair
    for copy in copies:
        copy.wait()


def fetch_kernel(slow_ref, fast_ref, sem):
    copy = pltpu.make_async_copy(slow_ref, fast_ref, sem)
    copy.start()
    copy.wait()


def grad_kernel(dpre_ref, got_ref, other_ref, tab_ref, w_ref, o_ref, rows, grad, sems):
    load_rows(got_ref, other_ref, rows)
    mixing = (w_ref[...].astype(F32) * 0.5).astype(BF16)
    copies = []
    for g in range(GROUPS):
        fields = [3 * g + i for i in range(3)]
        left = left_of([mode_block(rows, f).astype(BF16) for f in fields], mixing)
        for chunk in range(4):
            ts = slice(chunk * 256, chunk * 256 + 256)
            right = jnp.concatenate([tab_ref[:, ts]] + [dpre_ref[f, :, ts] for f in fields], axis=0)
            total = dot(left, right).astype(BF16)
            for i, f in enumerate(fields):
                grad[f, :, ts] = total[i * 64 : i * 64 + 64]
        part = pl.ds(3 * g, 3)
        copies.append(pltpu.make_async_copy(grad.at[part], o_ref.at[part], sems.at[g]))
        copies[g].start()
    for copy in copies:
        copy.wait()


def weight_grad_kernel(fact_ref, spec_ref, point_ref):
    fact = fact_ref[...].astype(F32)
    place = lanes((1, 256)) & 127
    place = place - 24 * ((place * 171) >> 12)
    mode = (place * 43) >> 7
    empty = jnp.zeros((32, 128), F32)
    for half in range(2):
        rows = slice(half * 24, half * 24 + 24)
        s = jnp.concatenate([fact[:, rows].reshape(96, 128), empty], axis=0).T
        d = jnp.concatenate([fact[:, 48:96][:, rows].reshape(96, 128), empty], axis=0)
        left = jnp.concatenate([s[:64], s[64:]], axis=1) * (1.0 / math.sqrt(BATCH * DEPTH))
        right = jnp.concatenate([d, turn(d, 1.0)], axis=0).astype(BF16)
        parts = [jnp.where(mode == m, left, 0.0).astype(BF16) for m in range(8)]
        g = dot(jnp.concatenate(parts, axis=0), right)
        g = g.reshape(8, 64, 128)
        modes = slice(half * 8, half * 8 + 8)
        spec_ref[modes, 0] = g[:, :, :64]
        spec_ref[modes, 1] = g[:, :, 64:]
    point = fact[0, 96:] + fact[1, 96:] + fact[2, 96:] + fact[3, 96:]
    point = (point + swap(point)) * (1.0 / math.sqrt(BATCH * DEPTH * DURATION))
    point_ref[...] = point[:, :64]


FAST = pl.BlockSpec(memory_space=pltpu.VMEM)
SLOW = pl.BlockSpec(memory_space=pl.ANY)


def call(kernel, out_shape, in_specs, out_specs, scratch=(), limit=8):
    return pl.pallas_call(
        kernel,
        out_shape=out_shape,
        in_specs=in_specs,
        out_specs=out_specs,
        scratch_shapes=list(scratch),
        compiler_params=pltpu.CompilerParams(vmem_limit_bytes=limit * MIB),
    )


def shape(*dims, dtype=BF16):
    return jax.ShapeDtypeStruct(dims, dtype)


def exchange(v, axes):
    return lax.all_to_all(v, axes, 0, 0, tiled=True)


def to_other_core(v):
    return lax.ppermute(v, "core", [(0, 1), (1, 0)])


def spread(own, other, table, rows):
    scratch = [pltpu.VMEM((33 * rows, 128), F32)]
    if rows == ROWS:
        scratch.append(pltpu.VMEM((72, 128), F32))
    kernel = functools.partial(spread_kernel, rows=rows)
    return call(kernel, shape(32, rows, 128), [FAST] * 3, FAST, scratch)(own, other, table)


def gather(got, table, rows):
    return call(
        functools.partial(gather_kernel, rows=rows),
        (shape(16, 3, 8, 128),) * 2,
        [FAST] * 2,
        (FAST, FAST),
        [pltpu.VMEM((33 * rows, 128), F32)],
    )(got, table)


def local(inputs, cotangent, spec_weight, point_weight):
    tab = jnp.asarray(time_rows())
    fields = inputs.reshape(FIELDS, CHANNELS, DURATION)
    cots = cotangent.reshape(FIELDS, CHANNELS, DURATION)
    part4 = shape(16, 4, 8, 128)
    rows = pltpu.VMEM((FIELDS * 32 + 8, 128), F32)
    whole_field = pltpu.VMEM((FIELDS, CHANNELS, DURATION), BF16)
    sems = pltpu.SemaphoreType.DMA((GROUPS,))

    own, send, table, mixing, fields, forward, inverse = call(
        coeff_kernel,
        (
            pltpu.VMEM((16, 3, 8, 128), BF16),
            pltpu.VMEM((16, 3, 8, 128), BF16),
            pltpu.VMEM((64, DURATION), BF16),
            pltpu.VMEM((CHANNELS, CHANNELS), BF16),
            pltpu.VMEM((FIELDS, CHANNELS, DURATION), BF16),
            pltpu.VMEM((64, 32), BF16),
            pltpu.VMEM((16, 128), BF16),
        ),
        [SLOW] * 3,
        (FAST,) * 7,
        [rows, pltpu.SemaphoreType.DMA((5,))],
        limit=56,
    )(*(pltpu.with_memory_space_constraint(v, pltpu.HBM) for v in (fields, tab, point_weight)))
    weights = call(
        weight_kernel,
        shape(16, 64, 128),
        [SLOW],
        FAST,
        [pltpu.VMEM((16, 2, CHANNELS, CHANNELS), F32), pltpu.SemaphoreType.DMA((4,))],
    )(pltpu.with_memory_space_constraint(spec_weight, pltpu.HBM))
    other, weights = lax.optimization_barrier((to_other_core(send), weights))
    got = exchange(spread(own, other, forward, PAIRS), CHIP)
    mixed, spectrum = call(
        mix_kernel,
        (shape(32, PAIRS, 128), shape(PAIRS, 128, dtype=F32)),
        [FAST] * 2,
        (FAST,) * 2,
    )(got, weights)
    got = exchange(mixed, CHIP)
    own, send = gather(got, inverse, PAIRS)
    dpre, own, send = call(
        field_kernel,
        (pltpu.HBM((FIELDS, CHANNELS, DURATION), BF16), part4, part4),
        [FAST] * 6,
        (SLOW, FAST, FAST),
        [rows, rows, whole_field, sems],
        limit=16,
    )(pltpu.with_memory_space_constraint(fields, pltpu.VMEM), cots, own, to_other_core(send), table, mixing)
    got = exchange(spread(own, to_other_core(send), forward, ROWS), CHIP)
    dmodes, dmixed = call(
        adjoint_kernel,
        (shape(32, ROWS, 128), shape(PAIRS, 128, dtype=F32)),
        [FAST] * 2,
        (FAST, FAST),
    )(got, weights)
    got = exchange(dmodes, CHIP)
    factors = call(
        factor_kernel,
        pltpu.HBM((4, 160, 128), BF16),
        [FAST] * 3,
        FAST,
        [pltpu.VMEM((160, 128), F32)],
    )(got, spectrum, dmixed)
    factors = exchange(factors, "dp")
    own, send = gather(got, inverse, ROWS)
    dpre = call(
        fetch_kernel,
        pltpu.VMEM((FIELDS, CHANNELS, DURATION), BF16),
        [SLOW],
        FAST,
        [pltpu.SemaphoreType.DMA],
        limit=1,
    )(pltpu.with_memory_space_constraint(dpre, pltpu.HBM))
    other, dpre = lax.optimization_barrier((to_other_core(send), dpre))
    input_grad = call(
        grad_kernel,
        pltpu.HBM((FIELDS, CHANNELS, DURATION), BF16),
        [FAST] * 5,
        SLOW,
        [rows, whole_field, sems],
        limit=12,
    )(pltpu.with_memory_space_constraint(dpre, pltpu.VMEM), own, other, table, mixing)
    spec_grad, point_grad = call(
        weight_grad_kernel,
        (shape(16, 2, 64, 64, dtype=F32), shape(64, 64, dtype=F32)),
        [FAST],
        (FAST, FAST),
    )(factors)
    return (input_grad.reshape(inputs.shape), spec_grad, point_grad)


def solution(mesh):
    fine = Mesh(mesh.devices.reshape(4, 2, 4, 4, 2), ("dp",) + FIELD)
    fields = P("dp", FIELD, None, None)
    weights = P(FIELD, None, None, None)
    return jax.shard_map(
        local,
        mesh=fine,
        in_specs=(fields, fields, weights, P()),
        out_specs=(fields, weights, P()),
        check_vma=False,
    )
```

```python
import functools
import math

import jax
import jax.numpy as jnp
import ml_dtypes
import numpy as np
from jax import lax
from jax.experimental import pallas as pl
from jax.experimental.pallas import tpu as pltpu
from jax.sharding import Mesh
from jax.sharding import PartitionSpec as P

DEPTH = 512
DURATION = 1024
CHANNELS = 64
DMODES = 32
TMODES = 32
BATCH = 12

CHIP = ("z", "y", "x")
FIELD = CHIP + ("core",)
BF16 = jnp.bfloat16
F32 = jnp.float32
SCALE = 1.0 / math.sqrt(DEPTH * DURATION)
INV_SCALE = 1.0 / math.sqrt(DMODES * TMODES)
NN = (((1,), (0,)), ((), ()))
NT = (((1,), (1,)), ((), ()))
MIB = 1024 * 1024
FIELDS = 24
GROUPS = 8
PAIRS = 48
ROWS = 56


def time_rows():
    m = np.arange(TMODES)
    phase = ((m[:, None] * np.arange(DURATION)[None, :]) % DURATION) * (2.0 * np.pi / DURATION)
    return np.concatenate([np.cos(phase), -np.sin(phase)], axis=0).astype(ml_dtypes.bfloat16)


def depth_table(k, x, sine):
    freq = jnp.where(k < DMODES // 2, k, k - DMODES)
    phase = ((freq * x - jnp.where(sine, DEPTH // 4, 0) + DEPTH // 2) & (DEPTH - 1)) - DEPTH // 2
    return jnp.cos(phase.astype(F32) * (2.0 * math.pi / DEPTH))


def high_or_low(v, low):
    high = v.astype(BF16).astype(F32)
    return jnp.where(low, v - high, high).astype(BF16)


def position(i):
    return 8 * (lax.axis_index(FIELD) ^ (i >> 3)) + (i & 7)


def forward_table():
    row = lax.broadcasted_iota(jnp.int32, (64, 32), 0)
    col = lax.broadcasted_iota(jnp.int32, (64, 32), 1)
    return high_or_low(depth_table(row & 31, position(col & 15), row >= 32), col >= 16)


def inverse_table():
    row = lax.broadcasted_iota(jnp.int32, (16, 128), 0)
    col = lax.broadcasted_iota(jnp.int32, (16, 128), 1)
    return high_or_low(depth_table(col & 31, position(row), (col & 32) != 0), col >= 64)


def lanes(shape):
    return lax.broadcasted_iota(jnp.int32, shape, len(shape) - 1)


def swap(v):
    return pltpu.roll(v, 64, 1)


def turn(v, first):
    return swap(v) * jnp.where(lanes(v.shape) < 64, first, -first).astype(F32)


def split_pair(v):
    high = v.astype(BF16).astype(F32)
    return jnp.where(lanes(v.shape) < 64, high, v - high)


def dot(a, b, dims=NN):
    return lax.dot_general(a, b, dims, preferred_element_type=F32)


def store_rows(scratch, b, own_ref, send_ref):
    core = lax.axis_index("core")
    for c, ref in ((core, own_ref), (1 - core, send_ref)):
        rows = scratch[pl.ds(pl.multiple_of(b * 256 + c * 128, 128), 128), :]
        ref[:, b] = rows.reshape(16, 8, 128).astype(BF16)


def load_rows(own_ref, other_ref, scratch):
    core = lax.axis_index("core")
    for b in range(3):
        for c, ref in ((core, own_ref), (1 - core, other_ref)):
            rows = ref[:, b].astype(F32).reshape(128, 128)
            scratch[pl.ds(pl.multiple_of(b * 256 + c * 128, 128), 128), :] = rows


def field_rows(field):
    b, xl = divmod(field, 8)
    return pl.ds(b * 256 + xl, 32, stride=8)


def mode_block(scratch, field):
    g = scratch[field_rows(field), :]
    return jnp.concatenate([g[:, :64], g[:, 64:]], axis=0).T


def left_of(blocks, mixing):
    zero = jnp.zeros((64, 64), BF16)
    rows = []
    for i, g in enumerate(blocks):
        rows.append(jnp.concatenate([g] + [mixing if k == i else zero for k in range(len(blocks))], axis=1))
    return jnp.concatenate(rows, axis=0)


def gelu_slope_twice(pre, cot):
    root = math.sqrt(2.0 / math.pi)
    p = (root * 0.044715) * (pre * pre) + root
    th = jnp.tanh(pre * p)
    q = 3.0 * p - 2.0 * root
    return ((1.0 + th) * (1.0 + (pre * q) * (1.0 - th))) * cot


def own_pair(kp, rows):
    row = lax.broadcasted_iota(jnp.int32, (rows, 128), 0)
    first = row - lanes((rows, 128)) // 64 * 3 - 6 * kp
    return (first >= 0) & (first < 3)


def coeff_kernel(
    in_ref, tab_ref, mix_ref, own_ref, send_ref, table, mixing, fields, forward, inverse, scratch, sems
):
    copies = [
        pltpu.make_async_copy(tab_ref, table, sems.at[3]),
        pltpu.make_async_copy(mix_ref, mixing, sems.at[4]),
    ]
    for b in range(3):
        part = pl.ds(8 * b, 8)
        copies.append(pltpu.make_async_copy(in_ref.at[part], fields.at[part], sems.at[b]))
    for copy in copies:
        copy.start()
    forward[...] = forward_table()
    inverse[...] = inverse_table()
    copies[0].wait()
    for b in range(3):
        copies[2 + b].wait()
        coeffs = dot(table[...], fields[8 * b : 8 * b + 8].reshape(512, DURATION), NT) * SCALE
        for i in range(8):
            cols = slice(i * 64, i * 64 + 64)
            scratch[field_rows(8 * b + i), :] = jnp.concatenate([coeffs[:32, cols], coeffs[32:, cols]], axis=1)
        store_rows(scratch, b, own_ref, send_ref)
    copies[1].wait()


def weight_kernel(w_ref, o_ref, scratch, sems):
    copies = []
    for part in range(4):
        modes = pl.ds(4 * part, 4)
        copies.append(pltpu.make_async_copy(w_ref.at[modes], scratch.at[modes], sems.at[part]))
        copies[part].start()
    for part in range(4):
        copies[part].wait()
        modes = slice(4 * part, 4 * part + 4)
        o_ref[modes] = jnp.concatenate([scratch[modes, 0], scratch[modes, 1]], axis=2).astype(BF16)


def spread_kernel(own_ref, other_ref, tab_ref, o_ref, scratch, *point, rows):
    table = tab_ref[...]
    both = jnp.concatenate([own_ref[:, :3].astype(F32), other_ref[:, :3].astype(F32)], axis=2).astype(BF16)
    both = both.reshape(PAIRS, 16, 128)
    for group in range(4):
        data = jnp.concatenate([both[group * 12 + i] for i in range(12)], axis=1)
        modes = dot(table, jnp.concatenate([data, data], axis=0))
        for i in range(12):
            cols = slice(i * 128, i * 128 + 128)
            part = modes[:32, cols] + turn(modes[32:, cols], 1.0)
            scratch[pl.ds(group * 12 + i, 32, stride=rows), :] = part
    if point:
        (pairs,) = point
        total = own_ref[:8, 3].astype(F32).reshape(64, 128) + other_ref[:8, 3].astype(F32).reshape(64, 128)
        pairs[:64] = split_pair(total + swap(total))
        for i in range(2):
            scratch[pl.ds(PAIRS + i, 32, stride=rows), :] = pairs[pl.ds(i, 32, stride=2), :]
        for i in range(2, 8):
            scratch[pl.ds(PAIRS + i, 32, stride=rows), :] = jnp.zeros((32, 128), F32)
    o_ref[...] = scratch[: 32 * rows].reshape(32, rows, 128).astype(BF16)


def mix_kernel(recv_ref, w_ref, o_ref, spec_ref):
    spec = jnp.sum(recv_ref[...].astype(F32), axis=0)
    spec_ref[...] = spec
    low = lanes(spec.shape) < 64
    other = swap(spec)
    real = jnp.where(low, spec, other)
    imag = jnp.where(low, other, spec)
    cols = []
    for kp in range(8):
        own = own_pair(kp, PAIRS)
        cols.append(
            jnp.concatenate([jnp.where(own, real, 0.0), jnp.where(own, imag, 0.0)], axis=0).astype(BF16)
        )
    prod = dot(jnp.concatenate(cols, axis=1), w_ref[...].reshape(1024, 128))
    mixed = (prod[:PAIRS] + turn(prod[PAIRS:], -1.0)).astype(BF16)
    o_ref[...] = jnp.broadcast_to(mixed[None], (32, PAIRS, 128))


def adjoint_kernel(recv_ref, w_ref, o_ref, dmix_ref):
    total = jnp.sum(recv_ref[...].astype(F32), axis=0)
    dmix = total[:PAIRS]
    dmix_ref[...] = dmix
    both = jnp.concatenate([dmix, turn(dmix, 1.0)], axis=0).astype(BF16)
    prod = dot(both, w_ref[...].reshape(1024, 128), NT)
    real = jnp.zeros((PAIRS, 128), F32)
    imag = jnp.zeros((PAIRS, 128), F32)
    for kp in range(8):
        own = own_pair(kp, PAIRS)
        cols = slice(kp * 128, kp * 128 + 128)
        real = real + jnp.where(own, prod[:PAIRS, cols], 0.0)
        imag = imag + jnp.where(own, prod[PAIRS:, cols], 0.0)
    real = real + swap(real)
    imag = imag + swap(imag)
    dspec = jnp.where(lanes(real.shape) < 64, real, imag) * SCALE
    point = total[PAIRS:]
    point = split_pair(point + swap(point))
    message = jnp.concatenate([dspec, point], axis=0).astype(BF16)
    o_ref[...] = jnp.broadcast_to(message[None], (32, ROWS, 128))


def factor_kernel(recv_ref, spec_ref, dmix_ref, fact_ref, fact):
    fact[:PAIRS] = spec_ref[...]
    fact[PAIRS : 2 * PAIRS] = dmix_ref[...]
    point = recv_ref[:, PAIRS:].astype(F32)
    for k in range(32):
        fact[2 * PAIRS + 2 * k : 2 * PAIRS + 2 * k + 2, :] = point[k, :2]
    fact_ref[...] = jnp.broadcast_to(fact[...].astype(BF16)[None], (4, 160, 128))


def gather_kernel(recv_ref, tab_ref, own_ref, send_ref, scratch, *, rows):
    table = tab_ref[...]
    scratch[: 32 * rows] = recv_ref[...].astype(F32).reshape(32 * rows, 128)
    for group in range(4):
        cols = []
        for i in range(12):
            modes = scratch[pl.ds(group * 12 + i, 32, stride=rows), :]
            pair = jnp.concatenate([modes, turn(modes, -1.0)], axis=0)
            cols.append(jnp.concatenate([pair, pair], axis=0).astype(BF16))
        back = dot(table, jnp.concatenate(cols, axis=1))
        for i in range(12):
            m, b = divmod(group * 12 + i, 3)
            part = back[:, i * 128 : i * 128 + 128].astype(BF16)
            own_ref[m, b] = part[:8]
            send_ref[m, b] = part[8:]


def field_kernel(
    in_ref, cot_ref, got_ref, other_ref, tab_ref, w_ref, dpre_ref, own_ref, send_ref, rows, scratch, dpre, sems
):
    load_rows(got_ref, other_ref, rows)
    mix_t = w_ref[...].astype(F32).T.astype(BF16)
    point = jnp.zeros((64, 64), F32)
    copies = []

    def fields_of(g):
        return [3 * g + i for i in range(3)]

    def pre_of(g):
        left = left_of([(mode_block(rows, f) * INV_SCALE).astype(BF16) for f in fields_of(g)], mix_t)
        out = []
        for chunk in range(4):
            ts = slice(chunk * 256, chunk * 256 + 256)
            right = jnp.concatenate([tab_ref[:, ts]] + [in_ref[f, :, ts] for f in fields_of(g)], axis=0)
            out.append(dot(left, right))
        return out

    pre = pre_of(0)
    for g in range(GROUPS):
        following = pre_of(g + 1) if g + 1 < GROUPS else None
        for chunk in range(4):
            ts = slice(chunk * 256, chunk * 256 + 256)
            for i, f in enumerate(fields_of(g)):
                slope = gelu_slope_twice(pre[chunk][i * 64 : i * 64 + 64], cot_ref[f, :, ts].astype(F32))
                dpre[f, :, ts] = slope.astype(BF16)
        pre = following
        part = pl.ds(3 * g, 3)
        copies.append(pltpu.make_async_copy(dpre.at[part], dpre_ref.at[part], sems.at[g]))
        copies[g].start()
        left = jnp.concatenate([tab_ref[...]] + [in_ref[f] for f in fields_of(g)], axis=0)
        r = dot(left, dpre[3 * g : 3 * g + 3].reshape(192, DURATION), NT)
        for i, f in enumerate(fields_of(g)):
            cols = slice(i * 64, i * 64 + 64)
            point = point + r[64 + i * 64 : 128 + i * 64, cols]
            drows = jnp.concatenate([r[:32, cols], r[32:64, cols]], axis=1)
            scratch[field_rows(f), :] = drows * (0.5 * INV_SCALE)
            if f % 8 == 7:
                store_rows(scratch, f // 8, own_ref, send_ref)
    point = 0.5 * point
    pair = split_pair(jnp.concatenate([point, point], axis=1))
    pair = jnp.concatenate([pair, jnp.zeros_like(pair)], axis=0).reshape(16, 8, 128).astype(BF16)
    own_ref[:, 3] = pair
    send_ref[:, 3] = pair
    for copy in copies:
        copy.wait()


def fetch_kernel(slow_ref, fast_ref, sem):
    copy = pltpu.make_async_copy(slow_ref, fast_ref, sem)
    copy.start()
    copy.wait()


def grad_kernel(dpre_ref, got_ref, other_ref, tab_ref, w_ref, o_ref, rows, grad, sems):
    load_rows(got_ref, other_ref, rows)
    mixing = (w_ref[...].astype(F32) * 0.5).astype(BF16)
    copies = []
    for g in range(GROUPS):
        fields = [3 * g + i for i in range(3)]
        left = left_of([mode_block(rows, f).astype(BF16) for f in fields], mixing)
        for chunk in range(4):
            ts = slice(chunk * 256, chunk * 256 + 256)
            right = jnp.concatenate([tab_ref[:, ts]] + [dpre_ref[f, :, ts] for f in fields], axis=0)
            total = dot(left, right).astype(BF16)
            for i, f in enumerate(fields):
                grad[f, :, ts] = total[i * 64 : i * 64 + 64]
        part = pl.ds(3 * g, 3)
        copies.append(pltpu.make_async_copy(grad.at[part], o_ref.at[part], sems.at[g]))
        copies[g].start()
    for copy in copies:
        copy.wait()


def weight_grad_kernel(fact_ref, spec_ref, point_ref):
    fact = fact_ref[...].astype(F32)
    place = lanes((1, 256)) & 127
    place = place - 24 * ((place * 171) >> 12)
    mode = (place * 43) >> 7
    empty = jnp.zeros((32, 128), F32)
    for half in range(2):
        rows = slice(half * 24, half * 24 + 24)
        s = jnp.concatenate([fact[:, rows].reshape(96, 128), empty], axis=0).T
        d = jnp.concatenate([fact[:, 48:96][:, rows].reshape(96, 128), empty], axis=0)
        left = jnp.concatenate([s[:64], s[64:]], axis=1)
        right = jnp.concatenate([d, turn(d, 1.0)], axis=0).astype(BF16)
        parts = [jnp.where(mode == m, left, 0.0).astype(BF16) for m in range(8)]
        g = dot(jnp.concatenate(parts, axis=0), right) * (1.0 / math.sqrt(BATCH * DEPTH))
        g = g.reshape(8, 64, 128)
        modes = slice(half * 8, half * 8 + 8)
        spec_ref[modes, 0] = g[:, :, :64]
        spec_ref[modes, 1] = g[:, :, 64:]
    point = fact[0, 96:] + fact[1, 96:] + fact[2, 96:] + fact[3, 96:]
    point = (point + swap(point)) * (1.0 / math.sqrt(BATCH * DEPTH * DURATION))
    point_ref[...] = point[:, :64]


FAST = pl.BlockSpec(memory_space=pltpu.VMEM)
SLOW = pl.BlockSpec(memory_space=pl.ANY)


def call(kernel, out_shape, in_specs, out_specs, scratch=(), limit=8):
    return pl.pallas_call(
        kernel,
        out_shape=out_shape,
        in_specs=in_specs,
        out_specs=out_specs,
        scratch_shapes=list(scratch),
        compiler_params=pltpu.CompilerParams(vmem_limit_bytes=limit * MIB),
    )


def shape(*dims, dtype=BF16):
    return jax.ShapeDtypeStruct(dims, dtype)


def exchange(v, axes):
    return lax.all_to_all(v, axes, 0, 0, tiled=True)


def to_other_core(v):
    return lax.ppermute(v, "core", [(0, 1), (1, 0)])


def spread(own, other, table, rows):
    scratch = [pltpu.VMEM((33 * rows, 128), F32)]
    if rows == ROWS:
        scratch.append(pltpu.VMEM((72, 128), F32))
    kernel = functools.partial(spread_kernel, rows=rows)
    return call(kernel, shape(32, rows, 128), [FAST] * 3, FAST, scratch)(own, other, table)


def gather(got, table, rows):
    return call(
        functools.partial(gather_kernel, rows=rows),
        (shape(16, 3, 8, 128),) * 2,
        [FAST] * 2,
        (FAST, FAST),
        [pltpu.VMEM((33 * rows, 128), F32)],
    )(got, table)


def local(inputs, cotangent, spec_weight, point_weight):
    tab = jnp.asarray(time_rows())
    fields = inputs.reshape(FIELDS, CHANNELS, DURATION)
    cots = cotangent.reshape(FIELDS, CHANNELS, DURATION)
    part4 = shape(16, 4, 8, 128)
    rows = pltpu.VMEM((FIELDS * 32 + 8, 128), F32)
    whole_field = pltpu.VMEM((FIELDS, CHANNELS, DURATION), BF16)
    sems = pltpu.SemaphoreType.DMA((GROUPS,))

    own, send, table, mixing, fields, forward, inverse = call(
        coeff_kernel,
        (
            pltpu.VMEM((16, 3, 8, 128), BF16),
            pltpu.VMEM((16, 3, 8, 128), BF16),
            pltpu.VMEM((64, DURATION), BF16),
            pltpu.VMEM((CHANNELS, CHANNELS), BF16),
            pltpu.VMEM((FIELDS, CHANNELS, DURATION), BF16),
            pltpu.VMEM((64, 32), BF16),
            pltpu.VMEM((16, 128), BF16),
        ),
        [SLOW] * 3,
        (FAST,) * 7,
        [rows, pltpu.SemaphoreType.DMA((5,))],
        limit=56,
    )(*(pltpu.with_memory_space_constraint(v, pltpu.HBM) for v in (fields, tab, point_weight)))
    weights = call(
        weight_kernel,
        shape(16, 64, 128),
        [SLOW],
        FAST,
        [pltpu.VMEM((16, 2, CHANNELS, CHANNELS), F32), pltpu.SemaphoreType.DMA((4,))],
    )(pltpu.with_memory_space_constraint(spec_weight, pltpu.HBM))
    other, weights = lax.optimization_barrier((to_other_core(send), weights))
    got = exchange(spread(own, other, forward, PAIRS), CHIP)
    mixed, spectrum = call(
        mix_kernel,
        (shape(32, PAIRS, 128), shape(PAIRS, 128, dtype=F32)),
        [FAST] * 2,
        (FAST,) * 2,
    )(got, weights)
    got = exchange(mixed, CHIP)
    own, send = gather(got, inverse, PAIRS)
    dpre, own, send = call(
        field_kernel,
        (pltpu.HBM((FIELDS, CHANNELS, DURATION), BF16), part4, part4),
        [FAST] * 6,
        (SLOW, FAST, FAST),
        [rows, rows, whole_field, sems],
        limit=16,
    )(pltpu.with_memory_space_constraint(fields, pltpu.VMEM), cots, own, to_other_core(send), table, mixing)
    got = exchange(spread(own, to_other_core(send), forward, ROWS), CHIP)
    dmodes, dmixed = call(
        adjoint_kernel,
        (shape(32, ROWS, 128), shape(PAIRS, 128, dtype=F32)),
        [FAST] * 2,
        (FAST, FAST),
    )(got, weights)
    got = exchange(dmodes, CHIP)
    factors = call(
        factor_kernel,
        pltpu.HBM((4, 160, 128), BF16),
        [FAST] * 3,
        FAST,
        [pltpu.VMEM((160, 128), F32)],
    )(got, spectrum, dmixed)
    factors = exchange(factors, "dp")
    own, send = gather(got, inverse, ROWS)
    dpre = call(
        fetch_kernel,
        pltpu.VMEM((FIELDS, CHANNELS, DURATION), BF16),
        [SLOW],
        FAST,
        [pltpu.SemaphoreType.DMA],
        limit=1,
    )(pltpu.with_memory_space_constraint(dpre, pltpu.HBM))
    other, dpre = lax.optimization_barrier((to_other_core(send), dpre))
    input_grad = call(
        grad_kernel,
        pltpu.HBM((FIELDS, CHANNELS, DURATION), BF16),
        [FAST] * 5,
        SLOW,
        [rows, whole_field, sems],
        limit=12,
    )(pltpu.with_memory_space_constraint(dpre, pltpu.VMEM), own, other, table, mixing)
    spec_grad, point_grad = call(
        weight_grad_kernel,
        (shape(16, 2, 64, 64, dtype=F32), shape(64, 64, dtype=F32)),
        [FAST],
        (FAST, FAST),
    )(factors)
    return (input_grad.reshape(inputs.shape), spec_grad, point_grad)


def solution(mesh):
    fine = Mesh(mesh.devices.reshape(4, 2, 4, 4, 2), ("dp",) + FIELD)
    fields = P("dp", FIELD, None, None)
    weights = P(FIELD, None, None, None)
    return jax.shard_map(
        local,
        mesh=fine,
        in_specs=(fields, fields, weights, P()),
        out_specs=(fields, weights, P()),
        check_vma=False,
    )
```

```python
import functools
import math

import jax
import jax.numpy as jnp
import ml_dtypes
import numpy as np
from jax import lax
from jax.experimental import pallas as pl
from jax.experimental.pallas import tpu as pltpu
from jax.sharding import Mesh
from jax.sharding import PartitionSpec as P

DEPTH = 512
DURATION = 1024
CHANNELS = 64
DMODES = 32
TMODES = 32
BATCH = 12

CHIP = ("z", "y", "x")
FIELD = CHIP + ("core",)
BF16 = jnp.bfloat16
F32 = jnp.float32
SCALE = 1.0 / math.sqrt(DEPTH * DURATION)
INV_SCALE = 1.0 / math.sqrt(DMODES * TMODES)
NN = (((1,), (0,)), ((), ()))
NT = (((1,), (1,)), ((), ()))
MIB = 1024 * 1024
FIELDS = 24
GROUPS = 8
PAIRS = 48
ROWS = 56


def time_rows():
    m = np.arange(TMODES)
    phase = ((m[:, None] * np.arange(DURATION)[None, :]) % DURATION) * (2.0 * np.pi / DURATION)
    return np.concatenate([np.cos(phase), -np.sin(phase)], axis=0).astype(ml_dtypes.bfloat16)


def depth_table(k, x, sine):
    freq = jnp.where(k < DMODES // 2, k, k - DMODES)
    phase = ((freq * x - jnp.where(sine, DEPTH // 4, 0) + DEPTH // 2) & (DEPTH - 1)) - DEPTH // 2
    return jnp.cos(phase.astype(F32) * (2.0 * math.pi / DEPTH))


def high_or_low(v, low):
    high = v.astype(BF16).astype(F32)
    return jnp.where(low, v - high, high).astype(BF16)


def position(i):
    return 8 * (lax.axis_index(FIELD) ^ (i >> 3)) + (i & 7)


def forward_table():
    row = lax.broadcasted_iota(jnp.int32, (64, 32), 0)
    col = lax.broadcasted_iota(jnp.int32, (64, 32), 1)
    return high_or_low(depth_table(row & 31, position(col & 15), row >= 32), col >= 16)


def inverse_table():
    row = lax.broadcasted_iota(jnp.int32, (16, 128), 0)
    col = lax.broadcasted_iota(jnp.int32, (16, 128), 1)
    return high_or_low(depth_table(col & 31, position(row), (col & 32) != 0), col >= 64)


def lanes(shape):
    return lax.broadcasted_iota(jnp.int32, shape, len(shape) - 1)


def swap(v):
    return pltpu.roll(v, 64, 1)


def turn(v, first):
    return swap(v) * jnp.where(lanes(v.shape) < 64, first, -first).astype(F32)


def split_pair(v):
    high = v.astype(BF16).astype(F32)
    return jnp.where(lanes(v.shape) < 64, high, v - high)


def dot(a, b, dims=NN):
    return lax.dot_general(a, b, dims, preferred_element_type=F32)


def store_rows(scratch, b, own_ref, send_ref):
    core = lax.axis_index("core")
    for c, ref in ((core, own_ref), (1 - core, send_ref)):
        rows = scratch[pl.ds(pl.multiple_of(b * 256 + c * 128, 128), 128), :]
        ref[:, b] = rows.reshape(16, 8, 128).astype(BF16)


def load_rows(own_ref, other_ref, scratch):
    core = lax.axis_index("core")
    for b in range(3):
        for c, ref in ((core, own_ref), (1 - core, other_ref)):
            rows = ref[:, b].astype(F32).reshape(128, 128)
            scratch[pl.ds(pl.multiple_of(b * 256 + c * 128, 128), 128), :] = rows


def field_rows(field):
    b, xl = divmod(field, 8)
    return pl.ds(b * 256 + xl, 32, stride=8)


def mode_block(scratch, field):
    g = scratch[field_rows(field), :]
    return jnp.concatenate([g[:, :64], g[:, 64:]], axis=0).T


def left_of(blocks, mixing):
    zero = jnp.zeros((64, 64), BF16)
    rows = []
    for i, g in enumerate(blocks):
        rows.append(jnp.concatenate([g] + [mixing if k == i else zero for k in range(len(blocks))], axis=1))
    return jnp.concatenate(rows, axis=0)


def gelu_slope_twice(pre, cot):
    root = math.sqrt(2.0 / math.pi)
    p = (root * 0.044715) * (pre * pre) + root
    th = jnp.tanh(pre * p)
    q = 3.0 * p - 2.0 * root
    return ((1.0 + th) * (1.0 + (pre * q) * (1.0 - th))) * cot


def own_pair(kp, rows):
    row = lax.broadcasted_iota(jnp.int32, (rows, 128), 0)
    first = row - lanes((rows, 128)) // 64 * 3 - 6 * kp
    return (first >= 0) & (first < 3)


def coeff_kernel(
    in_ref, tab_ref, mix_ref, own_ref, send_ref, table, mixing, fields, forward, inverse, scratch, sems
):
    copies = [
        pltpu.make_async_copy(tab_ref, table, sems.at[3]),
        pltpu.make_async_copy(mix_ref, mixing, sems.at[4]),
    ]
    for b in range(3):
        part = pl.ds(8 * b, 8)
        copies.append(pltpu.make_async_copy(in_ref.at[part], fields.at[part], sems.at[b]))
    for copy in copies:
        copy.start()
    forward[...] = forward_table()
    inverse[...] = inverse_table()
    copies[0].wait()
    for b in range(3):
        copies[2 + b].wait()
        coeffs = dot(table[...], fields[8 * b : 8 * b + 8].reshape(512, DURATION), NT) * SCALE
        for i in range(8):
            cols = slice(i * 64, i * 64 + 64)
            scratch[field_rows(8 * b + i), :] = jnp.concatenate([coeffs[:32, cols], coeffs[32:, cols]], axis=1)
        store_rows(scratch, b, own_ref, send_ref)
    copies[1].wait()


def weight_kernel(w_ref, o_ref, scratch, sems):
    copies = []
    for part in range(4):
        modes = pl.ds(4 * part, 4)
        copies.append(pltpu.make_async_copy(w_ref.at[modes], scratch.at[modes], sems.at[part]))
        copies[part].start()
    for part in range(4):
        copies[part].wait()
        modes = slice(4 * part, 4 * part + 4)
        o_ref[modes] = jnp.concatenate([scratch[modes, 0], scratch[modes, 1]], axis=2).astype(BF16)


def spread_kernel(own_ref, other_ref, tab_ref, o_ref, scratch, *point, rows):
    table = tab_ref[...]
    both = jnp.concatenate([own_ref[:, :3].astype(F32), other_ref[:, :3].astype(F32)], axis=2).astype(BF16)
    both = both.reshape(PAIRS, 16, 128)
    for group in range(4):
        data = jnp.concatenate([both[group * 12 + i] for i in range(12)], axis=1)
        modes = dot(table, jnp.concatenate([data, data], axis=0))
        for i in range(12):
            cols = slice(i * 128, i * 128 + 128)
            part = modes[:32, cols] + turn(modes[32:, cols], 1.0)
            scratch[pl.ds(group * 12 + i, 32, stride=rows), :] = part
    if point:
        (pairs,) = point
        total = own_ref[:8, 3].astype(F32).reshape(64, 128) + other_ref[:8, 3].astype(F32).reshape(64, 128)
        pairs[:64] = split_pair(total + swap(total))
        for i in range(2):
            scratch[pl.ds(PAIRS + i, 32, stride=rows), :] = pairs[pl.ds(i, 32, stride=2), :]
        for i in range(2, 8):
            scratch[pl.ds(PAIRS + i, 32, stride=rows), :] = jnp.zeros((32, 128), F32)
    o_ref[...] = scratch[: 32 * rows].reshape(32, rows, 128).astype(BF16)


def mix_kernel(recv_ref, w_ref, o_ref, spec_ref):
    spec = jnp.sum(recv_ref[...].astype(F32), axis=0)
    spec_ref[...] = spec
    low = lanes(spec.shape) < 64
    other = swap(spec)
    real = jnp.where(low, spec, other)
    imag = jnp.where(low, other, spec)
    cols = []
    for kp in range(8):
        own = own_pair(kp, PAIRS)
        cols.append(
            jnp.concatenate([jnp.where(own, real, 0.0), jnp.where(own, imag, 0.0)], axis=0).astype(BF16)
        )
    prod = dot(jnp.concatenate(cols, axis=1), w_ref[...].reshape(1024, 128))
    mixed = (prod[:PAIRS] + turn(prod[PAIRS:], -1.0)).astype(BF16)
    o_ref[...] = jnp.broadcast_to(mixed[None], (32, PAIRS, 128))


def adjoint_kernel(recv_ref, w_ref, o_ref, dmix_ref):
    total = jnp.sum(recv_ref[...].astype(F32), axis=0)
    dmix = total[:PAIRS]
    dmix_ref[...] = dmix
    both = jnp.concatenate([dmix, turn(dmix, 1.0)], axis=0).astype(BF16)
    prod = dot(both, w_ref[...].reshape(1024, 128), NT)
    real = jnp.zeros((PAIRS, 128), F32)
    imag = jnp.zeros((PAIRS, 128), F32)
    for kp in range(8):
        own = own_pair(kp, PAIRS)
        cols = slice(kp * 128, kp * 128 + 128)
        real = real + jnp.where(own, prod[:PAIRS, cols], 0.0)
        imag = imag + jnp.where(own, prod[PAIRS:, cols], 0.0)
    real = real + swap(real)
    imag = imag + swap(imag)
    dspec = jnp.where(lanes(real.shape) < 64, real, imag) * SCALE
    point = total[PAIRS:]
    point = split_pair(point + swap(point))
    message = jnp.concatenate([dspec, point], axis=0).astype(BF16)
    o_ref[...] = jnp.broadcast_to(message[None], (32, ROWS, 128))


def factor_kernel(recv_ref, spec_ref, dmix_ref, fact_ref, fact, tiles):
    fact[:PAIRS] = spec_ref[...]
    fact[PAIRS : 2 * PAIRS] = dmix_ref[...]
    tiles[:256] = recv_ref[:, PAIRS:].astype(F32).reshape(256, 128)
    first, second = (tiles[pl.ds(i, 32, stride=8), :] for i in range(2))
    both = jnp.where(lanes((32, 128)) < 64, first + swap(first), second + swap(second))
    fact[2 * PAIRS :] = both
    fact_ref[...] = jnp.broadcast_to(fact[...].astype(BF16)[None], (4, 128, 128))


def gather_kernel(recv_ref, tab_ref, own_ref, send_ref, scratch, *, rows):
    table = tab_ref[...]
    scratch[: 32 * rows] = recv_ref[...].astype(F32).reshape(32 * rows, 128)
    for group in range(4):
        cols = []
        for i in range(12):
            modes = scratch[pl.ds(group * 12 + i, 32, stride=rows), :]
            pair = jnp.concatenate([modes, turn(modes, -1.0)], axis=0)
            cols.append(jnp.concatenate([pair, pair], axis=0).astype(BF16))
        back = dot(table, jnp.concatenate(cols, axis=1))
        for i in range(12):
            m, b = divmod(group * 12 + i, 3)
            part = back[:, i * 128 : i * 128 + 128].astype(BF16)
            own_ref[m, b] = part[:8]
            send_ref[m, b] = part[8:]


def field_kernel(
    in_ref, cot_ref, got_ref, other_ref, tab_ref, w_ref, dpre_ref, own_ref, send_ref, rows, scratch, dpre, sems
):
    load_rows(got_ref, other_ref, rows)
    mix_t = w_ref[...].astype(F32).T.astype(BF16)
    point = jnp.zeros((64, 64), F32)
    copies = []

    def fields_of(g):
        return [3 * g + i for i in range(3)]

    def pre_of(g):
        left = left_of([(mode_block(rows, f) * INV_SCALE).astype(BF16) for f in fields_of(g)], mix_t)
        out = []
        for chunk in range(4):
            ts = slice(chunk * 256, chunk * 256 + 256)
            right = jnp.concatenate([tab_ref[:, ts]] + [in_ref[f, :, ts] for f in fields_of(g)], axis=0)
            out.append(dot(left, right))
        return out

    pre = pre_of(0)
    for g in range(GROUPS):
        following = pre_of(g + 1) if g + 1 < GROUPS else None
        for chunk in range(4):
            ts = slice(chunk * 256, chunk * 256 + 256)
            for i, f in enumerate(fields_of(g)):
                slope = gelu_slope_twice(pre[chunk][i * 64 : i * 64 + 64], cot_ref[f, :, ts].astype(F32))
                dpre[f, :, ts] = slope.astype(BF16)
        pre = following
        part = pl.ds(3 * g, 3)
        copies.append(pltpu.make_async_copy(dpre.at[part], dpre_ref.at[part], sems.at[g]))
        copies[g].start()
        left = jnp.concatenate([tab_ref[...]] + [in_ref[f] for f in fields_of(g)], axis=0)
        r = dot(left, dpre[3 * g : 3 * g + 3].reshape(192, DURATION), NT)
        for i, f in enumerate(fields_of(g)):
            cols = slice(i * 64, i * 64 + 64)
            point = point + r[64 + i * 64 : 128 + i * 64, cols]
            drows = jnp.concatenate([r[:32, cols], r[32:64, cols]], axis=1)
            scratch[field_rows(f), :] = drows * (0.5 * INV_SCALE)
            if f % 8 == 7:
                store_rows(scratch, f // 8, own_ref, send_ref)
    point = 0.5 * point
    pair = split_pair(jnp.concatenate([point, point], axis=1))
    pair = jnp.concatenate([pair, jnp.zeros_like(pair)], axis=0).reshape(16, 8, 128).astype(BF16)
    own_ref[:, 3] = pair
    send_ref[:, 3] = pair
    for copy in copies:
        copy.wait()


def fetch_kernel(slow_ref, fast_ref, sem):
    copy = pltpu.make_async_copy(slow_ref, fast_ref, sem)
    copy.start()
    copy.wait()


def grad_kernel(dpre_ref, got_ref, other_ref, tab_ref, w_ref, o_ref, rows, grad, sems):
    load_rows(got_ref, other_ref, rows)
    mixing = (w_ref[...].astype(F32) * 0.5).astype(BF16)
    copies = []
    for g in range(GROUPS):
        fields = [3 * g + i for i in range(3)]
        left = left_of([mode_block(rows, f).astype(BF16) for f in fields], mixing)
        for chunk in range(4):
            ts = slice(chunk * 256, chunk * 256 + 256)
            right = jnp.concatenate([tab_ref[:, ts]] + [dpre_ref[f, :, ts] for f in fields], axis=0)
            total = dot(left, right).astype(BF16)
            for i, f in enumerate(fields):
                grad[f, :, ts] = total[i * 64 : i * 64 + 64]
        part = pl.ds(3 * g, 3)
        copies.append(pltpu.make_async_copy(grad.at[part], o_ref.at[part], sems.at[g]))
        copies[g].start()
    for copy in copies:
        copy.wait()


def weight_grad_kernel(fact_ref, spec_ref, point_ref, whole_point):
    fact = fact_ref[...].astype(F32)
    place = lanes((1, 256)) & 127
    place = place - 24 * ((place * 171) >> 12)
    mode = (place * 43) >> 7
    empty = jnp.zeros((32, 128), F32)
    for half in range(2):
        rows = slice(half * 24, half * 24 + 24)
        s = jnp.concatenate([fact[:, rows].reshape(96, 128), empty], axis=0).T
        d = jnp.concatenate([fact[:, 48:96][:, rows].reshape(96, 128), empty], axis=0)
        left = jnp.concatenate([s[:64], s[64:]], axis=1)
        right = jnp.concatenate([d, turn(d, 1.0)], axis=0).astype(BF16)
        parts = [jnp.where(mode == m, left, 0.0).astype(BF16) for m in range(8)]
        g = dot(jnp.concatenate(parts, axis=0), right) * (1.0 / math.sqrt(BATCH * DEPTH))
        g = g.reshape(8, 64, 128)
        modes = slice(half * 8, half * 8 + 8)
        spec_ref[modes, 0] = g[:, :, :64]
        spec_ref[modes, 1] = g[:, :, 64:]
    point = fact[0, 96:] + fact[1, 96:] + fact[2, 96:] + fact[3, 96:]
    point = point * (1.0 / math.sqrt(BATCH * DEPTH * DURATION))
    whole_point[pl.ds(0, 32, stride=2), :] = point
    whole_point[pl.ds(1, 32, stride=2), :] = swap(point)
    point_ref[...] = whole_point[:64, :64]


FAST = pl.BlockSpec(memory_space=pltpu.VMEM)
SLOW = pl.BlockSpec(memory_space=pl.ANY)


def call(kernel, out_shape, in_specs, out_specs, scratch=(), limit=8):
    return pl.pallas_call(
        kernel,
        out_shape=out_shape,
        in_specs=in_specs,
        out_specs=out_specs,
        scratch_shapes=list(scratch),
        compiler_params=pltpu.CompilerParams(vmem_limit_bytes=limit * MIB),
    )


def shape(*dims, dtype=BF16):
    return jax.ShapeDtypeStruct(dims, dtype)


def exchange(v, axes):
    return lax.all_to_all(v, axes, 0, 0, tiled=True)


def to_other_core(v):
    return lax.ppermute(v, "core", [(0, 1), (1, 0)])


def spread(own, other, table, rows):
    scratch = [pltpu.VMEM((33 * rows, 128), F32)]
    if rows == ROWS:
        scratch.append(pltpu.VMEM((72, 128), F32))
    kernel = functools.partial(spread_kernel, rows=rows)
    return call(kernel, shape(32, rows, 128), [FAST] * 3, FAST, scratch)(own, other, table)


def gather(got, table, rows):
    return call(
        functools.partial(gather_kernel, rows=rows),
        (shape(16, 3, 8, 128),) * 2,
        [FAST] * 2,
        (FAST, FAST),
        [pltpu.VMEM((33 * rows, 128), F32)],
    )(got, table)


def local(inputs, cotangent, spec_weight, point_weight):
    tab = jnp.asarray(time_rows())
    fields = inputs.reshape(FIELDS, CHANNELS, DURATION)
    cots = cotangent.reshape(FIELDS, CHANNELS, DURATION)
    part4 = shape(16, 4, 8, 128)
    rows = pltpu.VMEM((FIELDS * 32 + 8, 128), F32)
    whole_field = pltpu.VMEM((FIELDS, CHANNELS, DURATION), BF16)
    sems = pltpu.SemaphoreType.DMA((GROUPS,))

    own, send, table, mixing, fields, forward, inverse = call(
        coeff_kernel,
        (
            pltpu.VMEM((16, 3, 8, 128), BF16),
            pltpu.VMEM((16, 3, 8, 128), BF16),
            pltpu.VMEM((64, DURATION), BF16),
            pltpu.VMEM((CHANNELS, CHANNELS), BF16),
            pltpu.VMEM((FIELDS, CHANNELS, DURATION), BF16),
            pltpu.VMEM((64, 32), BF16),
            pltpu.VMEM((16, 128), BF16),
        ),
        [SLOW] * 3,
        (FAST,) * 7,
        [rows, pltpu.SemaphoreType.DMA((5,))],
        limit=56,
    )(*(pltpu.with_memory_space_constraint(v, pltpu.HBM) for v in (fields, tab, point_weight)))
    weights = call(
        weight_kernel,
        shape(16, 64, 128),
        [SLOW],
        FAST,
        [pltpu.VMEM((16, 2, CHANNELS, CHANNELS), F32), pltpu.SemaphoreType.DMA((4,))],
    )(pltpu.with_memory_space_constraint(spec_weight, pltpu.HBM))
    other, weights = lax.optimization_barrier((to_other_core(send), weights))
    got = exchange(spread(own, other, forward, PAIRS), CHIP)
    mixed, spectrum = call(
        mix_kernel,
        (shape(32, PAIRS, 128), shape(PAIRS, 128, dtype=F32)),
        [FAST] * 2,
        (FAST,) * 2,
    )(got, weights)
    got = exchange(mixed, CHIP)
    own, send = gather(got, inverse, PAIRS)
    dpre, own, send = call(
        field_kernel,
        (pltpu.HBM((FIELDS, CHANNELS, DURATION), BF16), part4, part4),
        [FAST] * 6,
        (SLOW, FAST, FAST),
        [rows, rows, whole_field, sems],
        limit=16,
    )(pltpu.with_memory_space_constraint(fields, pltpu.VMEM), cots, own, to_other_core(send), table, mixing)
    got = exchange(spread(own, to_other_core(send), forward, ROWS), CHIP)
    dmodes, dmixed = call(
        adjoint_kernel,
        (shape(32, ROWS, 128), shape(PAIRS, 128, dtype=F32)),
        [FAST] * 2,
        (FAST, FAST),
    )(got, weights)
    got = exchange(dmodes, CHIP)
    factors = call(
        factor_kernel,
        pltpu.HBM((4, 128, 128), BF16),
        [FAST] * 3,
        FAST,
        [pltpu.VMEM((128, 128), F32), pltpu.VMEM((264, 128), F32)],
    )(got, spectrum, dmixed)
    factors = exchange(factors, "dp")
    own, send = gather(got, inverse, ROWS)
    dpre = call(
        fetch_kernel,
        pltpu.VMEM((FIELDS, CHANNELS, DURATION), BF16),
        [SLOW],
        FAST,
        [pltpu.SemaphoreType.DMA],
        limit=1,
    )(pltpu.with_memory_space_constraint(dpre, pltpu.HBM))
    other, dpre = lax.optimization_barrier((to_other_core(send), dpre))
    input_grad = call(
        grad_kernel,
        pltpu.HBM((FIELDS, CHANNELS, DURATION), BF16),
        [FAST] * 5,
        SLOW,
        [rows, whole_field, sems],
        limit=12,
    )(pltpu.with_memory_space_constraint(dpre, pltpu.VMEM), own, other, table, mixing)
    spec_grad, point_grad = call(
        weight_grad_kernel,
        (shape(16, 2, 64, 64, dtype=F32), shape(64, 64, dtype=F32)),
        [FAST],
        (FAST, FAST),
        [pltpu.VMEM((72, 128), F32)],
    )(factors)
    return (input_grad.reshape(inputs.shape), spec_grad, point_grad)


def solution(mesh):
    fine = Mesh(mesh.devices.reshape(4, 2, 4, 4, 2), ("dp",) + FIELD)
    fields = P("dp", FIELD, None, None)
    weights = P(FIELD, None, None, None)
    return jax.shard_map(
        local,
        mesh=fine,
        in_specs=(fields, fields, weights, P()),
        out_specs=(fields, weights, P()),
        check_vma=False,
    )
```

```python
import functools
import math

import jax
import jax.numpy as jnp
import ml_dtypes
import numpy as np
from jax import lax
from jax.experimental import pallas as pl
from jax.experimental.pallas import tpu as pltpu
from jax.sharding import Mesh
from jax.sharding import PartitionSpec as P

DEPTH = 512
DURATION = 1024
CHANNELS = 64
DMODES = 32
TMODES = 32
BATCH = 12

CHIP = ("z", "y", "x")
FIELD = CHIP + ("core",)
BF16 = jnp.bfloat16
F32 = jnp.float32
SCALE = 1.0 / math.sqrt(DEPTH * DURATION)
INV_SCALE = 1.0 / math.sqrt(DMODES * TMODES)
NN = (((1,), (0,)), ((), ()))
NT = (((1,), (1,)), ((), ()))
MIB = 1024 * 1024
FIELDS = 24
GROUPS = 8
PAIRS = 48
ROWS = 56


def time_rows():
    m = np.arange(TMODES)
    phase = ((m[:, None] * np.arange(DURATION)[None, :]) % DURATION) * (2.0 * np.pi / DURATION)
    return np.concatenate([np.cos(phase), -np.sin(phase)], axis=0).astype(ml_dtypes.bfloat16)


def depth_table(k, x, sine):
    freq = jnp.where(k < DMODES // 2, k, k - DMODES)
    phase = ((freq * x - jnp.where(sine, DEPTH // 4, 0) + DEPTH // 2) & (DEPTH - 1)) - DEPTH // 2
    return jnp.cos(phase.astype(F32) * (2.0 * math.pi / DEPTH))


def high_or_low(v, low):
    high = v.astype(BF16).astype(F32)
    return jnp.where(low, v - high, high).astype(BF16)


def position(i):
    return 8 * (lax.axis_index(FIELD) ^ (i >> 3)) + (i & 7)


def forward_table():
    row = lax.broadcasted_iota(jnp.int32, (64, 32), 0)
    col = lax.broadcasted_iota(jnp.int32, (64, 32), 1)
    return high_or_low(depth_table(row & 31, position(col & 15), row >= 32), col >= 16)


def inverse_table():
    row = lax.broadcasted_iota(jnp.int32, (16, 128), 0)
    col = lax.broadcasted_iota(jnp.int32, (16, 128), 1)
    return high_or_low(depth_table(col & 31, position(row), (col & 32) != 0), col >= 64)


def lanes(shape):
    return lax.broadcasted_iota(jnp.int32, shape, len(shape) - 1)


def swap(v):
    return pltpu.roll(v, 64, 1)


def turn(v, first):
    return swap(v) * jnp.where(lanes(v.shape) < 64, first, -first).astype(F32)


def split_pair(v):
    high = v.astype(BF16).astype(F32)
    return jnp.where(lanes(v.shape) < 64, high, v - high)


def dot(a, b, dims=NN):
    return lax.dot_general(a, b, dims, preferred_element_type=F32)


def store_rows(scratch, b, own_ref, send_ref):
    core = lax.axis_index("core")
    for c, ref in ((core, own_ref), (1 - core, send_ref)):
        rows = scratch[pl.ds(pl.multiple_of(b * 256 + c * 128, 128), 128), :]
        ref[:, b] = rows.reshape(16, 8, 128).astype(BF16)


def load_rows(own_ref, other_ref, scratch):
    core = lax.axis_index("core")
    for b in range(3):
        for c, ref in ((core, own_ref), (1 - core, other_ref)):
            rows = ref[:, b].astype(F32).reshape(128, 128)
            scratch[pl.ds(pl.multiple_of(b * 256 + c * 128, 128), 128), :] = rows


def field_rows(field):
    b, xl = divmod(field, 8)
    return pl.ds(b * 256 + xl, 32, stride=8)


def mode_block(scratch, field):
    g = scratch[field_rows(field), :]
    return jnp.concatenate([g[:, :64], g[:, 64:]], axis=0).T


def left_of(blocks, mixing):
    zero = jnp.zeros((64, 64), BF16)
    rows = []
    for i, g in enumerate(blocks):
        rows.append(jnp.concatenate([g] + [mixing if k == i else zero for k in range(len(blocks))], axis=1))
    return jnp.concatenate(rows, axis=0)


def gelu_slope_twice(pre, cot):
    root = math.sqrt(2.0 / math.pi)
    p = (root * 0.044715) * (pre * pre) + root
    th = jnp.tanh(pre * p)
    q = 3.0 * p - 2.0 * root
    return ((1.0 + th) * (1.0 + (pre * q) * (1.0 - th))) * cot


def own_pair(kp, rows):
    row = lax.broadcasted_iota(jnp.int32, (rows, 128), 0)
    first = row - lanes((rows, 128)) // 64 * 3 - 6 * kp
    return (first >= 0) & (first < 3)


def coeff_kernel(
    in_ref, tab_ref, mix_ref, own_ref, send_ref, table, mixing, fields, forward, inverse, scratch, sems
):
    copies = [
        pltpu.make_async_copy(tab_ref, table, sems.at[3]),
        pltpu.make_async_copy(mix_ref, mixing, sems.at[4]),
    ]
    for b in range(3):
        part = pl.ds(8 * b, 8)
        copies.append(pltpu.make_async_copy(in_ref.at[part], fields.at[part], sems.at[b]))
    for copy in copies:
        copy.start()
    forward[...] = forward_table()
    inverse[...] = inverse_table()
    copies[0].wait()
    for b in range(3):
        copies[2 + b].wait()
        coeffs = dot(table[...], fields[8 * b : 8 * b + 8].reshape(512, DURATION), NT) * SCALE
        for i in range(8):
            cols = slice(i * 64, i * 64 + 64)
            scratch[field_rows(8 * b + i), :] = jnp.concatenate([coeffs[:32, cols], coeffs[32:, cols]], axis=1)
        store_rows(scratch, b, own_ref, send_ref)
    copies[1].wait()


def weight_kernel(w_ref, o_ref):
    o_ref[...] = jnp.concatenate([w_ref[:, 0], w_ref[:, 1]], axis=2).astype(BF16)


def spread_kernel(own_ref, other_ref, tab_ref, o_ref, scratch, *point, rows):
    table = tab_ref[...]
    both = jnp.concatenate([own_ref[:, :3].astype(F32), other_ref[:, :3].astype(F32)], axis=2).astype(BF16)
    both = both.reshape(PAIRS, 16, 128)
    for group in range(4):
        data = jnp.concatenate([both[group * 12 + i] for i in range(12)], axis=1)
        modes = dot(table, jnp.concatenate([data, data], axis=0))
        for i in range(12):
            cols = slice(i * 128, i * 128 + 128)
            part = modes[:32, cols] + turn(modes[32:, cols], 1.0)
            scratch[pl.ds(group * 12 + i, 32, stride=rows), :] = part
    if point:
        (pairs,) = point
        total = own_ref[:8, 3].astype(F32).reshape(64, 128) + other_ref[:8, 3].astype(F32).reshape(64, 128)
        pairs[:64] = split_pair(total + swap(total))
        for i in range(2):
            scratch[pl.ds(PAIRS + i, 32, stride=rows), :] = pairs[pl.ds(i, 32, stride=2), :]
        for i in range(2, 8):
            scratch[pl.ds(PAIRS + i, 32, stride=rows), :] = jnp.zeros((32, 128), F32)
    o_ref[...] = scratch[: 32 * rows].reshape(32, rows, 128).astype(BF16)


def mix_kernel(recv_ref, w_ref, o_ref, spec_ref):
    spec = jnp.sum(recv_ref[...].astype(F32), axis=0)
    spec_ref[...] = spec
    low = lanes(spec.shape) < 64
    other = swap(spec)
    real = jnp.where(low, spec, other)
    imag = jnp.where(low, other, spec)
    cols = []
    for kp in range(8):
        own = own_pair(kp, PAIRS)
        cols.append(
            jnp.concatenate([jnp.where(own, real, 0.0), jnp.where(own, imag, 0.0)], axis=0).astype(BF16)
        )
    prod = dot(jnp.concatenate(cols, axis=1), w_ref[...].reshape(1024, 128))
    mixed = (prod[:PAIRS] + turn(prod[PAIRS:], -1.0)).astype(BF16)
    o_ref[...] = jnp.broadcast_to(mixed[None], (32, PAIRS, 128))


def adjoint_kernel(recv_ref, w_ref, o_ref, dmix_ref):
    total = jnp.sum(recv_ref[...].astype(F32), axis=0)
    dmix = total[:PAIRS]
    dmix_ref[...] = dmix
    both = jnp.concatenate([dmix, turn(dmix, 1.0)], axis=0).astype(BF16)
    prod = dot(both, w_ref[...].reshape(1024, 128), NT)
    real = jnp.zeros((PAIRS, 128), F32)
    imag = jnp.zeros((PAIRS, 128), F32)
    for kp in range(8):
        own = own_pair(kp, PAIRS)
        cols = slice(kp * 128, kp * 128 + 128)
        real = real + jnp.where(own, prod[:PAIRS, cols], 0.0)
        imag = imag + jnp.where(own, prod[PAIRS:, cols], 0.0)
    real = real + swap(real)
    imag = imag + swap(imag)
    dspec = jnp.where(lanes(real.shape) < 64, real, imag) * SCALE
    point = total[PAIRS:]
    point = split_pair(point + swap(point))
    message = jnp.concatenate([dspec, point], axis=0).astype(BF16)
    o_ref[...] = jnp.broadcast_to(message[None], (32, ROWS, 128))


def factor_kernel(recv_ref, spec_ref, dmix_ref, fact_ref, fact, tiles):
    fact[:PAIRS] = spec_ref[...]
    fact[PAIRS : 2 * PAIRS] = dmix_ref[...]
    tiles[:256] = recv_ref[:, PAIRS:].astype(F32).reshape(256, 128)
    first, second = (tiles[pl.ds(i, 32, stride=8), :] for i in range(2))
    both = jnp.where(lanes((32, 128)) < 64, first + swap(first), second + swap(second))
    fact[2 * PAIRS :] = both
    fact_ref[...] = jnp.broadcast_to(fact[...].astype(BF16)[None], (4, 128, 128))


def gather_kernel(recv_ref, tab_ref, own_ref, send_ref, scratch, *, rows):
    table = tab_ref[...]
    scratch[: 32 * rows] = recv_ref[...].astype(F32).reshape(32 * rows, 128)
    for group in range(4):
        cols = []
        for i in range(12):
            modes = scratch[pl.ds(group * 12 + i, 32, stride=rows), :]
            pair = jnp.concatenate([modes, turn(modes, -1.0)], axis=0)
            cols.append(jnp.concatenate([pair, pair], axis=0).astype(BF16))
        back = dot(table, jnp.concatenate(cols, axis=1))
        for i in range(12):
            m, b = divmod(group * 12 + i, 3)
            part = back[:, i * 128 : i * 128 + 128].astype(BF16)
            own_ref[m, b] = part[:8]
            send_ref[m, b] = part[8:]


def field_kernel(
    in_ref, cot_ref, got_ref, other_ref, tab_ref, w_ref, dpre_ref, own_ref, send_ref, rows, scratch, dpre, sems
):
    load_rows(got_ref, other_ref, rows)
    mix_t = w_ref[...].astype(F32).T.astype(BF16)
    point = jnp.zeros((64, 64), F32)
    copies = []

    def fields_of(g):
        return [3 * g + i for i in range(3)]

    def pre_of(g):
        left = left_of([(mode_block(rows, f) * INV_SCALE).astype(BF16) for f in fields_of(g)], mix_t)
        out = []
        for chunk in range(4):
            ts = slice(chunk * 256, chunk * 256 + 256)
            right = jnp.concatenate([tab_ref[:, ts]] + [in_ref[f, :, ts] for f in fields_of(g)], axis=0)
            out.append(dot(left, right))
        return out

    pre = pre_of(0)
    for g in range(GROUPS):
        following = pre_of(g + 1) if g + 1 < GROUPS else None
        for chunk in range(4):
            ts = slice(chunk * 256, chunk * 256 + 256)
            for i, f in enumerate(fields_of(g)):
                slope = gelu_slope_twice(pre[chunk][i * 64 : i * 64 + 64], cot_ref[f, :, ts].astype(F32))
                dpre[f, :, ts] = slope.astype(BF16)
        pre = following
        part = pl.ds(3 * g, 3)
        copies.append(pltpu.make_async_copy(dpre.at[part], dpre_ref.at[part], sems.at[g]))
        copies[g].start()
        left = jnp.concatenate([tab_ref[...]] + [in_ref[f] for f in fields_of(g)], axis=0)
        r = dot(left, dpre[3 * g : 3 * g + 3].reshape(192, DURATION), NT)
        for i, f in enumerate(fields_of(g)):
            cols = slice(i * 64, i * 64 + 64)
            point = point + r[64 + i * 64 : 128 + i * 64, cols]
            drows = jnp.concatenate([r[:32, cols], r[32:64, cols]], axis=1)
            scratch[field_rows(f), :] = drows * (0.5 * INV_SCALE)
            if f % 8 == 7:
                store_rows(scratch, f // 8, own_ref, send_ref)
    point = 0.5 * point
    pair = split_pair(jnp.concatenate([point, point], axis=1))
    pair = jnp.concatenate([pair, jnp.zeros_like(pair)], axis=0).reshape(16, 8, 128).astype(BF16)
    own_ref[:, 3] = pair
    send_ref[:, 3] = pair
    for copy in copies:
        copy.wait()


def fetch_kernel(slow_ref, fast_ref, sem):
    copy = pltpu.make_async_copy(slow_ref, fast_ref, sem)
    copy.start()
    copy.wait()


def grad_kernel(dpre_ref, got_ref, other_ref, tab_ref, w_ref, o_ref, rows, grad, sems):
    load_rows(got_ref, other_ref, rows)
    mixing = (w_ref[...].astype(F32) * 0.5).astype(BF16)
    copies = []
    for g in range(GROUPS):
        fields = [3 * g + i for i in range(3)]
        left = left_of([mode_block(rows, f).astype(BF16) for f in fields], mixing)
        for chunk in range(4):
            ts = slice(chunk * 256, chunk * 256 + 256)
            right = jnp.concatenate([tab_ref[:, ts]] + [dpre_ref[f, :, ts] for f in fields], axis=0)
            total = dot(left, right).astype(BF16)
            for i, f in enumerate(fields):
                grad[f, :, ts] = total[i * 64 : i * 64 + 64]
        part = pl.ds(3 * g, 3)
        copies.append(pltpu.make_async_copy(grad.at[part], o_ref.at[part], sems.at[g]))
        copies[g].start()
    for copy in copies:
        copy.wait()


def weight_grad_kernel(fact_ref, spec_ref, point_ref, whole_point):
    fact = fact_ref[...].astype(F32)
    place = lanes((1, 256)) & 127
    place = place - 24 * ((place * 171) >> 12)
    mode = (place * 43) >> 7
    empty = jnp.zeros((32, 128), F32)
    for half in range(2):
        rows = slice(half * 24, half * 24 + 24)
        s = jnp.concatenate([fact[:, rows].reshape(96, 128), empty], axis=0).T
        d = jnp.concatenate([fact[:, 48:96][:, rows].reshape(96, 128), empty], axis=0)
        left = jnp.concatenate([s[:64], s[64:]], axis=1)
        right = jnp.concatenate([d, turn(d, 1.0)], axis=0).astype(BF16)
        parts = [jnp.where(mode == m, left, 0.0).astype(BF16) for m in range(8)]
        g = dot(jnp.concatenate(parts, axis=0), right) * (1.0 / math.sqrt(BATCH * DEPTH))
        g = g.reshape(8, 64, 128)
        modes = slice(half * 8, half * 8 + 8)
        spec_ref[modes, 0] = g[:, :, :64]
        spec_ref[modes, 1] = g[:, :, 64:]
    point = fact[0, 96:] + fact[1, 96:] + fact[2, 96:] + fact[3, 96:]
    point = point * (1.0 / math.sqrt(BATCH * DEPTH * DURATION))
    whole_point[pl.ds(0, 32, stride=2), :] = point
    whole_point[pl.ds(1, 32, stride=2), :] = swap(point)
    point_ref[...] = whole_point[:64, :64]


FAST = pl.BlockSpec(memory_space=pltpu.VMEM)
SLOW = pl.BlockSpec(memory_space=pl.ANY)


def call(kernel, out_shape, in_specs, out_specs, scratch=(), limit=8):
    return pl.pallas_call(
        kernel,
        out_shape=out_shape,
        in_specs=in_specs,
        out_specs=out_specs,
        scratch_shapes=list(scratch),
        compiler_params=pltpu.CompilerParams(vmem_limit_bytes=limit * MIB),
    )


def shape(*dims, dtype=BF16):
    return jax.ShapeDtypeStruct(dims, dtype)


def exchange(v, axes):
    return lax.all_to_all(v, axes, 0, 0, tiled=True)


def to_other_core(v):
    return lax.ppermute(v, "core", [(0, 1), (1, 0)])


def spread(own, other, table, rows):
    scratch = [pltpu.VMEM((33 * rows, 128), F32)]
    if rows == ROWS:
        scratch.append(pltpu.VMEM((72, 128), F32))
    kernel = functools.partial(spread_kernel, rows=rows)
    return call(kernel, shape(32, rows, 128), [FAST] * 3, FAST, scratch)(own, other, table)


def gather(got, table, rows):
    return call(
        functools.partial(gather_kernel, rows=rows),
        (shape(16, 3, 8, 128),) * 2,
        [FAST] * 2,
        (FAST, FAST),
        [pltpu.VMEM((33 * rows, 128), F32)],
    )(got, table)


def local(inputs, cotangent, spec_weight, point_weight):
    tab = jnp.asarray(time_rows())
    fields = inputs.reshape(FIELDS, CHANNELS, DURATION)
    cots = cotangent.reshape(FIELDS, CHANNELS, DURATION)
    part4 = shape(16, 4, 8, 128)
    rows = pltpu.VMEM((FIELDS * 32 + 8, 128), F32)
    whole_field = pltpu.VMEM((FIELDS, CHANNELS, DURATION), BF16)
    sems = pltpu.SemaphoreType.DMA((GROUPS,))

    own, send, table, mixing, fields, forward, inverse = call(
        coeff_kernel,
        (
            pltpu.VMEM((16, 3, 8, 128), BF16),
            pltpu.VMEM((16, 3, 8, 128), BF16),
            pltpu.VMEM((64, DURATION), BF16),
            pltpu.VMEM((CHANNELS, CHANNELS), BF16),
            pltpu.VMEM((FIELDS, CHANNELS, DURATION), BF16),
            pltpu.VMEM((64, 32), BF16),
            pltpu.VMEM((16, 128), BF16),
        ),
        [SLOW] * 3,
        (FAST,) * 7,
        [rows, pltpu.SemaphoreType.DMA((5,))],
        limit=56,
    )(*(pltpu.with_memory_space_constraint(v, pltpu.HBM) for v in (fields, tab, point_weight)))
    weights = call(weight_kernel, shape(16, CHANNELS, 128), [FAST], FAST)(spec_weight)
    other, weights = lax.optimization_barrier((to_other_core(send), weights))
    got = exchange(spread(own, other, forward, PAIRS), CHIP)
    mixed, spectrum = call(
        mix_kernel,
        (shape(32, PAIRS, 128), shape(PAIRS, 128, dtype=F32)),
        [FAST] * 2,
        (FAST,) * 2,
    )(got, weights)
    got = exchange(mixed, CHIP)
    own, send = gather(got, inverse, PAIRS)
    dpre, own, send = call(
        field_kernel,
        (pltpu.HBM((FIELDS, CHANNELS, DURATION), BF16), part4, part4),
        [FAST] * 6,
        (SLOW, FAST, FAST),
        [rows, rows, whole_field, sems],
        limit=16,
    )(pltpu.with_memory_space_constraint(fields, pltpu.VMEM), cots, own, to_other_core(send), table, mixing)
    got = exchange(spread(own, to_other_core(send), forward, ROWS), CHIP)
    dmodes, dmixed = call(
        adjoint_kernel,
        (shape(32, ROWS, 128), shape(PAIRS, 128, dtype=F32)),
        [FAST] * 2,
        (FAST, FAST),
    )(got, weights)
    got = exchange(dmodes, CHIP)
    factors = call(
        factor_kernel,
        pltpu.HBM((4, 128, 128), BF16),
        [FAST] * 3,
        FAST,
        [pltpu.VMEM((128, 128), F32), pltpu.VMEM((264, 128), F32)],
    )(got, spectrum, dmixed)
    factors = exchange(factors, "dp")
    own, send = gather(got, inverse, ROWS)
    dpre = call(
        fetch_kernel,
        pltpu.VMEM((FIELDS, CHANNELS, DURATION), BF16),
        [SLOW],
        FAST,
        [pltpu.SemaphoreType.DMA],
        limit=1,
    )(pltpu.with_memory_space_constraint(dpre, pltpu.HBM))
    other, dpre = lax.optimization_barrier((to_other_core(send), dpre))
    input_grad = call(
        grad_kernel,
        pltpu.HBM((FIELDS, CHANNELS, DURATION), BF16),
        [FAST] * 5,
        SLOW,
        [rows, whole_field, sems],
        limit=12,
    )(pltpu.with_memory_space_constraint(dpre, pltpu.VMEM), own, other, table, mixing)
    spec_grad, point_grad = call(
        weight_grad_kernel,
        (shape(16, 2, 64, 64, dtype=F32), shape(64, 64, dtype=F32)),
        [FAST],
        (FAST, FAST),
        [pltpu.VMEM((72, 128), F32)],
    )(factors)
    return (input_grad.reshape(inputs.shape), spec_grad, point_grad)


def solution(mesh):
    fine = Mesh(mesh.devices.reshape(4, 2, 4, 4, 2), ("dp",) + FIELD)
    fields = P("dp", FIELD, None, None)
    weights = P(FIELD, None, None, None)
    return jax.shard_map(
        local,
        mesh=fine,
        in_specs=(fields, fields, weights, P()),
        out_specs=(fields, weights, P()),
        check_vma=False,
    )
```
